32 devices in a mesh: groups: 2 (over x), pos: 16 (over z, y, core).
Axes of the slice: x: 2, y: 2, z: 4, core: 2. Of those that a mesh axis runs over, the one named last changes fastest.
Arguments:
- object_field: float32 [4, 4096, 768], P('groups', 'pos'), parts along dimension 0, may hold values from -6 to 6
- probe: float32 [4, 256, 256], P('groups'), parts along dimension 0, may hold values from -6 to 6
- amplitudes: bfloat16 [192, 256, 256], P(('groups', 'pos')), parts along dimension 0, may hold values from 0.099609375 to 4
- offsets: int32 [192, 2], P(('groups', 'pos')), parts along dimension 0, may hold values from 0 to 4095, as said below
- counts: int32 [32], P('groups'), parts along dimension 0, may hold values from 1 to 6, as said below
Outputs:
- object_out: float32 [4, 4096, 768], P('groups', 'pos'), parts along dimension 0
- probe_out: float32 [4, 256, 256], P('groups'), parts along dimension 0
The draws below stay inside these ranges and needn't reach their ends.
There are 2 independent parts, one for each index of `groups`. The reference program is written for one: setup_inputs(seed, part) draws one part's arguments, and reference() takes and returns one part's arrays. A program takes and returns all parts, laid end to end along the dimension named above; each array names one. Nothing has to cross between parts.
Inputs may be any that keep to these rules, and one draw needn't show every extreme that they name: `offsets`: slot s has its row offset within strip s // 6, that is from (s // 6) * 256 to (s // 6) * 256 + 255, and its column offset from 0 to 512. `counts`: every strip has at least one live slot; some strip has all 6 slots live.
All inputs are finite; a program needn't handle non-finite values.
Results may differ from the reference program's by a relative error of at most 0.0003.
Values sent between devices are 32-bit elements; how exact they have to be, the bound alone decides.
No kernel may reach another device: no remote copies, remote signals or barrier semaphores. Data moves between devices by JAX's collectives and lax.ppermute only.
A program may use at most 64 MiB of HBM per device.

```python
import math
import jax
import jax.numpy as jnp
from jax import lax

PATTERN_SIDE = 256
STRIP_HEIGHT = 256
OBJECT_WIDTH = 768
CAP = 6
ITERS = 2
NROWS = 4096
POSITION_SLOTS = 96
N_POS = 16


def draw_offsets(key, part):
    key = jax.random.fold_in(key, 11)
    key_row_draw, key_column_draw = jax.random.split(key)
    slot_numbers = jnp.arange(POSITION_SLOTS, dtype=jnp.int32)
    strip_ids = slot_numbers // CAP
    inside_strip = jax.random.randint(key_row_draw, (POSITION_SLOTS,), 0, STRIP_HEIGHT, dtype=jnp.int32)
    inside_strip = jnp.where(slot_numbers == POSITION_SLOTS - 1, STRIP_HEIGHT - 1, inside_strip)
    inside_strip = jnp.where(slot_numbers == 0, STRIP_HEIGHT - 1, inside_strip)
    column_range = jax.random.randint(key_column_draw, (POSITION_SLOTS,), 0, OBJECT_WIDTH - PATTERN_SIDE + 1, dtype=jnp.int32)
    column_range = jnp.where(slot_numbers == 0, 0, column_range)
    return jnp.stack([strip_ids * STRIP_HEIGHT + inside_strip, column_range], axis=1).astype(jnp.int32)


def draw_counts(key, part):
    key = jax.random.fold_in(key, 23)
    key_first, key_second, key_busy = jax.random.split(key, 3)
    first = jax.random.randint(key_first, (N_POS,), 1, CAP + 1, dtype=jnp.int32)
    second = jax.random.randint(key_second, (N_POS,), 1, CAP + 1, dtype=jnp.int32)
    busiest = jax.random.randint(key_busy, (), 0, N_POS, dtype=jnp.int32)
    loads = jnp.minimum(first, second)
    return jnp.where(jnp.arange(N_POS, dtype=jnp.int32) == busiest, CAP, loads).astype(jnp.int32)


def level_of(stream_key, shape, shards, smallest, top_value):
    level, own = 1.0, jax.random.fold_in(stream_key, 6)
    for position, blocks in shards:
        steps = jnp.exp(jax.random.uniform(jax.random.fold_in(own, position), (blocks,), jnp.float32, smallest / len(shards), top_value / len(shards)))
        level = level * jnp.repeat(steps, shape[position] // blocks).reshape([-1 if axis == position else 1 for axis in range(len(shape))])
    return level


def noise(key, shape, width, bound, pieces=(), kind=jnp.bfloat16):
    entries = width * jax.random.normal(key, shape, jnp.float32)
    if pieces:
        entries = entries * level_of(key, shape, pieces, -0.22, 0.18)
    return jnp.clip(entries, -bound, bound).astype(kind)


def setup_inputs(seed: int = 0, part: int = 0) -> dict:
    arg_keys = jax.random.split(jax.random.key(seed), 6)
    own_keys = jax.random.split(jax.random.fold_in(arg_keys[5], part), 6)
    object_field = noise(own_keys[0], (2, NROWS, OBJECT_WIDTH), 1.0, 6.0, ((1, 16),), jnp.float32)
    probe = noise(own_keys[1], (2, PATTERN_SIDE, PATTERN_SIDE), 1.0, 6.0, (), jnp.float32)
    amplitudes = jnp.clip(jnp.exp(math.log(4.0) - 3.6927934 * jax.random.uniform(own_keys[2], (POSITION_SLOTS, PATTERN_SIDE, PATTERN_SIDE), jnp.float32) ** level_of(own_keys[2], (POSITION_SLOTS, PATTERN_SIDE, PATTERN_SIDE), ((0, 16),), -0.2, 0.2)), 0.099609375, 4.0).astype(jnp.bfloat16)
    offsets = draw_offsets(jax.random.fold_in(jax.random.fold_in(arg_keys[5], part), 71), part)
    counts = draw_counts(jax.random.fold_in(jax.random.fold_in(arg_keys[5], part), 71), part)
    return {"object_field": object_field, "probe": probe, "amplitudes": amplitudes, "offsets": offsets, "counts": counts}


def wave_residual(patch_re, patch_im, probe_re, probe_im, amplitude):
    exit_wave = lax.complex(probe_re * patch_re - probe_im * patch_im, probe_re * patch_im + probe_im * patch_re)
    spectrum = jnp.fft.fft2(exit_wave, norm='ortho')
    spec_re = jnp.real(spectrum)
    spec_im = jnp.imag(spectrum)
    keeping = 1.0 - amplitude / jnp.sqrt(spec_re * spec_re + spec_im * spec_im + 1.0)
    back_wave = jnp.fft.ifft2(lax.complex(spec_re * keeping, spec_im * keeping), norm='ortho')
    return (jnp.real(back_wave), jnp.imag(back_wave))

def reference(object_field, probe, amplitudes, offsets, counts):
    object_rows = object_field.shape[1]
    slot_count = amplitudes.shape[0]
    slot_numbers = jnp.arange(slot_count, dtype=jnp.int32)
    owners = slot_numbers // CAP
    live_mask = (slot_numbers % CAP < counts[owners]).astype(jnp.float32)
    live_total = jnp.sum(counts).astype(jnp.float32)
    object_now = object_field
    probe_now = probe
    for iteration in range(ITERS):
        padded = jnp.pad(object_now, ((0, 0), (0, PATTERN_SIDE), (0, 0)))
        probe_re = probe_now[0]
        probe_im = probe_now[1]

        def one_slot(carry, slot_index):
            grad_probe, grad_object = carry
            slot_row = offsets[slot_index, 0].astype(jnp.int32)
            slot_col = offsets[slot_index, 1].astype(jnp.int32)
            zero_index = jnp.zeros((), jnp.int32)
            window = lax.dynamic_slice(padded, (zero_index, slot_row, slot_col), (2, PATTERN_SIDE, PATTERN_SIDE))
            amplitude = amplitudes[slot_index].astype(jnp.float32)
            resid_re, resid_im = wave_residual(window[0], window[1], probe_re, probe_im, amplitude)
            resid_re = resid_re * live_mask[slot_index]
            resid_im = resid_im * live_mask[slot_index]
            probe_term = jnp.stack([window[0] * resid_re + window[1] * resid_im, window[0] * resid_im - window[1] * resid_re])
            object_term = jnp.stack([probe_re * resid_re + probe_im * resid_im, probe_re * resid_im - probe_im * resid_re])
            current = lax.dynamic_slice(grad_object, (zero_index, slot_row, slot_col), (2, PATTERN_SIDE, PATTERN_SIDE))
            grad_object = lax.dynamic_update_slice(grad_object, current + object_term, (zero_index, slot_row, slot_col))
            return ((grad_probe + probe_term, grad_object), None)
        start_probe = jnp.zeros((2, PATTERN_SIDE, PATTERN_SIDE), jnp.float32)
        start_object = jnp.zeros((2, object_rows + PATTERN_SIDE, object_field.shape[2]), jnp.float32)
        (grad_probe, grad_object), unused = lax.scan(one_slot, (start_probe, start_object), slot_numbers)
        object_rate = 1.0 / (jnp.max(probe_re * probe_re + probe_im * probe_im) + 1e-06)
        object_now = object_now - object_rate * grad_object[:, :object_rows, :]
        probe_now = probe_now - 8.0 / live_total * grad_probe
    return (object_now, probe_now)
```

```python
from functools import partial
import math

import jax
import jax.numpy as jnp
import numpy as np
from jax import lax
from jax.experimental import pallas as pl
from jax.experimental.pallas import tpu as pltpu
from jax.sharding import PartitionSpec as P

ITERS = 2
ROW_TILE = 8
LANE_TILE = 128


def split_bf16(array):
    high = array.astype(jnp.bfloat16)
    low = (array - high.astype(np.float32)).astype(jnp.bfloat16)
    return high, low


def constants(side):
    half = side // 2
    index = np.arange(half)
    angle = 2.0 * np.pi / half * (index[:, None] * index[None, :] % half)
    cosine, sine = np.cos(angle), np.sin(angle)
    scale = 1.0 / math.sqrt(side)
    fwd = (np.block([[cosine, -sine], [sine, cosine]]) * scale).astype(np.float32)
    fwd_hi, fwd_lo = split_bf16(fwd)
    bwd_hi, bwd_lo = fwd_hi.T, fwd_lo.T
    right = np.stack([np.concatenate([hi, hi, lo], axis=0) for hi, lo in ((fwd_hi, fwd_lo), (bwd_hi, bwd_lo))])
    left = np.stack([np.concatenate([hi, hi, lo], axis=1) for hi, lo in ((bwd_hi, bwd_lo), (fwd_hi, fwd_lo))])
    turn = 2.0 * np.pi / side * index
    lane_twiddle = np.stack([np.broadcast_to(f(turn)[None, :], (ROW_TILE, half)) for f in (np.cos, np.sin)])
    row_twiddle = np.stack([np.broadcast_to(f(turn)[:, None], (half, LANE_TILE)) for f in (np.cos, np.sin)])
    order = np.concatenate([np.arange(0, side, 2), np.arange(1, side, 2)])
    sort = np.zeros((side, side), np.float32)
    sort[order, np.arange(side)] = 1.0
    return (
        right,
        left,
        lane_twiddle.astype(np.float32),
        row_twiddle.astype(np.float32),
        sort.astype(jnp.bfloat16),
    )


def permute_kernel(amp_ref, sort_ref, sort_t_ref, out_ref):
    def one(slot, carry):
        rows = jnp.dot(sort_t_ref[...], amp_ref[slot], preferred_element_type=jnp.float32)
        both = jnp.dot(rows.astype(jnp.bfloat16), sort_ref[...], preferred_element_type=jnp.float32)
        out_ref[slot] = both.astype(jnp.bfloat16)
        return carry

    lax.fori_loop(0, amp_ref.shape[0], one, 0)


def sorted_amplitudes(amplitudes, sort):
    return pl.pallas_call(
        permute_kernel,
        out_shape=jax.ShapeDtypeStruct(amplitudes.shape, amplitudes.dtype),
        compiler_params=pltpu.CompilerParams(vmem_limit_bytes=16 * 2**20),
        cost_estimate=pl.CostEstimate(flops=400_000_000, bytes_accessed=1_600_000, transcendentals=0),
        name="sort_amplitudes",
    )(amplitudes, jnp.asarray(sort), jnp.asarray(sort.T))


def hi_lo(value):
    high = value.astype(jnp.bfloat16)
    return high, (value - high.astype(jnp.float32)).astype(jnp.bfloat16)


def times_right(value, matrix):
    high, low = hi_lo(value)
    return jnp.dot(jnp.concatenate([high, low, high], axis=1), matrix, preferred_element_type=jnp.float32)


def times_left(matrix, value):
    high, low = hi_lo(value)
    return jnp.dot(matrix, jnp.concatenate([high, low, high], axis=0), preferred_element_type=jnp.float32)


def one_slot(slot, place_ref, amp_ref, probe_ref, right_ref, left_ref, lane_tw, row_tw, ext, grad, grad_probe):
    side = probe_ref.shape[1]
    half = side // 2
    width = ext.shape[2]
    row, col = place_ref[slot, 0], place_ref[slot, 1]
    row_base = pl.multiple_of(row // ROW_TILE * ROW_TILE, ROW_TILE)
    col_base = pl.multiple_of(col // LANE_TILE * LANE_TILE, LANE_TILE)
    row_rem, col_rem = row - row_base, col - col_base
    col_wrap = pl.multiple_of(jnp.minimum(col_base + side, width - LANE_TILE), LANE_TILE)
    row_wrap = pl.multiple_of(row_base + side, ROW_TILE)
    col_mid = pl.multiple_of(col_base + LANE_TILE, LANE_TILE)
    lanes = lax.broadcasted_iota(jnp.int32, (side, LANE_TILE), 1)
    from_wrap = lanes < col_rem
    lanes8 = lax.broadcasted_iota(jnp.int32, (ROW_TILE, LANE_TILE), 1) < col_rem
    rows8 = lax.broadcasted_iota(jnp.int32, (ROW_TILE, LANE_TILE), 0) < row_rem

    def window(part):
        def block(base, size, wrapped):
            first = ext[part, pl.ds(base, size), pl.ds(col_base, LANE_TILE)]
            last = ext[part, pl.ds(base, size), pl.ds(col_wrap, LANE_TILE)]
            middle = ext[part, pl.ds(base, size), pl.ds(col_mid, LANE_TILE)]
            return jnp.where(wrapped, last, first), middle

        left_block, right_block = block(row_base, side, from_wrap)
        left_low, right_low = block(row_wrap, ROW_TILE, lanes8)
        left_block = jnp.concatenate(
            [jnp.where(rows8, left_low, left_block[:ROW_TILE]), left_block[ROW_TILE:]], axis=0
        )
        right_block = jnp.concatenate(
            [jnp.where(rows8, right_low, right_block[:ROW_TILE]), right_block[ROW_TILE:]], axis=0
        )
        return jnp.concatenate([left_block, right_block], axis=1)

    def turned(part):
        return pltpu.roll(pltpu.roll(probe_ref[part], row_rem, 0), col_rem, 1)

    probe_re, probe_im = turned(0), turned(1)
    patch_re, patch_im = window(0), window(1)
    exit_re = probe_re * patch_re - probe_im * patch_im
    exit_im = probe_re * patch_im + probe_im * patch_re

    lane_cos = jnp.concatenate([lane_tw[0]] * (side // ROW_TILE), axis=0)
    lane_sin = jnp.concatenate([lane_tw[1]] * (side // ROW_TILE), axis=0)
    row_cos = jnp.concatenate([row_tw[0]] * (side // LANE_TILE), axis=1)
    row_sin = jnp.concatenate([row_tw[1]] * (side // LANE_TILE), axis=1)

    dif_re = exit_re[:, :half] - exit_re[:, half:]
    dif_im = exit_im[:, :half] - exit_im[:, half:]
    even = jnp.concatenate([exit_re[:, :half] + exit_re[:, half:], exit_im[:, :half] + exit_im[:, half:]], axis=1)
    odd = jnp.concatenate([dif_re * lane_cos + dif_im * lane_sin, dif_im * lane_cos - dif_re * lane_sin], axis=1)
    wave = times_right(jnp.concatenate([even, odd], axis=0), right_ref[0])
    wave_re = jnp.concatenate([wave[:side, :half], wave[side:, :half]], axis=1)
    wave_im = jnp.concatenate([wave[:side, half:], wave[side:, half:]], axis=1)
    dif_re = wave_re[:half] - wave_re[half:]
    dif_im = wave_im[:half] - wave_im[half:]
    even = jnp.concatenate([wave_re[:half] + wave_re[half:], wave_im[:half] + wave_im[half:]], axis=0)
    odd = jnp.concatenate([dif_re * row_cos + dif_im * row_sin, dif_im * row_cos - dif_re * row_sin], axis=0)
    spec = times_left(left_ref[0], jnp.concatenate([even, odd], axis=1))
    spec_re = jnp.concatenate([spec[:half, :side], spec[:half, side:]], axis=0)
    spec_im = jnp.concatenate([spec[half:, :side], spec[half:, side:]], axis=0)
    amplitude = amp_ref[slot].astype(jnp.float32)
    keeping = 1.0 - amplitude * lax.rsqrt(spec_re * spec_re + spec_im * spec_im + 1.0)
    spec_re = spec_re * keeping
    spec_im = spec_im * keeping
    both = jnp.concatenate(
        [
            jnp.concatenate([spec_re[:half], spec_im[:half]], axis=0),
            jnp.concatenate([spec_re[half:], spec_im[half:]], axis=0),
        ],
        axis=1,
    )
    back = times_left(left_ref[1], both)
    even_re, even_im = back[:half, :side], back[half:, :side]
    odd_re = back[:half, side:] * row_cos - back[half:, side:] * row_sin
    odd_im = back[:half, side:] * row_sin + back[half:, side:] * row_cos
    wave_re = jnp.concatenate([even_re + odd_re, even_re - odd_re], axis=0)
    wave_im = jnp.concatenate([even_im + odd_im, even_im - odd_im], axis=0)
    both = jnp.concatenate(
        [
            jnp.concatenate([wave_re[:, :half], wave_im[:, :half]], axis=1),
            jnp.concatenate([wave_re[:, half:], wave_im[:, half:]], axis=1),
        ],
        axis=0,
    )
    back = times_right(both, right_ref[1])
    even_re, even_im = back[:side, :half], back[:side, half:]
    odd_re = back[side:, :half] * lane_cos - back[side:, half:] * lane_sin
    odd_im = back[side:, :half] * lane_sin + back[side:, half:] * lane_cos
    resid_re = jnp.concatenate([even_re + odd_re, even_re - odd_re], axis=1)
    resid_im = jnp.concatenate([even_im + odd_im, even_im - odd_im], axis=1)

    row_back = lax.rem(side - row_rem, side)
    col_back = lax.rem(side - col_rem, side)

    def unturned(value):
        return pltpu.roll(pltpu.roll(value, col_back, 1), row_back, 0)

    grad_probe[0] += unturned(patch_re * resid_re + patch_im * resid_im)
    grad_probe[1] += unturned(patch_re * resid_im - patch_im * resid_re)

    def add(part, term):
        main = pl.ds(row_base, side)
        low = pl.ds(row_wrap, ROW_TILE)
        top = jnp.where(rows8, 0.0, term[:ROW_TILE, :LANE_TILE])
        top_mid = jnp.where(rows8, 0.0, term[:ROW_TILE, LANE_TILE:])
        left_block = jnp.concatenate([top, term[ROW_TILE:, :LANE_TILE]], axis=0)
        right_block = jnp.concatenate([top_mid, term[ROW_TILE:, LANE_TILE:]], axis=0)
        under = jnp.where(rows8, term[:ROW_TILE, :LANE_TILE], 0.0)
        grad[part, main, pl.ds(col_base, LANE_TILE)] += jnp.where(from_wrap, 0.0, left_block)
        grad[part, main, pl.ds(col_mid, LANE_TILE)] += right_block
        grad[part, main, pl.ds(col_wrap, LANE_TILE)] += jnp.where(from_wrap, left_block, 0.0)
        grad[part, low, pl.ds(col_base, LANE_TILE)] += jnp.where(lanes8, 0.0, under)
        grad[part, low, pl.ds(col_mid, LANE_TILE)] += jnp.where(rows8, term[:ROW_TILE, LANE_TILE:], 0.0)
        grad[part, low, pl.ds(col_wrap, LANE_TILE)] += jnp.where(lanes8, under, 0.0)

    add(0, probe_re * resid_re + probe_im * resid_im)
    add(1, probe_re * resid_im - probe_im * resid_re)


def iteration_kernel(first, *refs):
    if first:
        place_ref, info_ref, own_hbm, below_hbm, probe_ref = refs[:5]
        refs = refs[5:]
    else:
        place_ref, info_ref, own_hbm, above_hbm, low_hbm, below_hbm, probe_in, probe_sum, step_ref = refs[:9]
        refs = refs[9:]
    amp_ref, right_ref, left_ref, lane_tw, row_tw = refs[:5]
    refs = refs[5:]
    if first:
        own_out, low_out, grad_probe = refs[:3]
        ext, grad, sems, out_sems = refs[3:]
    else:
        own_out, low_out, grad_probe, probe_ref = refs[:4]
        ext, grad, sems, out_sems = refs[4:]
    rows = own_hbm.shape[1]
    own, low = pl.ds(0, rows), pl.ds(rows, rows)
    copies = [
        pltpu.make_async_copy(own_hbm, ext.at[:, own, :], sems.at[0]),
        pltpu.make_async_copy(below_hbm, ext.at[:, low, :], sems.at[1]),
    ]
    if not first:
        copies += [
            pltpu.make_async_copy(above_hbm, grad.at[:, own, :], sems.at[2]),
            pltpu.make_async_copy(low_hbm, grad.at[:, low, :], sems.at[3]),
        ]
    for copy in copies:
        copy.start()
    if not first:
        probe_ref[...] = probe_in[...] - step_ref[0] * probe_sum[...]
    power = probe_ref[0] * probe_ref[0] + probe_ref[1] * probe_ref[1]
    rate = 1.0 / (jnp.max(power) + 1e-06)
    grad_probe[...] = jnp.zeros_like(grad_probe)
    for copy in copies:
        copy.wait()
    if not first:
        ext[...] += grad[...]
    grad[...] = jnp.zeros_like(grad)

    def slot(index, carry):
        one_slot(index, place_ref, amp_ref, probe_ref, right_ref, left_ref, lane_tw, row_tw, ext, grad, grad_probe)
        return carry

    lax.fori_loop(0, info_ref[0], slot, 0)
    low_rate = rate * info_ref[1].astype(jnp.float32)
    grad[:, low, :] = -low_rate * grad[:, low, :]
    low_copy = pltpu.make_async_copy(grad.at[:, low, :], low_out, out_sems.at[0])
    low_copy.start()
    ext[:, own, :] = ext[:, own, :] - rate * grad[:, own, :]
    own_copy = pltpu.make_async_copy(ext.at[:, own, :], own_out, out_sems.at[1])
    own_copy.start()
    low_copy.wait()
    own_copy.wait()


def iteration(first, place, info, objects, probes, amplitudes, tables):
    shape = objects[0].shape
    smem = pl.BlockSpec(memory_space=pltpu.SMEM)
    vmem = pl.BlockSpec(memory_space=pltpu.VMEM)
    anywhere = pl.BlockSpec(memory_space=pl.ANY)
    probe_shape = jax.ShapeDtypeStruct(probes[0].shape, jnp.float32)
    strip = jax.ShapeDtypeStruct(shape, jnp.float32)
    if first:
        probe_specs = [vmem]
    else:
        probe_specs = [vmem, vmem, smem]
    extended = (shape[0], 2 * shape[1], shape[2])
    return pl.pallas_call(
        partial(iteration_kernel, first),
        out_shape=[strip, strip, probe_shape] + ([] if first else [probe_shape]),
        in_specs=[smem, smem] + [anywhere] * len(objects) + probe_specs + [vmem] * (1 + len(tables)),
        out_specs=[anywhere, anywhere, vmem] + ([] if first else [vmem]),
        scratch_shapes=[
            pltpu.VMEM(extended, jnp.float32),
            pltpu.VMEM(extended, jnp.float32),
            pltpu.SemaphoreType.DMA((4,)),
            pltpu.SemaphoreType.DMA((2,)),
        ],
        compiler_params=pltpu.CompilerParams(vmem_limit_bytes=40 * 2**20),
        cost_estimate=pl.CostEstimate(flops=8_000_000_000, bytes_accessed=8_000_000, transcendentals=400_000),
        name="iteration",
    )(place, info, *objects, *probes, amplitudes, *tables)


def passed_along(value, axis, by):
    size = lax.axis_size(axis)
    pairs = [(i, i + by) for i in range(size) if 0 <= i + by < size]
    return lax.ppermute(value, axis, pairs)


def swapped(value, axis, bit):
    size = lax.axis_size(axis)
    return lax.ppermute(value, axis, [(i, i ^ bit) for i in range(size)])


def summed(value, axis):
    size = lax.axis_size(axis)
    if size & (size - 1) or size < 4:
        return lax.psum(value, axis)
    index = lax.axis_index(axis)
    halved = []
    for bit in (1, 2):
        upper = (index & bit) != 0
        half = value.shape[1] // 2
        first, second = value[:, :half], value[:, half:]
        arrived = swapped(jnp.where(upper, first, second), axis, bit)
        value = jnp.where(upper, second, first) + arrived
        halved.append((bit, upper))
    bit = 4
    while bit < size:
        value = value + swapped(value, axis, bit)
        bit *= 2
    for bit, upper in reversed(halved):
        other = swapped(value, axis, bit)
        value = jnp.concatenate([jnp.where(upper, other, value), jnp.where(upper, value, other)], axis=1)
    return value


def on_device(object_field, probe, amplitudes, offsets, counts):
    strip_rows = object_field.shape[1]
    side = probe.shape[1]
    strip_count = lax.axis_size("pos")
    device_index = lax.axis_index("pos")
    right, left, lane_tw, row_tw, sort = constants(side)
    tables = tuple(jnp.asarray(t) for t in (right, left, lane_tw, row_tw))
    below = passed_along(object_field, "pos", -1)
    own_count = lax.dynamic_index_in_dim(counts, device_index, keepdims=False)
    not_last = (device_index + 1 < strip_count).astype(jnp.int32)
    info = jnp.stack([own_count, not_last])
    step = (8.0 / jnp.sum(counts).astype(jnp.float32))[None]
    place = jnp.stack([offsets[:, 0] - device_index * strip_rows, offsets[:, 1]], axis=1)
    amps = sorted_amplitudes(amplitudes, sort)
    own, low, grad_probe = iteration(True, place, info, (object_field, below), (probe,), amps, tables)
    probe_now = probe
    for _ in range(ITERS - 1):
        probe_sum = summed(grad_probe, "pos")
        above = passed_along(low, "pos", 1)
        below = passed_along(own, "pos", -1)
        own, low, grad_probe, probe_now = iteration(
            False, place, info, (own, above, low, below), (probe_now, probe_sum, step), amps, tables
        )
    probe_sum = summed(grad_probe, "pos")
    above = passed_along(low, "pos", 1)
    return (own + above, probe_now - step * probe_sum)


def solution(mesh):
    in_specs = (
        P("groups", "pos", None),
        P("groups", None, None),
        P(("groups", "pos"), None, None),
        P(("groups", "pos"), None),
        P("groups"),
    )
    out_specs = (P("groups", "pos", None), P("groups", None, None))
    return jax.shard_map(
        on_device, mesh=mesh, in_specs=in_specs, out_specs=out_specs, check_vma=False
    )
```

```python
from functools import partial
import math

import jax
import jax.numpy as jnp
import numpy as np
from jax import lax
from jax.experimental import pallas as pl
from jax.experimental.pallas import tpu as pltpu
from jax.sharding import PartitionSpec as P

ITERS = 2
ROW_TILE = 8
LANE_TILE = 128


def split_bf16(array):
    high = array.astype(jnp.bfloat16)
    low = (array - high.astype(np.float32)).astype(jnp.bfloat16)
    return high, low


def constants(side):
    half = side // 2
    index = np.arange(half)
    right, left = [], []
    parts = []
    for odd in (0, 1):
        angle = 2.0 * np.pi / side * (index[:, None] * (2 * index[None, :] + odd) % side)
        cosine, sine = np.cos(angle), np.sin(angle)
        matrix = (np.block([[cosine, -sine], [sine, cosine]]) / math.sqrt(side)).astype(np.float32)
        parts.append(split_bf16(matrix))
    right = [np.concatenate([hi, hi, lo], axis=0) for hi, lo in parts]
    right += [np.concatenate([hi.T, hi.T, lo.T], axis=0) for hi, lo in parts]
    left = [np.concatenate([hi.T, hi.T, lo.T], axis=1) for hi, lo in parts]
    left += [np.concatenate([hi, hi, lo], axis=1) for hi, lo in parts]
    order = np.concatenate([np.arange(0, side, 2), np.arange(1, side, 2)])
    sort = np.zeros((side, side), np.float32)
    sort[order, np.arange(side)] = 1.0
    return np.stack(right), np.stack(left), sort.astype(jnp.bfloat16)


def permute_kernel(amp_ref, sort_ref, sort_t_ref, out_ref):
    def one(slot, carry):
        rows = jnp.dot(sort_t_ref[...], amp_ref[slot], preferred_element_type=jnp.float32)
        both = jnp.dot(rows.astype(jnp.bfloat16), sort_ref[...], preferred_element_type=jnp.float32)
        out_ref[slot] = both.astype(jnp.bfloat16)
        return carry

    lax.fori_loop(0, amp_ref.shape[0], one, 0)


def sorted_amplitudes(amplitudes, sort):
    return pl.pallas_call(
        permute_kernel,
        out_shape=jax.ShapeDtypeStruct(amplitudes.shape, amplitudes.dtype),
        compiler_params=pltpu.CompilerParams(vmem_limit_bytes=16 * 2**20),
        cost_estimate=pl.CostEstimate(flops=400_000_000, bytes_accessed=1_600_000, transcendentals=0),
        name="sort_amplitudes",
    )(amplitudes, jnp.asarray(sort), jnp.asarray(sort.T))


def hi_lo(value):
    high = value.astype(jnp.bfloat16)
    return high, (value - high.astype(jnp.float32)).astype(jnp.bfloat16)


def times_right(value, matrix):
    high, low = hi_lo(value)
    return jnp.dot(jnp.concatenate([high, low, high], axis=1), matrix, preferred_element_type=jnp.float32)


def times_left(matrix, value):
    high, low = hi_lo(value)
    return jnp.dot(matrix, jnp.concatenate([high, low, high], axis=0), preferred_element_type=jnp.float32)


def one_slot(slot, place_ref, amp_ref, probe_ref, right_ref, left_ref, ext, grad, grad_probe):
    side = probe_ref.shape[1]
    half = side // 2
    width = ext.shape[2]
    row, col = place_ref[slot, 0], place_ref[slot, 1]
    row_base = pl.multiple_of(row // ROW_TILE * ROW_TILE, ROW_TILE)
    col_base = pl.multiple_of(col // LANE_TILE * LANE_TILE, LANE_TILE)
    row_rem, col_rem = row - row_base, col - col_base
    col_wrap = pl.multiple_of(jnp.minimum(col_base + side, width - LANE_TILE), LANE_TILE)
    row_wrap = pl.multiple_of(row_base + side, ROW_TILE)
    col_mid = pl.multiple_of(col_base + LANE_TILE, LANE_TILE)
    lanes = lax.broadcasted_iota(jnp.int32, (side, LANE_TILE), 1)
    from_wrap = lanes < col_rem
    lanes8 = lax.broadcasted_iota(jnp.int32, (ROW_TILE, LANE_TILE), 1) < col_rem
    rows8 = lax.broadcasted_iota(jnp.int32, (ROW_TILE, LANE_TILE), 0) < row_rem

    def window(part):
        def block(base, size, wrapped):
            first = ext[part, pl.ds(base, size), pl.ds(col_base, LANE_TILE)]
            last = ext[part, pl.ds(base, size), pl.ds(col_wrap, LANE_TILE)]
            middle = ext[part, pl.ds(base, size), pl.ds(col_mid, LANE_TILE)]
            return jnp.where(wrapped, last, first), middle

        left_block, right_block = block(row_base, side, from_wrap)
        left_low, right_low = block(row_wrap, ROW_TILE, lanes8)
        left_block = jnp.concatenate(
            [jnp.where(rows8, left_low, left_block[:ROW_TILE]), left_block[ROW_TILE:]], axis=0
        )
        right_block = jnp.concatenate(
            [jnp.where(rows8, right_low, right_block[:ROW_TILE]), right_block[ROW_TILE:]], axis=0
        )
        return jnp.concatenate([left_block, right_block], axis=1)

    def turned(part):
        return pltpu.roll(pltpu.roll(probe_ref[part], row_rem, 0), col_rem, 1)

    probe_re, probe_im = turned(0), turned(1)
    patch_re, patch_im = window(0), window(1)
    exit_re = probe_re * patch_re - probe_im * patch_im
    exit_im = probe_re * patch_im + probe_im * patch_re

    even = jnp.concatenate([exit_re[:, :half] + exit_re[:, half:], exit_im[:, :half] + exit_im[:, half:]], axis=1)
    odd = jnp.concatenate([exit_re[:, :half] - exit_re[:, half:], exit_im[:, :half] - exit_im[:, half:]], axis=1)
    even = times_right(even, right_ref[0])
    odd = times_right(odd, right_ref[1])
    wave_re = jnp.concatenate([even[:, :half], odd[:, :half]], axis=1)
    wave_im = jnp.concatenate([even[:, half:], odd[:, half:]], axis=1)
    even = jnp.concatenate([wave_re[:half] + wave_re[half:], wave_im[:half] + wave_im[half:]], axis=0)
    odd = jnp.concatenate([wave_re[:half] - wave_re[half:], wave_im[:half] - wave_im[half:]], axis=0)
    even = times_left(left_ref[0], even)
    odd = times_left(left_ref[1], odd)

    def kept(spec, rows):
        spec_re, spec_im = spec[:half], spec[half:]
        amplitude = amp_ref[slot, rows, :].astype(jnp.float32)
        keeping = 1.0 - amplitude * lax.rsqrt(spec_re * spec_re + spec_im * spec_im + 1.0)
        return jnp.concatenate([spec_re * keeping, spec_im * keeping], axis=0)

    even = times_left(left_ref[2], kept(even, slice(0, half)))
    odd = times_left(left_ref[3], kept(odd, slice(half, side)))
    wave_re = jnp.concatenate([even[:half] + odd[:half], even[:half] - odd[:half]], axis=0)
    wave_im = jnp.concatenate([even[half:] + odd[half:], even[half:] - odd[half:]], axis=0)
    even = times_right(jnp.concatenate([wave_re[:, :half], wave_im[:, :half]], axis=1), right_ref[2])
    odd = times_right(jnp.concatenate([wave_re[:, half:], wave_im[:, half:]], axis=1), right_ref[3])
    resid_re = jnp.concatenate([even[:, :half] + odd[:, :half], even[:, :half] - odd[:, :half]], axis=1)
    resid_im = jnp.concatenate([even[:, half:] + odd[:, half:], even[:, half:] - odd[:, half:]], axis=1)

    row_back = lax.rem(side - row_rem, side)
    col_back = lax.rem(side - col_rem, side)

    def unturned(value):
        return pltpu.roll(pltpu.roll(value, col_back, 1), row_back, 0)

    grad_probe[0] += unturned(patch_re * resid_re + patch_im * resid_im)
    grad_probe[1] += unturned(patch_re * resid_im - patch_im * resid_re)

    def add(part, term):
        main = pl.ds(row_base, side)
        low = pl.ds(row_wrap, ROW_TILE)
        top = jnp.where(rows8, 0.0, term[:ROW_TILE, :LANE_TILE])
        top_mid = jnp.where(rows8, 0.0, term[:ROW_TILE, LANE_TILE:])
        left_block = jnp.concatenate([top, term[ROW_TILE:, :LANE_TILE]], axis=0)
        right_block = jnp.concatenate([top_mid, term[ROW_TILE:, LANE_TILE:]], axis=0)
        under = jnp.where(rows8, term[:ROW_TILE, :LANE_TILE], 0.0)
        grad[part, main, pl.ds(col_base, LANE_TILE)] += jnp.where(from_wrap, 0.0, left_block)
        grad[part, main, pl.ds(col_mid, LANE_TILE)] += right_block
        grad[part, main, pl.ds(col_wrap, LANE_TILE)] += jnp.where(from_wrap, left_block, 0.0)
        grad[part, low, pl.ds(col_base, LANE_TILE)] += jnp.where(lanes8, 0.0, under)
        grad[part, low, pl.ds(col_mid, LANE_TILE)] += jnp.where(rows8, term[:ROW_TILE, LANE_TILE:], 0.0)
        grad[part, low, pl.ds(col_wrap, LANE_TILE)] += jnp.where(lanes8, under, 0.0)

    add(0, probe_re * resid_re + probe_im * resid_im)
    add(1, probe_re * resid_im - probe_im * resid_re)


def iteration_kernel(first, *refs):
    if first:
        place_ref, info_ref, own_hbm, below_hbm, probe_hbm = refs[:5]
        refs = refs[5:]
    else:
        place_ref, info_ref, step_ref, own_hbm, above_hbm, low_hbm, below_hbm, probe_hbm, sum_hbm = refs[:9]
        refs = refs[9:]
    amp_hbm, right_hbm, left_hbm, own_out, low_out, grad_out = refs[:6]
    refs = refs[6:]
    if not first:
        probe_out, refs = refs[0], refs[1:]
    ext, grad, probe_ref, grad_probe, amp_ref, right_ref, left_ref, sems, out_sems = refs
    rows = own_hbm.shape[1]
    own, low = pl.ds(0, rows), pl.ds(rows, rows)
    pairs = [(probe_hbm, probe_ref)]
    if not first:
        pairs += [(sum_hbm, grad_probe)]
    pairs += [(own_hbm, ext.at[:, own, :]), (below_hbm, ext.at[:, low, :])]
    if not first:
        pairs += [(above_hbm, grad.at[:, own, :]), (low_hbm, grad.at[:, low, :])]
    pairs += [(right_hbm, right_ref), (left_hbm, left_ref), (amp_hbm, amp_ref)]
    copies = [pltpu.make_async_copy(src, dst, sems.at[i]) for i, (src, dst) in enumerate(pairs)]
    for copy in copies:
        copy.start()
    early = 1 if first else 2
    for copy in copies[:early]:
        copy.wait()
    if not first:
        probe_ref[...] = probe_ref[...] - step_ref[0] * grad_probe[...]
    power = probe_ref[0] * probe_ref[0] + probe_ref[1] * probe_ref[1]
    rate = 1.0 / (jnp.max(power) + 1e-06)
    grad_probe[...] = jnp.zeros_like(grad_probe)
    for copy in copies[early:]:
        copy.wait()
    if not first:
        ext[...] += grad[...]
        probe_copy = pltpu.make_async_copy(probe_ref, probe_out, out_sems.at[3])
        probe_copy.start()
    grad[...] = jnp.zeros_like(grad)

    def slot(index, carry):
        one_slot(index, place_ref, amp_ref, probe_ref, right_ref, left_ref, ext, grad, grad_probe)
        return carry

    lax.fori_loop(0, info_ref[0], slot, 0)
    outs = [pltpu.make_async_copy(grad_probe, grad_out, out_sems.at[2])]
    outs[0].start()
    low_rate = rate * info_ref[1].astype(jnp.float32)
    grad[:, low, :] = -low_rate * grad[:, low, :]
    outs += [pltpu.make_async_copy(grad.at[:, low, :], low_out, out_sems.at[0])]
    outs[1].start()
    ext[:, own, :] = ext[:, own, :] - rate * grad[:, own, :]
    outs += [pltpu.make_async_copy(ext.at[:, own, :], own_out, out_sems.at[1])]
    outs[2].start()
    for copy in outs:
        copy.wait()
    if not first:
        probe_copy.wait()


def iteration(first, scalars, objects, probes, amplitudes, tables):
    shape = objects[0].shape
    smem = pl.BlockSpec(memory_space=pltpu.SMEM)
    anywhere = pl.BlockSpec(memory_space=pl.ANY)
    probe_shape = jax.ShapeDtypeStruct(probes[0].shape, jnp.float32)
    strip = jax.ShapeDtypeStruct(shape, jnp.float32)
    arrays = (*objects, *probes, amplitudes, *tables)
    out_shape = [strip, strip, probe_shape] + ([] if first else [probe_shape])
    extended = (shape[0], 2 * shape[1], shape[2])
    return pl.pallas_call(
        partial(iteration_kernel, first),
        out_shape=out_shape,
        in_specs=[smem] * len(scalars) + [anywhere] * len(arrays),
        out_specs=[anywhere] * len(out_shape),
        scratch_shapes=[
            pltpu.VMEM(extended, jnp.float32),
            pltpu.VMEM(extended, jnp.float32),
            pltpu.VMEM(probe_shape.shape, jnp.float32),
            pltpu.VMEM(probe_shape.shape, jnp.float32),
            pltpu.VMEM(amplitudes.shape, amplitudes.dtype),
            pltpu.VMEM(tables[0].shape, tables[0].dtype),
            pltpu.VMEM(tables[1].shape, tables[1].dtype),
            pltpu.SemaphoreType.DMA((len(arrays),)),
            pltpu.SemaphoreType.DMA((4,)),
        ],
        compiler_params=pltpu.CompilerParams(vmem_limit_bytes=20 * 2**20),
        cost_estimate=pl.CostEstimate(flops=8_000_000_000, bytes_accessed=8_000_000, transcendentals=400_000),
        name="iteration",
    )(*scalars, *arrays)


def passed_along(value, axis, by):
    size = lax.axis_size(axis)
    pairs = [(i, i + by) for i in range(size) if 0 <= i + by < size]
    return lax.ppermute(value, axis, pairs)


def summed(value, axis):
    size = lax.axis_size(axis)
    rows = value.shape[0] * value.shape[1]
    if rows % (size * ROW_TILE):
        return lax.psum(value, axis)
    shards = value.reshape(size, rows // size, value.shape[2])
    shard = jnp.sum(lax.all_to_all(shards, axis, 0, 0), axis=0)
    return lax.all_to_all(jnp.broadcast_to(shard, shards.shape), axis, 0, 0).reshape(value.shape)


def on_device(object_field, probe, amplitudes, offsets, counts):
    strip_rows = object_field.shape[1]
    side = probe.shape[1]
    strip_count = lax.axis_size("pos")
    device_index = lax.axis_index("pos")
    right, left, sort = constants(side)
    tables = (jnp.asarray(right), jnp.asarray(left))
    below = passed_along(object_field, "pos", -1)
    own_count = lax.dynamic_index_in_dim(counts, device_index, keepdims=False)
    not_last = (device_index + 1 < strip_count).astype(jnp.int32)
    info = jnp.stack([own_count, not_last])
    step = (8.0 / jnp.sum(counts).astype(jnp.float32))[None]
    place = jnp.stack([offsets[:, 0] - device_index * strip_rows, offsets[:, 1]], axis=1)
    amps = sorted_amplitudes(amplitudes, sort)
    own, low, grad_probe = iteration(True, (place, info), (object_field, below), (probe,), amps, tables)
    probe_now = probe
    for _ in range(ITERS - 1):
        above = passed_along(low, "pos", 1)
        below = passed_along(own, "pos", -1)
        probe_sum = summed(grad_probe, "pos")
        own, low, grad_probe, probe_now = iteration(
            False, (place, info, step), (own, above, low, below), (probe_now, probe_sum), amps, tables
        )
    above = passed_along(low, "pos", 1)
    probe_sum = summed(grad_probe, "pos")
    return (own + above, probe_now - step * probe_sum)


def solution(mesh):
    in_specs = (
        P("groups", "pos", None),
        P("groups", None, None),
        P(("groups", "pos"), None, None),
        P(("groups", "pos"), None),
        P("groups"),
    )
    out_specs = (P("groups", "pos", None), P("groups", None, None))
    return jax.shard_map(
        on_device, mesh=mesh, in_specs=in_specs, out_specs=out_specs, check_vma=False
    )
```

```python
from functools import partial
from itertools import zip_longest
import math

import jax
import jax.numpy as jnp
import numpy as np
from jax import lax
from jax.experimental import pallas as pl
from jax.experimental.pallas import tpu as pltpu
from jax.sharding import PartitionSpec as P

ITERS = 2
ROW_TILE = 8
LANE_TILE = 128


def split_bf16(array):
    high = array.astype(jnp.bfloat16)
    low = (array - high.astype(np.float32)).astype(jnp.bfloat16)
    return high, low


def constants(side):
    half = side // 2
    index = np.arange(half)
    parts = []
    for odd in (0, 1):
        angle = 2.0 * np.pi / side * (index[:, None] * (2 * index[None, :] + odd) % side)
        cosine, sine = np.cos(angle), np.sin(angle)
        matrix = (np.block([[cosine, -sine], [sine, cosine]]) / math.sqrt(side)).astype(np.float32)
        parts.append(split_bf16(matrix))
    tables = [[part, part.T] for pair in parts for part in pair]
    order = np.concatenate([np.arange(0, side, 2), np.arange(1, side, 2)])
    sort = np.zeros((side, side), np.float32)
    sort[order, np.arange(side)] = 1.0
    return np.stack([m for pair in tables for m in pair]), sort.astype(jnp.bfloat16)


def permute_kernel(amp_ref, sort_ref, sort_t_ref, out_ref):
    def one(slot, carry):
        rows = jnp.dot(sort_t_ref[...], amp_ref[slot], preferred_element_type=jnp.float32)
        both = jnp.dot(rows.astype(jnp.bfloat16), sort_ref[...], preferred_element_type=jnp.float32)
        out_ref[slot] = both.astype(jnp.bfloat16)
        return carry

    lax.fori_loop(0, amp_ref.shape[0], one, 0)


def sorted_amplitudes(amplitudes, sort):
    return pl.pallas_call(
        permute_kernel,
        out_shape=jax.ShapeDtypeStruct(amplitudes.shape, amplitudes.dtype),
        compiler_params=pltpu.CompilerParams(vmem_limit_bytes=16 * 2**20),
        cost_estimate=pl.CostEstimate(flops=400_000_000, bytes_accessed=1_600_000, transcendentals=0),
        name="sort_amplitudes",
    )(amplitudes, jnp.asarray(sort), jnp.asarray(sort.T))


def hi_lo(value):
    high = value.astype(jnp.bfloat16)
    return high, (value - high.astype(jnp.float32)).astype(jnp.bfloat16)


def matrix(table_ref, odd, turned, axis):
    high, low = table_ref[4 * odd + turned], table_ref[4 * odd + 2 + turned]
    return jnp.concatenate([high, high, low], axis=axis)


def times_right(value, table_ref, odd, turned):
    high, low = hi_lo(value)
    stacked = jnp.concatenate([high, low, high], axis=1)
    return jnp.dot(stacked, matrix(table_ref, odd, turned, 0), preferred_element_type=jnp.float32)


def times_left(table_ref, odd, turned, value):
    high, low = hi_lo(value)
    stacked = jnp.concatenate([high, low, high], axis=0)
    return jnp.dot(matrix(table_ref, odd, turned, 1), stacked, preferred_element_type=jnp.float32)


def slot_steps(slot, live, place_ref, amp_ref, probe_ref, table_ref, ext, grad, grad_probe):
    side = probe_ref.shape[1]
    half = side // 2
    width = ext.shape[2]
    row, col = place_ref[slot, 0], place_ref[slot, 1]
    row_base = pl.multiple_of(row // ROW_TILE * ROW_TILE, ROW_TILE)
    col_base = pl.multiple_of(col // LANE_TILE * LANE_TILE, LANE_TILE)
    row_rem, col_rem = row - row_base, col - col_base
    col_wrap = pl.multiple_of(jnp.minimum(col_base + side, width - LANE_TILE), LANE_TILE)
    row_wrap = pl.multiple_of(row_base + side, ROW_TILE)
    col_mid = pl.multiple_of(col_base + LANE_TILE, LANE_TILE)
    lanes = lax.broadcasted_iota(jnp.int32, (side, LANE_TILE), 1)
    from_wrap = lanes < col_rem
    lanes8 = lax.broadcasted_iota(jnp.int32, (ROW_TILE, LANE_TILE), 1) < col_rem
    rows8 = lax.broadcasted_iota(jnp.int32, (ROW_TILE, LANE_TILE), 0) < row_rem

    def window(part):
        def block(base, size, wrapped):
            first = ext[part, pl.ds(base, size), pl.ds(col_base, LANE_TILE)]
            last = ext[part, pl.ds(base, size), pl.ds(col_wrap, LANE_TILE)]
            middle = ext[part, pl.ds(base, size), pl.ds(col_mid, LANE_TILE)]
            return jnp.where(wrapped, last, first), middle

        left_block, right_block = block(row_base, side, from_wrap)
        left_low, right_low = block(row_wrap, ROW_TILE, lanes8)
        left_block = jnp.concatenate(
            [jnp.where(rows8, left_low, left_block[:ROW_TILE]), left_block[ROW_TILE:]], axis=0
        )
        right_block = jnp.concatenate(
            [jnp.where(rows8, right_low, right_block[:ROW_TILE]), right_block[ROW_TILE:]], axis=0
        )
        return jnp.concatenate([left_block, right_block], axis=1)

    def turned(part):
        return pltpu.roll(pltpu.roll(probe_ref[part], row_rem, 0), col_rem, 1)

    probe_re, probe_im = turned(0), turned(1)
    patch_re, patch_im = window(0), window(1)
    exit_re = probe_re * patch_re - probe_im * patch_im
    exit_im = probe_re * patch_im + probe_im * patch_re

    even = jnp.concatenate([exit_re[:, :half] + exit_re[:, half:], exit_im[:, :half] + exit_im[:, half:]], axis=1)
    odd = jnp.concatenate([exit_re[:, :half] - exit_re[:, half:], exit_im[:, :half] - exit_im[:, half:]], axis=1)
    even = times_right(even, table_ref, 0, 0)
    odd = times_right(odd, table_ref, 1, 0)
    yield
    wave_re = jnp.concatenate([even[:, :half], odd[:, :half]], axis=1)
    wave_im = jnp.concatenate([even[:, half:], odd[:, half:]], axis=1)
    even = jnp.concatenate([wave_re[:half] + wave_re[half:], wave_im[:half] + wave_im[half:]], axis=0)
    odd = jnp.concatenate([wave_re[:half] - wave_re[half:], wave_im[:half] - wave_im[half:]], axis=0)
    even = times_left(table_ref, 0, 1, even)
    odd = times_left(table_ref, 1, 1, odd)
    yield

    def kept(spec, rows):
        spec_re, spec_im = spec[:half], spec[half:]
        amplitude = amp_ref[slot, rows, :].astype(jnp.float32)
        keeping = 1.0 - amplitude * lax.rsqrt(spec_re * spec_re + spec_im * spec_im + 1.0)
        return jnp.concatenate([spec_re * keeping, spec_im * keeping], axis=0)

    even = times_left(table_ref, 0, 0, kept(even, slice(0, half)))
    odd = times_left(table_ref, 1, 0, kept(odd, slice(half, side)))
    wave_re = jnp.concatenate([even[:half] + odd[:half], even[:half] - odd[:half]], axis=0)
    wave_im = jnp.concatenate([even[half:] + odd[half:], even[half:] - odd[half:]], axis=0)
    yield
    even = times_right(jnp.concatenate([wave_re[:, :half], wave_im[:, :half]], axis=1), table_ref, 0, 1)
    odd = times_right(jnp.concatenate([wave_re[:, half:], wave_im[:, half:]], axis=1), table_ref, 1, 1)
    resid_re = jnp.concatenate([even[:, :half] + odd[:, :half], even[:, :half] - odd[:, :half]], axis=1)
    resid_im = jnp.concatenate([even[:, half:] + odd[:, half:], even[:, half:] - odd[:, half:]], axis=1)
    resid_re = resid_re * live
    resid_im = resid_im * live

    yield
    row_back = lax.rem(side - row_rem, side)
    col_back = lax.rem(side - col_rem, side)

    def unturned(value):
        return pltpu.roll(pltpu.roll(value, col_back, 1), row_back, 0)

    grad_probe[0] += unturned(patch_re * resid_re + patch_im * resid_im)
    grad_probe[1] += unturned(patch_re * resid_im - patch_im * resid_re)

    def add(part, term):
        main = pl.ds(row_base, side)
        low = pl.ds(row_wrap, ROW_TILE)
        top = jnp.where(rows8, 0.0, term[:ROW_TILE, :LANE_TILE])
        top_mid = jnp.where(rows8, 0.0, term[:ROW_TILE, LANE_TILE:])
        left_block = jnp.concatenate([top, term[ROW_TILE:, :LANE_TILE]], axis=0)
        right_block = jnp.concatenate([top_mid, term[ROW_TILE:, LANE_TILE:]], axis=0)
        under = jnp.where(rows8, term[:ROW_TILE, :LANE_TILE], 0.0)
        grad[part, main, pl.ds(col_base, LANE_TILE)] += jnp.where(from_wrap, 0.0, left_block)
        grad[part, main, pl.ds(col_mid, LANE_TILE)] += right_block
        grad[part, main, pl.ds(col_wrap, LANE_TILE)] += jnp.where(from_wrap, left_block, 0.0)
        grad[part, low, pl.ds(col_base, LANE_TILE)] += jnp.where(lanes8, 0.0, under)
        grad[part, low, pl.ds(col_mid, LANE_TILE)] += jnp.where(rows8, term[:ROW_TILE, LANE_TILE:], 0.0)
        grad[part, low, pl.ds(col_wrap, LANE_TILE)] += jnp.where(lanes8, under, 0.0)

    add(0, probe_re * resid_re + probe_im * resid_im)
    add(1, probe_re * resid_im - probe_im * resid_re)


def iteration_kernel(first, *refs):
    if first:
        place_ref, info_ref, own_hbm, below_hbm, probe_hbm = refs[:5]
        refs = refs[5:]
    else:
        place_ref, info_ref, step_ref, own_hbm, above_hbm, low_hbm, below_hbm, probe_hbm, sum_hbm = refs[:9]
        refs = refs[9:]
    amp_hbm, table_hbm, own_out, low_out, grad_out = refs[:5]
    refs = refs[5:]
    if not first:
        probe_out, refs = refs[0], refs[1:]
    ext, grad, probe_ref, grad_probe, amp_ref, table_ref, sems, out_sems = refs
    rows = own_hbm.shape[1]
    own, low = pl.ds(0, rows), pl.ds(rows, rows)
    pairs = [(probe_hbm, probe_ref)]
    if not first:
        pairs += [(sum_hbm, grad_probe)]
    pairs += [(own_hbm, ext.at[:, own, :]), (below_hbm, ext.at[:, low, :])]
    if not first:
        pairs += [(above_hbm, grad.at[:, own, :]), (low_hbm, grad.at[:, low, :])]
    pairs += [(table_hbm, table_ref), (amp_hbm, amp_ref)]
    copies = [pltpu.make_async_copy(src, dst, sems.at[i]) for i, (src, dst) in enumerate(pairs)]
    for copy in copies:
        copy.start()
    early = 1 if first else 2
    for copy in copies[:early]:
        copy.wait()
    if not first:
        probe_ref[...] = probe_ref[...] - step_ref[0] * grad_probe[...]
    power = probe_ref[0] * probe_ref[0] + probe_ref[1] * probe_ref[1]
    rate = 1.0 / (jnp.max(power) + 1e-06)
    grad_probe[...] = jnp.zeros_like(grad_probe)
    for copy in copies[early:]:
        copy.wait()
    if not first:
        ext[...] += grad[...]
        probe_copy = pltpu.make_async_copy(probe_ref, probe_out, out_sems.at[3])
        probe_copy.start()
    grad[...] = jnp.zeros_like(grad)

    count = info_ref[0]

    def slots(index, carry):
        steps = []
        for slot in (2 * index, 2 * index + 1):
            live = (slot < count).astype(jnp.float32)
            slot = jnp.minimum(slot, amp_ref.shape[0] - 1)
            steps.append(slot_steps(slot, live, place_ref, amp_ref, probe_ref, table_ref, ext, grad, grad_probe))
        for unused in zip_longest(*steps):
            pass
        return carry

    lax.fori_loop(0, (count + 1) // 2, slots, 0)
    outs = [pltpu.make_async_copy(grad_probe, grad_out, out_sems.at[2])]
    outs[0].start()
    low_rate = rate * info_ref[1].astype(jnp.float32)
    grad[:, low, :] = -low_rate * grad[:, low, :]
    outs += [pltpu.make_async_copy(grad.at[:, low, :], low_out, out_sems.at[0])]
    outs[1].start()
    ext[:, own, :] = ext[:, own, :] - rate * grad[:, own, :]
    outs += [pltpu.make_async_copy(ext.at[:, own, :], own_out, out_sems.at[1])]
    outs[2].start()
    for copy in outs:
        copy.wait()
    if not first:
        probe_copy.wait()


def iteration(first, scalars, objects, probes, amplitudes, table):
    shape = objects[0].shape
    smem = pl.BlockSpec(memory_space=pltpu.SMEM)
    anywhere = pl.BlockSpec(memory_space=pl.ANY)
    probe_shape = jax.ShapeDtypeStruct(probes[0].shape, jnp.float32)
    strip = jax.ShapeDtypeStruct(shape, jnp.float32)
    arrays = (*objects, *probes, amplitudes, table)
    out_shape = [strip, strip, probe_shape] + ([] if first else [probe_shape])
    extended = (shape[0], 2 * shape[1], shape[2])
    return pl.pallas_call(
        partial(iteration_kernel, first),
        out_shape=out_shape,
        in_specs=[smem] * len(scalars) + [anywhere] * len(arrays),
        out_specs=[anywhere] * len(out_shape),
        scratch_shapes=[
            pltpu.VMEM(extended, jnp.float32),
            pltpu.VMEM(extended, jnp.float32),
            pltpu.VMEM(probe_shape.shape, jnp.float32),
            pltpu.VMEM(probe_shape.shape, jnp.float32),
            pltpu.VMEM(amplitudes.shape, amplitudes.dtype),
            pltpu.VMEM(table.shape, table.dtype),
            pltpu.SemaphoreType.DMA((len(arrays),)),
            pltpu.SemaphoreType.DMA((4,)),
        ],
        compiler_params=pltpu.CompilerParams(vmem_limit_bytes=62 * 2**20),
        cost_estimate=pl.CostEstimate(flops=8_000_000_000, bytes_accessed=8_000_000, transcendentals=400_000),
        name="iteration",
    )(*scalars, *arrays)


def passed_along(value, axis, by):
    size = lax.axis_size(axis)
    pairs = [(i, i + by) for i in range(size) if 0 <= i + by < size]
    return lax.ppermute(value, axis, pairs)


def swapped(value, axis, bit):
    size = lax.axis_size(axis)
    return lax.ppermute(value, axis, [(i, i ^ bit) for i in range(size)])


def summed(value, axis, strips):
    size = lax.axis_size(axis)
    if size & (size - 1) or size < 8:
        return lax.psum(value, axis), strips
    index = lax.axis_index(axis)
    bits = [1 << k for k in range(size.bit_length() - 1)]
    bits = [bits[0], *bits[2:], bits[1]]
    halved = []
    for bit in bits[:2]:
        upper = (index & bit) != 0
        half = value.shape[1] // 2
        first, second = value[:, :half], value[:, half:]
        arrived = swapped(jnp.where(upper, first, second), axis, bit)
        value = jnp.where(upper, second, first) + arrived
        halved.append((bit, upper))
    for bit in bits[2:]:
        value = value + swapped(value, axis, bit)
    value, strips = lax.optimization_barrier((value, strips))
    for bit, upper in reversed(halved):
        other = swapped(value, axis, bit)
        value = jnp.concatenate([jnp.where(upper, other, value), jnp.where(upper, value, other)], axis=1)
    return value, strips


def on_device(object_field, probe, amplitudes, offsets, counts):
    strip_rows = object_field.shape[1]
    side = probe.shape[1]
    strip_count = lax.axis_size("pos")
    device_index = lax.axis_index("pos")
    table, sort = constants(side)
    table = jnp.asarray(table)
    below = passed_along(object_field, "pos", -1)
    own_count = lax.dynamic_index_in_dim(counts, device_index, keepdims=False)
    not_last = (device_index + 1 < strip_count).astype(jnp.int32)
    info = jnp.stack([own_count, not_last])
    step = (8.0 / jnp.sum(counts).astype(jnp.float32))[None]
    place = jnp.stack([offsets[:, 0] - device_index * strip_rows, offsets[:, 1]], axis=1)
    amps = sorted_amplitudes(amplitudes, sort)
    own, low, grad_probe = iteration(True, (place, info), (object_field, below), (probe,), amps, table)
    probe_now = probe
    for _ in range(ITERS - 1):
        above = passed_along(low, "pos", 1)
        below = passed_along(own, "pos", -1)
        probe_sum, (above, below) = summed(grad_probe, "pos", (above, below))
        own, low, grad_probe, probe_now = iteration(
            False, (place, info, step), (own, above, low, below), (probe_now, probe_sum), amps, table
        )
    above = passed_along(low, "pos", 1)
    probe_sum, above = summed(grad_probe, "pos", above)
    return (own + above, probe_now - step * probe_sum)


def solution(mesh):
    in_specs = (
        P("groups", "pos", None),
        P("groups", None, None),
        P(("groups", "pos"), None, None),
        P(("groups", "pos"), None),
        P("groups"),
    )
    out_specs = (P("groups", "pos", None), P("groups", None, None))
    return jax.shard_map(
        on_device, mesh=mesh, in_specs=in_specs, out_specs=out_specs, check_vma=False
    )
```

```python
from functools import partial
import math

import jax
import jax.numpy as jnp
import numpy as np
from jax import lax
from jax.experimental import pallas as pl
from jax.experimental.pallas import tpu as pltpu
from jax.sharding import PartitionSpec as P

ROW_TILE = 8
LANE_TILE = 128


def split_bf16(array):
    high = array.astype(jnp.bfloat16)
    low = (array - high.astype(np.float32)).astype(jnp.bfloat16)
    return high, low


def constants(side):
    half = side // 2
    index = np.arange(half)
    parts = []
    for odd in (0, 1):
        angle = 2.0 * np.pi / side * (index[:, None] * (2 * index[None, :] + odd) % side)
        cosine, sine = np.cos(angle), np.sin(angle)
        matrix = (np.block([[cosine, -sine], [sine, cosine]]) / math.sqrt(side)).astype(np.float32)
        parts.append(split_bf16(matrix))
    tables = [[part, part.T] for pair in parts for part in pair]
    order = np.concatenate([np.arange(0, side, 2), np.arange(1, side, 2)])
    sort = np.zeros((side, side), np.float32)
    sort[order, np.arange(side)] = 1.0
    return np.stack([m for pair in tables for m in pair]), sort.astype(jnp.bfloat16)


def permute_kernel(amp_ref, sort_ref, sort_t_ref, out_ref):
    def one(slot, carry):
        rows = jnp.dot(sort_t_ref[...], amp_ref[slot], preferred_element_type=jnp.float32)
        both = jnp.dot(rows.astype(jnp.bfloat16), sort_ref[...], preferred_element_type=jnp.float32)
        out_ref[slot] = both.astype(jnp.bfloat16)
        return carry

    lax.fori_loop(0, amp_ref.shape[0], one, 0)


def sorted_amplitudes(amplitudes, sort):
    return pl.pallas_call(
        permute_kernel,
        out_shape=jax.ShapeDtypeStruct(amplitudes.shape, amplitudes.dtype),
        compiler_params=pltpu.CompilerParams(vmem_limit_bytes=16 * 2**20),
        cost_estimate=pl.CostEstimate(flops=400_000_000, bytes_accessed=1_600_000, transcendentals=0),
        name="sort_amplitudes",
    )(amplitudes, jnp.asarray(sort), jnp.asarray(sort.T))


def hi_lo(value):
    high = value.astype(jnp.bfloat16)
    return high, (value - high.astype(jnp.float32)).astype(jnp.bfloat16)


def matrix(table_ref, odd, turned, axis):
    high, low = table_ref[4 * odd + turned], table_ref[4 * odd + 2 + turned]
    return jnp.concatenate([high, high, low], axis=axis)


def times_right(value, table_ref, odd, turned):
    high, low = hi_lo(value)
    stacked = jnp.concatenate([high, low, high], axis=1)
    return jnp.dot(stacked, matrix(table_ref, odd, turned, 0), preferred_element_type=jnp.float32)


def times_left(table_ref, odd, turned, value):
    high, low = hi_lo(value)
    stacked = jnp.concatenate([high, low, high], axis=0)
    return jnp.dot(matrix(table_ref, odd, turned, 1), stacked, preferred_element_type=jnp.float32)


def window_of(ext, row, col, side):
    width = ext.shape[2]
    row_base = pl.multiple_of(row // ROW_TILE * ROW_TILE, ROW_TILE)
    col_base = pl.multiple_of(col // LANE_TILE * LANE_TILE, LANE_TILE)
    row_rem, col_rem = row - row_base, col - col_base
    col_wrap = pl.multiple_of(jnp.minimum(col_base + side, width - LANE_TILE), LANE_TILE)
    row_wrap = pl.multiple_of(row_base + side, ROW_TILE)
    col_mid = pl.multiple_of(col_base + LANE_TILE, LANE_TILE)
    from_wrap = lax.broadcasted_iota(jnp.int32, (side, LANE_TILE), 1) < col_rem
    lanes8 = lax.broadcasted_iota(jnp.int32, (ROW_TILE, LANE_TILE), 1) < col_rem
    rows8 = lax.broadcasted_iota(jnp.int32, (ROW_TILE, LANE_TILE), 0) < row_rem

    def patch(part):
        def block(base, size, wrapped):
            first = ext[part, pl.ds(base, size), pl.ds(col_base, LANE_TILE)]
            last = ext[part, pl.ds(base, size), pl.ds(col_wrap, LANE_TILE)]
            middle = ext[part, pl.ds(base, size), pl.ds(col_mid, LANE_TILE)]
            return jnp.where(wrapped, last, first), middle

        left_block, right_block = block(row_base, side, from_wrap)
        left_low, right_low = block(row_wrap, ROW_TILE, lanes8)
        left_block = jnp.concatenate(
            [jnp.where(rows8, left_low, left_block[:ROW_TILE]), left_block[ROW_TILE:]], axis=0
        )
        right_block = jnp.concatenate(
            [jnp.where(rows8, right_low, right_block[:ROW_TILE]), right_block[ROW_TILE:]], axis=0
        )
        return jnp.concatenate([left_block, right_block], axis=1)

    def add(grad, part, term):
        main = pl.ds(row_base, side)
        low = pl.ds(row_wrap, ROW_TILE)
        top = jnp.where(rows8, 0.0, term[:ROW_TILE, :LANE_TILE])
        top_mid = jnp.where(rows8, 0.0, term[:ROW_TILE, LANE_TILE:])
        left_block = jnp.concatenate([top, term[ROW_TILE:, :LANE_TILE]], axis=0)
        right_block = jnp.concatenate([top_mid, term[ROW_TILE:, LANE_TILE:]], axis=0)
        under = jnp.where(rows8, term[:ROW_TILE, :LANE_TILE], 0.0)
        grad[part, main, pl.ds(col_base, LANE_TILE)] += jnp.where(from_wrap, 0.0, left_block)
        grad[part, main, pl.ds(col_mid, LANE_TILE)] += right_block
        grad[part, main, pl.ds(col_wrap, LANE_TILE)] += jnp.where(from_wrap, left_block, 0.0)
        grad[part, low, pl.ds(col_base, LANE_TILE)] += jnp.where(lanes8, 0.0, under)
        grad[part, low, pl.ds(col_mid, LANE_TILE)] += jnp.where(rows8, term[:ROW_TILE, LANE_TILE:], 0.0)
        grad[part, low, pl.ds(col_wrap, LANE_TILE)] += jnp.where(lanes8, under, 0.0)

    return row_rem, col_rem, patch, add


def stacked_right(values, table_ref, odd, turned):
    rows = values[0].shape[0]
    product = times_right(jnp.concatenate(values, axis=0), table_ref, odd, turned)
    return [product[rows * i : rows * (i + 1)] for i in range(len(values))]


def add_slots(slots, lives, place_ref, amp_ref, probe_ref, table_ref, ext, grad, grad_probe):
    side = probe_ref.shape[1]
    half = side // 2
    windows = [window_of(ext, place_ref[slot, 0], place_ref[slot, 1], side) for slot in slots]
    patches, probes, evens, odds = [], [], [], []
    for row_rem, col_rem, patch, unused in windows:
        probe_re, probe_im = (pltpu.roll(pltpu.roll(probe_ref[part], row_rem, 0), col_rem, 1) for part in (0, 1))
        patch_re, patch_im = patch(0), patch(1)
        exit_re = probe_re * patch_re - probe_im * patch_im
        exit_im = probe_re * patch_im + probe_im * patch_re
        patches.append((patch_re, patch_im))
        probes.append((probe_re, probe_im))
        evens.append(
            jnp.concatenate([exit_re[:, :half] + exit_re[:, half:], exit_im[:, :half] + exit_im[:, half:]], axis=1)
        )
        odds.append(
            jnp.concatenate([exit_re[:, :half] - exit_re[:, half:], exit_im[:, :half] - exit_im[:, half:]], axis=1)
        )
    evens = stacked_right(evens, table_ref, 0, 0)
    odds = stacked_right(odds, table_ref, 1, 0)
    specs = []
    for even, odd in zip(evens, odds):
        wave_re = jnp.concatenate([even[:, :half], odd[:, :half]], axis=1)
        wave_im = jnp.concatenate([even[:, half:], odd[:, half:]], axis=1)
        even = jnp.concatenate([wave_re[:half] + wave_re[half:], wave_im[:half] + wave_im[half:]], axis=0)
        odd = jnp.concatenate([wave_re[:half] - wave_re[half:], wave_im[:half] - wave_im[half:]], axis=0)
        specs.append((times_left(table_ref, 0, 1, even), times_left(table_ref, 1, 1, odd)))

    def kept(spec, slot, live, rows):
        spec_re, spec_im = spec[:half], spec[half:]
        amplitude = amp_ref[slot, rows, :].astype(jnp.float32)
        keeping = live - live * amplitude * lax.rsqrt(spec_re * spec_re + spec_im * spec_im + 1.0)
        return jnp.concatenate([spec_re * keeping, spec_im * keeping], axis=0)

    evens, odds = [], []
    for (even, odd), slot, live in zip(specs, slots, lives):
        even = times_left(table_ref, 0, 0, kept(even, slot, live, slice(0, half)))
        odd = times_left(table_ref, 1, 0, kept(odd, slot, live, slice(half, side)))
        wave_re = jnp.concatenate([even[:half] + odd[:half], even[:half] - odd[:half]], axis=0)
        wave_im = jnp.concatenate([even[half:] + odd[half:], even[half:] - odd[half:]], axis=0)
        evens.append(jnp.concatenate([wave_re[:, :half], wave_im[:, :half]], axis=1))
        odds.append(jnp.concatenate([wave_re[:, half:], wave_im[:, half:]], axis=1))
    evens = stacked_right(evens, table_ref, 0, 1)
    odds = stacked_right(odds, table_ref, 1, 1)
    for even, odd, (patch_re, patch_im), (probe_re, probe_im), (row_rem, col_rem, unused, add) in zip(
        evens, odds, patches, probes, windows
    ):
        resid_re = jnp.concatenate([even[:, :half] + odd[:, :half], even[:, :half] - odd[:, :half]], axis=1)
        resid_im = jnp.concatenate([even[:, half:] + odd[:, half:], even[:, half:] - odd[:, half:]], axis=1)
        row_back = lax.rem(side - row_rem, side)
        col_back = lax.rem(side - col_rem, side)
        terms = (patch_re * resid_re + patch_im * resid_im, patch_re * resid_im - patch_im * resid_re)
        for part, term in enumerate(terms):
            grad_probe[part] += pltpu.roll(pltpu.roll(term, col_back, 1), row_back, 0)
        add(grad, 0, probe_re * resid_re + probe_im * resid_im)
        add(grad, 1, probe_re * resid_im - probe_im * resid_re)


def iteration_kernel(first, last, *refs):
    if first:
        place_ref, info_ref, own_hbm, below_hbm, probe_hbm = refs[:5]
        refs = refs[5:]
    else:
        place_ref, info_ref, step_ref, own_hbm, above_hbm, low_hbm, below_hbm, probe_hbm, sum_hbm = refs[:9]
        refs = refs[9:]
    amp_hbm, table_hbm, own_out, grad_out = refs[:4]
    refs = refs[4:]
    if last:
        low_outs, refs = refs[:2], refs[2:]
    else:
        low_outs, refs = (refs[0].at[0], refs[0].at[1]), refs[1:]
    if not first:
        probe_out, refs = refs[0], refs[1:]
    ext, grad, probe_ref, grad_probe, amp_ref, table_ref, sems, out_sems = refs
    rows = own_hbm.shape[1]
    own, low = pl.ds(0, rows), pl.ds(rows, rows)
    pairs = [(probe_hbm, probe_ref)]
    if not first:
        pairs += [(sum_hbm, grad_probe)]
    strips = [(own_hbm, ext, own), (below_hbm, ext, low)]
    if not first:
        strips += [(above_hbm, grad, own), (low_hbm, grad, low)]
    pairs += [(src.at[part], dst.at[part, where, :]) for src, dst, where in strips for part in (0, 1)]
    pairs += [(table_hbm, table_ref), (amp_hbm, amp_ref)]
    copies = [pltpu.make_async_copy(src, dst, sems.at[i]) for i, (src, dst) in enumerate(pairs)]
    for copy in copies:
        copy.start()
    early = 1 if first else 2
    for copy in copies[:early]:
        copy.wait()
    if not first:
        probe_ref[...] = probe_ref[...] - step_ref[0] * grad_probe[...]
    power = probe_ref[0] * probe_ref[0] + probe_ref[1] * probe_ref[1]
    rate = 1.0 / (jnp.max(power) + 1e-06)
    grad_probe[...] = jnp.zeros_like(grad_probe)
    for copy in copies[early:]:
        copy.wait()
    if not first:
        ext[...] += grad[...]
        probe_copy = pltpu.make_async_copy(probe_ref, probe_out, out_sems.at[5])
        probe_copy.start()
    grad[...] = jnp.zeros_like(grad)

    count = info_ref[0]

    def slots(index, carry):
        pair = (2 * index, jnp.minimum(2 * index + 1, amp_ref.shape[0] - 1))
        lives = [(2 * index + k < count).astype(jnp.float32) for k in (0, 1)]
        add_slots(pair, lives, place_ref, amp_ref, probe_ref, table_ref, ext, grad, grad_probe)
        return carry

    lax.fori_loop(0, (count + 1) // 2, slots, 0)
    outs = [pltpu.make_async_copy(grad_probe, grad_out, out_sems.at[4])]
    outs[-1].start()
    low_rate = rate * info_ref[1].astype(jnp.float32)
    for part in (0, 1):
        grad[part, low, :] = -low_rate * grad[part, low, :]
        outs.append(pltpu.make_async_copy(grad.at[part, low, :], low_outs[part], out_sems.at[part]))
        outs[-1].start()
    for part in (0, 1):
        ext[part, own, :] = ext[part, own, :] - rate * grad[part, own, :]
        outs.append(pltpu.make_async_copy(ext.at[part, own, :], own_out.at[part], out_sems.at[2 + part]))
        outs[-1].start()
    for copy in outs:
        copy.wait()
    if not first:
        probe_copy.wait()


def iteration(first, last, scalars, objects, probes, amplitudes, table):
    shape = objects[0].shape
    smem = pl.BlockSpec(memory_space=pltpu.SMEM)
    anywhere = pl.BlockSpec(memory_space=pl.ANY)
    probe_shape = jax.ShapeDtypeStruct(probes[0].shape, jnp.float32)
    strip = jax.ShapeDtypeStruct(shape, jnp.float32)
    arrays = (*objects, *probes, amplitudes, table)
    plane = jax.ShapeDtypeStruct(shape[1:], jnp.float32)
    out_shape = [strip, probe_shape] + ([plane, plane] if last else [strip]) + ([] if first else [probe_shape])
    extended = (shape[0], 2 * shape[1], shape[2])
    return pl.pallas_call(
        partial(iteration_kernel, first, last),
        out_shape=out_shape,
        in_specs=[smem] * len(scalars) + [anywhere] * len(arrays),
        out_specs=[anywhere] * len(out_shape),
        scratch_shapes=[
            pltpu.VMEM(extended, jnp.float32),
            pltpu.VMEM(extended, jnp.float32),
            pltpu.VMEM(probe_shape.shape, jnp.float32),
            pltpu.VMEM(probe_shape.shape, jnp.float32),
            pltpu.VMEM(amplitudes.shape, amplitudes.dtype),
            pltpu.VMEM(table.shape, table.dtype),
            pltpu.SemaphoreType.DMA((len(arrays) + len(objects),)),
            pltpu.SemaphoreType.DMA((6,)),
        ],
        compiler_params=pltpu.CompilerParams(vmem_limit_bytes=62 * 2**20),
        cost_estimate=pl.CostEstimate(flops=8_000_000_000, bytes_accessed=8_000_000, transcendentals=400_000),
        name="iteration",
    )(*scalars, *arrays)


def passed_along(value, axis, by):
    size = lax.axis_size(axis)
    pairs = [(i, i + by) for i in range(size) if 0 <= i + by < size]
    return lax.ppermute(value, axis, pairs)


def swapped(value, axis, bit):
    size = lax.axis_size(axis)
    return lax.ppermute(value, axis, [(i, i ^ bit) for i in range(size)])


def gathered(value, axis, halved):
    for bit, upper in reversed(halved):
        other = swapped(value, axis, bit)
        value = jnp.concatenate([jnp.where(upper, other, value), jnp.where(upper, value, other)], axis=1)
    return value


def quartered(value, axis):
    size = lax.axis_size(axis)
    if size & (size - 1) or size < 8:
        return lax.psum(value, axis), []
    index = lax.axis_index(axis)
    bits = [1 << k for k in range(size.bit_length() - 1)]
    bits = [bits[0], *bits[2:], bits[1]]
    halved = []
    for bit in bits[:2]:
        upper = (index & bit) != 0
        half = value.shape[1] // 2
        first, second = value[:, :half], value[:, half:]
        arrived = swapped(jnp.where(upper, first, second), axis, bit)
        value = jnp.where(upper, second, first) + arrived
        halved.append((bit, upper))
    for bit in bits[2:]:
        value = value + swapped(value, axis, bit)
    return value, halved


def on_device(object_field, probe, amplitudes, offsets, counts):
    strip_rows = object_field.shape[1]
    side = probe.shape[1]
    strip_count = lax.axis_size("pos")
    device_index = lax.axis_index("pos")
    table, sort = constants(side)
    table = jnp.asarray(table)
    below = passed_along(object_field, "pos", -1)
    own_count = lax.dynamic_index_in_dim(counts, device_index, keepdims=False)
    not_last = (device_index + 1 < strip_count).astype(jnp.int32)
    info = jnp.stack([own_count, not_last])
    step = (8.0 / jnp.sum(counts).astype(jnp.float32))[None]
    place = jnp.stack([offsets[:, 0] - device_index * strip_rows, offsets[:, 1]], axis=1)
    amps = sorted_amplitudes(amplitudes, sort)
    own, grad_probe, low = iteration(True, False, (place, info), (object_field, below), (probe,), amps, table)
    above = passed_along(low, "pos", 1)
    below = passed_along(own, "pos", -1)
    quarter, halved = quartered(grad_probe, "pos")
    quarter, above, below = lax.optimization_barrier((quarter, above, below))
    probe_sum = gathered(quarter, "pos", halved)
    own, grad_probe, low_re, low_im, probe_now = iteration(
        False, True, (place, info, step), (own, above, low, below), (probe, probe_sum), amps, table
    )
    above_re = passed_along(low_re, "pos", 1)
    quarter, halved = quartered(grad_probe, "pos")
    quarter, above_re, low_im = lax.optimization_barrier((quarter, above_re, low_im))
    above_im = passed_along(low_im, "pos", 1)
    probe_sum = gathered(quarter, "pos", halved)
    return (own + jnp.stack([above_re, above_im]), probe_now - step * probe_sum)


def solution(mesh):
    in_specs = (
        P("groups", "pos", None),
        P("groups", None, None),
        P(("groups", "pos"), None, None),
        P(("groups", "pos"), None),
        P("groups"),
    )
    out_specs = (P("groups", "pos", None), P("groups", None, None))
    return jax.shard_map(
        on_device, mesh=mesh, in_specs=in_specs, out_specs=out_specs, check_vma=False
    )
```

```python
from functools import partial
from itertools import zip_longest
import math

import jax
import jax.numpy as jnp
import numpy as np
from jax import lax
from jax.experimental import pallas as pl
from jax.experimental.pallas import tpu as pltpu
from jax.sharding import PartitionSpec as P

LANE_TILE = 128


def split_bf16(array):
    high = array.astype(jnp.bfloat16)
    low = (array - high.astype(np.float32)).astype(jnp.bfloat16)
    return high, low


def constants(side):
    half = side // 2
    index = np.arange(half)
    parts = []
    for odd in (0, 1):
        angle = 2.0 * np.pi / side * (index[:, None] * (2 * index[None, :] + odd) % side)
        cosine, sine = np.cos(angle), np.sin(angle)
        matrix = (np.block([[cosine, -sine], [sine, cosine]]) / math.sqrt(side)).astype(np.float32)
        parts.append(split_bf16(matrix))
    tables = [[part, part.T] for pair in parts for part in pair]
    order = np.concatenate([np.arange(0, side, 2), np.arange(1, side, 2)])
    sort = np.zeros((side, side), np.float32)
    sort[order, np.arange(side)] = 1.0
    return np.stack([m for pair in tables for m in pair]), sort.astype(jnp.bfloat16)


def permute_kernel(amp_ref, sort_ref, sort_t_ref, out_ref):
    def one(slot, carry):
        rows = jnp.dot(sort_t_ref[...], amp_ref[slot], preferred_element_type=jnp.float32)
        both = jnp.dot(rows.astype(jnp.bfloat16), sort_ref[...], preferred_element_type=jnp.float32)
        out_ref[slot] = both.astype(jnp.bfloat16)
        return carry

    lax.fori_loop(0, amp_ref.shape[0], one, 0)


def sorted_amplitudes(amplitudes, sort):
    return pl.pallas_call(
        permute_kernel,
        out_shape=jax.ShapeDtypeStruct(amplitudes.shape, amplitudes.dtype),
        compiler_params=pltpu.CompilerParams(vmem_limit_bytes=16 * 2**20),
        cost_estimate=pl.CostEstimate(flops=400_000_000, bytes_accessed=1_600_000, transcendentals=0),
        name="sort_amplitudes",
    )(amplitudes, jnp.asarray(sort), jnp.asarray(sort.T))


def hi_lo(value):
    high = value.astype(jnp.bfloat16)
    return high, (value - high.astype(jnp.float32)).astype(jnp.bfloat16)


def matrix(table_ref, odd, turned, axis):
    high, low = table_ref[4 * odd + turned], table_ref[4 * odd + 2 + turned]
    return jnp.concatenate([high, high, low], axis=axis)


def times_right(value, table_ref, odd, turned):
    high, low = hi_lo(value)
    stacked = jnp.concatenate([high, low, high], axis=1)
    return jnp.dot(stacked, matrix(table_ref, odd, turned, 0), preferred_element_type=jnp.float32)


def times_left(table_ref, odd, turned, value):
    high, low = hi_lo(value)
    stacked = jnp.concatenate([high, low, high], axis=0)
    return jnp.dot(matrix(table_ref, odd, turned, 1), stacked, preferred_element_type=jnp.float32)


def lane_rotated(left, right, shift, wrapped):
    left, right = pltpu.roll(left, shift, 1), pltpu.roll(right, shift, 1)
    return jnp.where(wrapped, right, left), jnp.where(wrapped, left, right)


def slot_steps(slot, live, place_ref, amp_ref, probe_ref, table_ref, ext, grad, grad_probe):
    side = probe_ref.shape[1]
    half = side // 2
    row, col = place_ref[slot, 0], place_ref[slot, 1]
    rows = pl.ds(row, side)
    first = col // LANE_TILE
    shift = col - first * LANE_TILE
    third = jnp.minimum(first + 2, ext.shape[1] - 1)
    lanes = lax.broadcasted_iota(jnp.int32, (side, LANE_TILE), 1)
    wrapped = lanes < shift

    def patch(part):
        return jnp.where(wrapped, ext[part, third, rows, :], ext[part, first, rows, :]), ext[part, first + 1, rows, :]

    def probe(part):
        return lane_rotated(probe_ref[part, :, :half], probe_ref[part, :, half:], shift, wrapped)

    patch_re, patch_im = patch(0), patch(1)
    probe_re, probe_im = probe(0), probe(1)
    exit_re = [p * q - r * s for p, q, r, s in zip(probe_re, patch_re, probe_im, patch_im)]
    exit_im = [p * q + r * s for p, q, r, s in zip(probe_re, patch_im, probe_im, patch_re)]
    even = jnp.concatenate([exit_re[0] + exit_re[1], exit_im[0] + exit_im[1]], axis=1)
    odd = jnp.concatenate([exit_re[0] - exit_re[1], exit_im[0] - exit_im[1]], axis=1)
    even = times_right(even, table_ref, 0, 0)
    odd = times_right(odd, table_ref, 1, 0)
    yield
    wave_re = jnp.concatenate([even[:, :half], odd[:, :half]], axis=1)
    wave_im = jnp.concatenate([even[:, half:], odd[:, half:]], axis=1)
    even = jnp.concatenate([wave_re[:half] + wave_re[half:], wave_im[:half] + wave_im[half:]], axis=0)
    odd = jnp.concatenate([wave_re[:half] - wave_re[half:], wave_im[:half] - wave_im[half:]], axis=0)
    even = times_left(table_ref, 0, 1, even)
    odd = times_left(table_ref, 1, 1, odd)
    yield

    def kept(spec, rows):
        spec_re, spec_im = spec[:half], spec[half:]
        amplitude = amp_ref[slot, rows, :].astype(jnp.float32)
        keeping = live - live * amplitude * lax.rsqrt(spec_re * spec_re + spec_im * spec_im + 1.0)
        return jnp.concatenate([spec_re * keeping, spec_im * keeping], axis=0)

    even = times_left(table_ref, 0, 0, kept(even, slice(0, half)))
    odd = times_left(table_ref, 1, 0, kept(odd, slice(half, side)))
    wave_re = jnp.concatenate([even[:half] + odd[:half], even[:half] - odd[:half]], axis=0)
    wave_im = jnp.concatenate([even[half:] + odd[half:], even[half:] - odd[half:]], axis=0)
    yield
    even = times_right(jnp.concatenate([wave_re[:, :half], wave_im[:, :half]], axis=1), table_ref, 0, 1)
    odd = times_right(jnp.concatenate([wave_re[:, half:], wave_im[:, half:]], axis=1), table_ref, 1, 1)
    yield
    resid_re = (even[:, :half] + odd[:, :half], even[:, :half] - odd[:, :half])
    resid_im = (even[:, half:] + odd[:, half:], even[:, half:] - odd[:, half:])
    back = jnp.where(shift == 0, 0, LANE_TILE - shift)
    from_left = lanes < LANE_TILE - shift
    for part in (0, 1):
        if part == 0:
            terms = [p * q + r * s for p, q, r, s in zip(patch_re, resid_re, patch_im, resid_im)]
        else:
            terms = [p * q - r * s for p, q, r, s in zip(patch_re, resid_im, patch_im, resid_re)]
        left, right = (pltpu.roll(term, back, 1) for term in terms)
        grad_probe[part, :, :half] += jnp.where(from_left, left, right)
        grad_probe[part, :, half:] += jnp.where(from_left, right, left)
    for part in (0, 1):
        if part == 0:
            terms = [p * q + r * s for p, q, r, s in zip(probe_re, resid_re, probe_im, resid_im)]
        else:
            terms = [p * q - r * s for p, q, r, s in zip(probe_re, resid_im, probe_im, resid_re)]
        grad[part, first, rows, :] += jnp.where(wrapped, 0.0, terms[0])
        grad[part, first + 1, rows, :] += terms[1]
        grad[part, third, rows, :] += jnp.where(wrapped, terms[0], 0.0)


def iteration_kernel(first, *refs):
    if first:
        place_ref, info_ref, own_hbm, below_hbm, probe_hbm = refs[:5]
        refs = refs[5:]
    else:
        place_ref, info_ref, step_ref, own_hbm, low_hbm = refs[:5]
        above_hbms, below_hbms, probe_hbm, sum_hbm = refs[5:7], refs[7:9], refs[9], refs[10]
        refs = refs[11:]
    amp_hbm, table_hbm, own_out, low_out, grad_out = refs[:5]
    refs = refs[5:]
    if not first:
        probe_out, refs = refs[0], refs[1:]
    ext, grad, probe_ref, grad_probe, amp_ref, table_ref, sems, strip_sems, out_sems = refs
    rows = own_hbm.shape[1]
    columns = ext.shape[1]
    own, low = pl.ds(0, rows), pl.ds(rows, rows)

    def strip_copies(index, hbm, vmem, where, out=False, parts=(0, 1)):
        copies = []
        for part in parts:
            for column in range(columns):
                pair = (hbm.at[part, :, pl.ds(column * LANE_TILE, LANE_TILE)], vmem.at[part, column, where, :])
                sem = (out_sems if out else strip_sems).at[index, part * columns + column]
                copies.append(pltpu.make_async_copy(*(reversed(pair) if out else pair), sem))
        return copies

    pairs = [(probe_hbm, probe_ref)]
    if not first:
        pairs += [(sum_hbm, grad_probe)]
    early = len(pairs)
    pairs += [(table_hbm, table_ref), (amp_hbm, amp_ref)]
    copies = [pltpu.make_async_copy(src, dst, sems.at[i]) for i, (src, dst) in enumerate(pairs)]
    strips = strip_copies(0, own_hbm, ext, own)
    if first:
        strips += strip_copies(1, below_hbm, ext, low)
    else:
        strips += strip_copies(1, low_hbm, grad, low)
    for copy in copies[:early] + strips + copies[early:]:
        copy.start()
    if not first:
        for index, hbms, vmem, where, by_pair in (
            (2, above_hbms, grad, own, info_ref[2]),
            (3, below_hbms, ext, low, info_ref[3]),
        ):
            for choice in (0, 1):

                @pl.when(by_pair == choice)
                def _():
                    for copy in strip_copies(index, hbms[choice], vmem, where):
                        copy.start()

            strips += strip_copies(index, hbms[0], vmem, where)
    for copy in copies[:early]:
        copy.wait()
    if not first:
        probe_ref[...] = probe_ref[...] - step_ref[0] * grad_probe[...]
        probe_copy = pltpu.make_async_copy(probe_ref, probe_out, sems.at[5])
        probe_copy.start()
    power = probe_ref[0] * probe_ref[0] + probe_ref[1] * probe_ref[1]
    rate = 1.0 / (jnp.max(power) + 1e-06)
    grad_probe[...] = jnp.zeros_like(grad_probe)
    for copy in strips + copies[early:]:
        copy.wait()
    if not first:
        ext[...] += grad[...]
    grad[...] = jnp.zeros_like(grad)

    count = info_ref[0]

    def slots(index, carry):
        steps = []
        for slot in (2 * index, 2 * index + 1):
            live = (slot < count).astype(jnp.float32)
            slot = jnp.minimum(slot, amp_ref.shape[0] - 1)
            steps.append(slot_steps(slot, live, place_ref, amp_ref, probe_ref, table_ref, ext, grad, grad_probe))
        for unused in zip_longest(*steps):
            pass
        return carry

    lax.fori_loop(0, (count + 1) // 2, slots, 0)
    outs = [pltpu.make_async_copy(grad_probe, grad_out, sems.at[4])]
    outs[0].start()
    low_rate = rate * info_ref[1].astype(jnp.float32)
    for part in (0, 1):
        grad[part, :, low, :] = -low_rate * grad[part, :, low, :]
        copies = strip_copies(0, low_out, grad, low, True, (part,))
        for copy in copies:
            copy.start()
        outs += copies
    for part in (0, 1):
        ext[part, :, own, :] = ext[part, :, own, :] - rate * grad[part, :, own, :]
        copies = strip_copies(1, own_out, ext, own, True, (part,))
        for copy in copies:
            copy.start()
        outs += copies
    for copy in outs:
        copy.wait()
    if not first:
        probe_copy.wait()


def iteration(first, scalars, objects, probes, amplitudes, table):
    shape = objects[0].shape
    smem = pl.BlockSpec(memory_space=pltpu.SMEM)
    anywhere = pl.BlockSpec(memory_space=pl.ANY)
    probe_shape = jax.ShapeDtypeStruct(probes[0].shape, jnp.float32)
    strip = jax.ShapeDtypeStruct(shape, jnp.float32)
    arrays = (*objects, *probes, amplitudes, table)
    out_shape = [strip, strip, probe_shape] + ([] if first else [probe_shape])
    columns = shape[2] // LANE_TILE
    extended = (shape[0], columns, 2 * shape[1], LANE_TILE)
    return pl.pallas_call(
        partial(iteration_kernel, first),
        out_shape=out_shape,
        in_specs=[smem] * len(scalars) + [anywhere] * len(arrays),
        out_specs=[anywhere] * len(out_shape),
        scratch_shapes=[
            pltpu.VMEM(extended, jnp.float32),
            pltpu.VMEM(extended, jnp.float32),
            pltpu.VMEM(probe_shape.shape, jnp.float32),
            pltpu.VMEM(probe_shape.shape, jnp.float32),
            pltpu.VMEM(amplitudes.shape, amplitudes.dtype),
            pltpu.VMEM(table.shape, table.dtype),
            pltpu.SemaphoreType.DMA((6,)),
            pltpu.SemaphoreType.DMA((4, shape[0] * columns)),
            pltpu.SemaphoreType.DMA((2, shape[0] * columns)),
        ],
        compiler_params=pltpu.CompilerParams(vmem_limit_bytes=62 * 2**20),
        cost_estimate=pl.CostEstimate(flops=8_000_000_000, bytes_accessed=8_000_000, transcendentals=400_000),
        name="iteration",
    )(*scalars, *arrays)


def passed_along(value, axis, by, group=None):
    size = lax.axis_size(axis)
    pairs = [(i, i + by) for i in range(size) if 0 <= i + by < size]
    if group is not None:
        pairs = [pair for pair in pairs if (min(pair) % 4 == 3) == bool(group)]
    return lax.ppermute(value, axis, pairs)


def swapped(value, axis, bit):
    size = lax.axis_size(axis)
    return lax.ppermute(value, axis, [(i, i ^ bit) for i in range(size)])


def summed_beside(value, axis, strips):
    size = lax.axis_size(axis)
    arrays = [array for array, by in strips]
    if size & (size - 1) or size < 8:
        moved = [[passed_along(array, axis, by, group) for array, by in strips] for group in (0, 1)]
        return lax.psum(value, axis), *moved
    index = lax.axis_index(axis)
    bits = [1 << k for k in range(size.bit_length() - 1)]
    bits = [bits[0], *bits[2:], bits[1]]
    early = [passed_along(array, axis, by, 0) for array, by in strips]
    halved = []
    for bit in bits[:2]:
        upper = (index & bit) != 0
        half = value.shape[1] // 2
        first, second = value[:, :half], value[:, half:]
        arrived = swapped(jnp.where(upper, first, second), axis, bit)
        value = jnp.where(upper, second, first) + arrived
        halved.append((bit, upper))
    value, arrays = lax.optimization_barrier((value, arrays))
    late = [passed_along(array, axis, by, 1) for array, (unused, by) in zip(arrays, strips)]
    for bit in bits[2:-1]:
        value = value + swapped(value, axis, bit)
    value, early = lax.optimization_barrier((value, early))
    value = value + swapped(value, axis, bits[-1])
    value, late = lax.optimization_barrier((value, late))
    for bit, upper in reversed(halved):
        other = swapped(value, axis, bit)
        value = jnp.concatenate([jnp.where(upper, other, value), jnp.where(upper, value, other)], axis=1)
    return value, early, late


def on_device(object_field, probe, amplitudes, offsets, counts):
    strip_rows = object_field.shape[1]
    side = probe.shape[1]
    strip_count = lax.axis_size("pos")
    device_index = lax.axis_index("pos")
    table, sort = constants(side)
    table = jnp.asarray(table)
    below = passed_along(object_field, "pos", -1)
    own_count = lax.dynamic_index_in_dim(counts, device_index, keepdims=False)
    not_last = device_index + 1 < strip_count
    from_above, from_below = device_index % 4 == 0, device_index % 4 == 3
    info = jnp.stack([own_count, *(flag.astype(jnp.int32) for flag in (not_last, from_above, from_below))])
    step = (8.0 / jnp.sum(counts).astype(jnp.float32))[None]
    place = jnp.stack([offsets[:, 0] - device_index * strip_rows, offsets[:, 1]], axis=1)
    amps = sorted_amplitudes(amplitudes, sort)
    own, low, grad_probe = iteration(True, (place, info), (object_field, below), (probe,), amps, table)
    probe_sum, early, late = summed_beside(grad_probe, "pos", [(low, 1), (own, -1)])
    strips = (own, low, early[0], late[0], early[1], late[1])
    own, low, grad_probe, probe_now = iteration(
        False, (place, info, step), strips, (probe, probe_sum), amps, table
    )
    probe_sum, early, late = summed_beside(grad_probe, "pos", [(low, 1)])
    above = jnp.where(from_above, late[0], early[0])
    return (own + above, probe_now - step * probe_sum)


def solution(mesh):
    in_specs = (
        P("groups", "pos", None),
        P("groups", None, None),
        P(("groups", "pos"), None, None),
        P(("groups", "pos"), None),
        P("groups"),
    )
    out_specs = (P("groups", "pos", None), P("groups", None, None))
    return jax.shard_map(
        on_device, mesh=mesh, in_specs=in_specs, out_specs=out_specs, check_vma=False
    )
```

```python
from functools import partial
from itertools import zip_longest
import math

import jax
import jax.numpy as jnp
import numpy as np
from jax import lax
from jax.experimental import pallas as pl
from jax.experimental.pallas import tpu as pltpu
from jax.sharding import PartitionSpec as P

LANE_TILE = 128


def split_bf16(array):
    high = array.astype(jnp.bfloat16)
    low = (array - high.astype(np.float32)).astype(jnp.bfloat16)
    return high, low


def constants(side):
    half = side // 2
    index = np.arange(half)
    parts = []
    for odd in (0, 1):
        angle = 2.0 * np.pi / side * (index[:, None] * (2 * index[None, :] + odd) % side)
        cosine, sine = np.cos(angle), np.sin(angle)
        matrix = (np.block([[cosine, -sine], [sine, cosine]]) / math.sqrt(side)).astype(np.float32)
        parts.append(split_bf16(matrix))
    tables = [[part, part.T] for pair in parts for part in pair]
    order = np.concatenate([np.arange(0, side, 2), np.arange(1, side, 2)])
    sort = np.zeros((side, side), np.float32)
    sort[order, np.arange(side)] = 1.0
    return np.stack([m for pair in tables for m in pair]), sort.astype(jnp.bfloat16)


def permute_kernel(amp_ref, sort_ref, sort_t_ref, out_ref):
    def one(slot, carry):
        rows = jnp.dot(sort_t_ref[...], amp_ref[slot], preferred_element_type=jnp.float32)
        both = jnp.dot(rows.astype(jnp.bfloat16), sort_ref[...], preferred_element_type=jnp.float32)
        out_ref[slot] = both.astype(jnp.bfloat16)
        return carry

    lax.fori_loop(0, amp_ref.shape[0], one, 0)


def sorted_amplitudes(amplitudes, sort):
    return pl.pallas_call(
        permute_kernel,
        out_shape=jax.ShapeDtypeStruct(amplitudes.shape, amplitudes.dtype),
        compiler_params=pltpu.CompilerParams(vmem_limit_bytes=63 * 2**20),
        cost_estimate=pl.CostEstimate(flops=400_000_000, bytes_accessed=1_600_000, transcendentals=0),
        name="sort_amplitudes",
    )(amplitudes, jnp.asarray(sort), jnp.asarray(sort.T))


def hi_lo(value):
    high = value.astype(jnp.bfloat16)
    return high, (value - high.astype(jnp.float32)).astype(jnp.bfloat16)


def matrix(table_ref, odd, turned, axis):
    high, low = table_ref[4 * odd + turned], table_ref[4 * odd + 2 + turned]
    return jnp.concatenate([high, high, low], axis=axis)


def times_right(value, table_ref, odd, turned):
    high, low = hi_lo(value)
    stacked = jnp.concatenate([high, low, high], axis=1)
    return jnp.dot(stacked, matrix(table_ref, odd, turned, 0), preferred_element_type=jnp.float32)


def times_left(table_ref, odd, turned, value):
    high, low = hi_lo(value)
    stacked = jnp.concatenate([high, low, high], axis=0)
    return jnp.dot(matrix(table_ref, odd, turned, 1), stacked, preferred_element_type=jnp.float32)


def lane_rotated(left, right, shift, wrapped):
    left, right = pltpu.roll(left, shift, 1), pltpu.roll(right, shift, 1)
    return jnp.where(wrapped, right, left), jnp.where(wrapped, left, right)


def slot_steps(slot, live, descent, place_ref, amp_ref, probe_ref, table_ref, ext, total, grad_probe):
    side = probe_ref.shape[1]
    half = side // 2
    row, col = place_ref[slot, 0], place_ref[slot, 1]
    rows = pl.ds(row, side)
    first = col // LANE_TILE
    shift = col - first * LANE_TILE
    third = jnp.minimum(first + 2, ext.shape[1] - 1)
    lanes = lax.broadcasted_iota(jnp.int32, (side, LANE_TILE), 1)
    wrapped = lanes < shift

    def patch(part):
        return jnp.where(wrapped, ext[part, third, rows, :], ext[part, first, rows, :]), ext[part, first + 1, rows, :]

    def probe(part):
        return lane_rotated(probe_ref[part, :, :half], probe_ref[part, :, half:], shift, wrapped)

    patch_re, patch_im = patch(0), patch(1)
    probe_re, probe_im = probe(0), probe(1)
    exit_re = [p * q - r * s for p, q, r, s in zip(probe_re, patch_re, probe_im, patch_im)]
    exit_im = [p * q + r * s for p, q, r, s in zip(probe_re, patch_im, probe_im, patch_re)]
    even = jnp.concatenate([exit_re[0] + exit_re[1], exit_im[0] + exit_im[1]], axis=1)
    odd = jnp.concatenate([exit_re[0] - exit_re[1], exit_im[0] - exit_im[1]], axis=1)
    even = times_right(even, table_ref, 0, 0)
    odd = times_right(odd, table_ref, 1, 0)
    yield
    wave_re = jnp.concatenate([even[:, :half], odd[:, :half]], axis=1)
    wave_im = jnp.concatenate([even[:, half:], odd[:, half:]], axis=1)
    even = jnp.concatenate([wave_re[:half] + wave_re[half:], wave_im[:half] + wave_im[half:]], axis=0)
    odd = jnp.concatenate([wave_re[:half] - wave_re[half:], wave_im[:half] - wave_im[half:]], axis=0)
    even = times_left(table_ref, 0, 1, even)
    odd = times_left(table_ref, 1, 1, odd)
    yield

    def kept(spec, rows):
        spec_re, spec_im = spec[:half], spec[half:]
        amplitude = amp_ref[slot, rows, :].astype(jnp.float32)
        keeping = live - live * amplitude * lax.rsqrt(spec_re * spec_re + spec_im * spec_im + 1.0)
        return jnp.concatenate([spec_re * keeping, spec_im * keeping], axis=0)

    even = times_left(table_ref, 0, 0, kept(even, slice(0, half)))
    odd = times_left(table_ref, 1, 0, kept(odd, slice(half, side)))
    wave_re = jnp.concatenate([even[:half] + odd[:half], even[:half] - odd[:half]], axis=0)
    wave_im = jnp.concatenate([even[half:] + odd[half:], even[half:] - odd[half:]], axis=0)
    yield
    even = times_right(jnp.concatenate([wave_re[:, :half], wave_im[:, :half]], axis=1), table_ref, 0, 1)
    odd = times_right(jnp.concatenate([wave_re[:, half:], wave_im[:, half:]], axis=1), table_ref, 1, 1)
    yield
    resid_re = (even[:, :half] + odd[:, :half], even[:, :half] - odd[:, :half])
    resid_im = (even[:, half:] + odd[:, half:], even[:, half:] - odd[:, half:])
    back = jnp.where(shift == 0, 0, LANE_TILE - shift)
    from_left = lanes < LANE_TILE - shift
    for part in (0, 1):
        if part == 0:
            terms = [p * q + r * s for p, q, r, s in zip(patch_re, resid_re, patch_im, resid_im)]
        else:
            terms = [p * q - r * s for p, q, r, s in zip(patch_re, resid_im, patch_im, resid_re)]
        left, right = (pltpu.roll(term, back, 1) for term in terms)
        grad_probe[part, :, :half] += jnp.where(from_left, left, right)
        grad_probe[part, :, half:] += jnp.where(from_left, right, left)
    for part in (0, 1):
        if part == 0:
            terms = [p * q + r * s for p, q, r, s in zip(probe_re, resid_re, probe_im, resid_im)]
        else:
            terms = [p * q - r * s for p, q, r, s in zip(probe_re, resid_im, probe_im, resid_re)]
        terms = [descent * term for term in terms]
        total[part, first, rows, :] += jnp.where(wrapped, 0.0, terms[0])
        total[part, first + 1, rows, :] += terms[1]
        total[part, third, rows, :] += jnp.where(wrapped, terms[0], 0.0)


def iteration_kernel(first, *refs):
    if first:
        place_ref, info_ref, own_hbm, below_hbm, probe_hbm = refs[:5]
        refs = refs[5:]
    else:
        place_ref, info_ref, step_ref, own_hbm, above_hbm, low_hbm, below_hbm, probe_hbm = refs[:8]
        sum_hbms, refs = refs[8:10], refs[10:]
    amp_hbm, table_hbm, own_out, keep_out, send_out = refs[:5]
    refs = refs[5:]
    if first:
        low_outs, refs = refs[:1], refs[1:]
    else:
        low_outs, probe_out, refs = refs[:2], refs[2], refs[3:]
    ext, total, probe_ref, grad_probe, amp_ref, table_ref, sems, in_sems, out_sems = refs
    rows = own_hbm.shape[1]
    columns = ext.shape[1]
    half = probe_ref.shape[1] // 2
    own, low = pl.ds(0, rows), pl.ds(rows, rows)
    mine = pl.ds(pl.multiple_of(info_ref[2] * half, half), half)
    others = pl.ds(pl.multiple_of((1 - info_ref[2]) * half, half), half)

    def strip_pairs(hbm, vmem, start, part):
        where = pl.ds(start, hbm.shape[1])
        return [
            (hbm.at[part, :, pl.ds(LANE_TILE * column, LANE_TILE)], vmem.at[part, column, where, :])
            for column in range(columns)
        ]

    pairs = [(probe_hbm, probe_ref)]
    if not first:
        pairs += [(sum_hbms[0], grad_probe.at[:, mine, :]), (sum_hbms[1], grad_probe.at[:, others, :])]
    early = len(pairs)
    strips = [(own_hbm, ext, 0), (below_hbm, ext, rows)]
    if not first:
        strips += [(above_hbm, total, 0), (low_hbm, total, rows)]
    for hbm, vmem, start in strips:
        pairs += strip_pairs(hbm, vmem, start, 0) + strip_pairs(hbm, vmem, start, 1)
    pairs += [(table_hbm, table_ref), (amp_hbm, amp_ref)]
    copies = [pltpu.make_async_copy(src, dst, in_sems.at[i]) for i, (src, dst) in enumerate(pairs)]
    for copy in copies:
        copy.start()
    if first:
        total[:, :, low, :] = jnp.zeros((2, columns, rows, LANE_TILE), jnp.float32)
    for copy in copies[:early]:
        copy.wait()
    if not first:
        probe_ref[...] = probe_ref[...] - step_ref[0] * grad_probe[...]
        probe_copy = pltpu.make_async_copy(probe_ref, probe_out, sems.at[2])
        probe_copy.start()
    power = probe_ref[0] * probe_ref[0] + probe_ref[1] * probe_ref[1]
    descent = -1.0 / (jnp.max(power) + 1e-06)
    grad_probe[...] = jnp.zeros_like(grad_probe)
    for copy in copies[early:]:
        copy.wait()
    if first:
        total[:, :, own, :] = ext[:, :, own, :]
    else:
        now = ext[:, :, own, :] + total[:, :, own, :]
        ext[:, :, own, :] = now
        total[:, :, own, :] = now
        ext[:, :, low, :] += total[:, :, low, :]
        total[:, :, low, :] = jnp.zeros((2, columns, rows, LANE_TILE), jnp.float32)

    count = info_ref[0]

    def slots(index, carry):
        steps = []
        for slot in (2 * index, 2 * index + 1):
            live = (slot < count).astype(jnp.float32)
            slot = jnp.minimum(slot, amp_ref.shape[0] - 1)
            steps.append(
                slot_steps(slot, live, descent, place_ref, amp_ref, probe_ref, table_ref, ext, total, grad_probe)
            )
        for unused in zip_longest(*steps):
            pass
        return carry

    lax.fori_loop(0, (count + 1) // 2, slots, 0)

    @pl.when(info_ref[1] == 0)
    def _():
        total[:, :, low, :] = jnp.zeros((2, columns, rows, LANE_TILE), jnp.float32)

    outs = [
        pltpu.make_async_copy(grad_probe.at[:, others, :], send_out, sems.at[0]),
        pltpu.make_async_copy(grad_probe.at[:, mine, :], keep_out, sems.at[1]),
    ]
    pairs = []
    start = rows
    for low_out in low_outs:
        pairs += strip_pairs(low_out, total, start, 0) + strip_pairs(low_out, total, start, 1)
        start += low_out.shape[1]
    pairs += strip_pairs(own_out, total, 0, 0) + strip_pairs(own_out, total, 0, 1)
    outs += [pltpu.make_async_copy(src, dst, out_sems.at[i]) for i, (dst, src) in enumerate(pairs)]
    for copy in outs:
        copy.start()
    for copy in outs:
        copy.wait()
    if not first:
        probe_copy.wait()


def iteration(first, scalars, objects, probes, amplitudes, table):
    parts, rows, width = objects[0].shape
    smem = pl.BlockSpec(memory_space=pltpu.SMEM)
    anywhere = pl.BlockSpec(memory_space=pl.ANY)
    probe_shape = jax.ShapeDtypeStruct(probes[0].shape, jnp.float32)
    half_shape = jax.ShapeDtypeStruct((parts, probe_shape.shape[1] // 2, probe_shape.shape[2]), jnp.float32)
    arrays = (*objects, *probes, amplitudes, table)
    low_rows = [rows] if first else [rows * 3 // 8, rows - rows * 3 // 8]
    strips = [jax.ShapeDtypeStruct((parts, r, width), jnp.float32) for r in [rows, *low_rows]]
    out_shape = [strips[0], half_shape, half_shape, *strips[1:]] + ([] if first else [probe_shape])
    columns = width // LANE_TILE
    extended = (parts, columns, 2 * rows, LANE_TILE)
    return pl.pallas_call(
        partial(iteration_kernel, first),
        out_shape=out_shape,
        in_specs=[smem] * len(scalars) + [anywhere] * len(arrays),
        out_specs=[anywhere] * len(out_shape),
        scratch_shapes=[
            pltpu.VMEM(extended, jnp.float32),
            pltpu.VMEM(extended, jnp.float32),
            pltpu.VMEM(probe_shape.shape, jnp.float32),
            pltpu.VMEM(probe_shape.shape, jnp.float32),
            pltpu.VMEM(amplitudes.shape, amplitudes.dtype),
            pltpu.VMEM(table.shape, table.dtype),
            pltpu.SemaphoreType.DMA((3,)),
            pltpu.SemaphoreType.DMA((5 + 4 * parts * columns,)),
            pltpu.SemaphoreType.DMA((3 * parts * columns,)),
        ],
        compiler_params=pltpu.CompilerParams(vmem_limit_bytes=62 * 2**20),
        cost_estimate=pl.CostEstimate(flops=8_000_000_000, bytes_accessed=8_000_000, transcendentals=400_000),
        name="iteration",
    )(*scalars, *arrays)


def passed_along(value, axis, by):
    size = lax.axis_size(axis)
    pairs = [(i, i + by) for i in range(size) if 0 <= i + by < size]
    return lax.ppermute(value, axis, pairs)


def swapped(value, axis, bit):
    size = lax.axis_size(axis)
    return lax.ppermute(value, axis, [(i, i ^ bit) for i in range(size)])


def upper_of(axis, bit):
    return (lax.axis_index(axis) & bit) != 0


def bits_of(axis):
    size = lax.axis_size(axis)
    if size & (size - 1) or size < 8:
        return []
    bits = [1 << k for k in range(size.bit_length() - 1)]
    return [bits[0], *bits[2:], bits[1]]


def joined(mine, other, upper):
    return jnp.concatenate([jnp.where(upper, other, mine), jnp.where(upper, mine, other)], axis=1)


def scattered(keep, send, axis):
    bits = bits_of(axis)
    if not bits:
        return lax.psum(joined(keep, send, upper_of(axis, 1)), axis)
    value = keep + swapped(send, axis, bits[0])
    upper = upper_of(axis, bits[1])
    half = value.shape[1] // 2
    first, second = value[:, :half], value[:, half:]
    arrived = swapped(jnp.where(upper, first, second), axis, bits[1])
    value = jnp.where(upper, second, first) + arrived
    for bit in bits[2:]:
        value = value + swapped(value, axis, bit)
    return value


def gathered(value, axis):
    bits = bits_of(axis)
    upper = upper_of(axis, 1)
    if not bits:
        half = value.shape[1] // 2
        first, second = value[:, :half], value[:, half:]
        return jnp.where(upper, second, first), jnp.where(upper, first, second)
    value = joined(value, swapped(value, axis, bits[1]), upper_of(axis, bits[1]))
    return value, swapped(value, axis, bits[0])


def on_device(object_field, probe, amplitudes, offsets, counts):
    strip_rows = object_field.shape[1]
    side = probe.shape[1]
    strip_count = lax.axis_size("pos")
    device_index = lax.axis_index("pos")
    table, sort = constants(side)
    table = jnp.asarray(table)
    below = passed_along(object_field, "pos", -1)
    own_count = lax.dynamic_index_in_dim(counts, device_index, keepdims=False)
    not_last = (device_index + 1 < strip_count).astype(jnp.int32)
    info = jnp.stack([own_count, not_last, device_index % 2])
    step = (8.0 / jnp.sum(counts).astype(jnp.float32))[None]
    place = jnp.stack([offsets[:, 0] - device_index * strip_rows, offsets[:, 1]], axis=1)
    amps = sorted_amplitudes(amplitudes, sort)
    own, keep, send, low = iteration(True, (place, info), (object_field, below), (probe,), amps, table)
    above = passed_along(low, "pos", 1)
    below = passed_along(own, "pos", -1)
    quarter = scattered(keep, send, "pos")
    quarter, above, below = lax.optimization_barrier((quarter, above, below))
    halves = gathered(quarter, "pos")
    own, keep, send, low_top, low_rest, probe_now = iteration(
        False, (place, info, step), (own, above, low, below), (probe, *halves), amps, table
    )
    above_top = passed_along(low_top, "pos", 1)
    quarter = scattered(keep, send, "pos")
    quarter, above_top, low_rest = lax.optimization_barrier((quarter, above_top, low_rest))
    above_rest = passed_along(low_rest, "pos", 1)
    probe_sum = joined(*gathered(quarter, "pos"), upper_of("pos", 1))
    return (own + jnp.concatenate([above_top, above_rest], axis=1), probe_now - step * probe_sum)


def solution(mesh):
    in_specs = (
        P("groups", "pos", None),
        P("groups", None, None),
        P(("groups", "pos"), None, None),
        P(("groups", "pos"), None),
        P("groups"),
    )
    out_specs = (P("groups", "pos", None), P("groups", None, None))
    return jax.shard_map(
        on_device, mesh=mesh, in_specs=in_specs, out_specs=out_specs, check_vma=False
    )
```

```python
from functools import partial
from itertools import zip_longest
import math

import jax
import jax.numpy as jnp
import numpy as np
from jax import lax
from jax.experimental import pallas as pl
from jax.experimental.pallas import tpu as pltpu
from jax.sharding import PartitionSpec as P

LANE_TILE = 128


def split_bf16(array):
    high = array.astype(jnp.bfloat16)
    low = (array - high.astype(np.float32)).astype(jnp.bfloat16)
    return high, low


def constants(side):
    half = side // 2
    index = np.arange(half)
    parts = []
    for odd in (0, 1):
        angle = 2.0 * np.pi / side * (index[:, None] * (2 * index[None, :] + odd) % side)
        cosine, sine = np.cos(angle), np.sin(angle)
        matrix = (np.block([[cosine, -sine], [sine, cosine]]) / math.sqrt(side)).astype(np.float32)
        parts.append(split_bf16(matrix))
    tables = [[part, part.T] for pair in parts for part in pair]
    order = np.concatenate([np.arange(0, side, 2), np.arange(1, side, 2)])
    sort = np.zeros((side, side), np.float32)
    sort[order, np.arange(side)] = 1.0
    return np.stack([m for pair in tables for m in pair]), sort.astype(jnp.bfloat16)


def permute_kernel(amp_ref, sort_ref, sort_t_ref, out_ref):
    def one(slot, carry):
        rows = jnp.dot(sort_t_ref[...], amp_ref[slot], preferred_element_type=jnp.float32)
        both = jnp.dot(rows.astype(jnp.bfloat16), sort_ref[...], preferred_element_type=jnp.float32)
        out_ref[slot] = both.astype(jnp.bfloat16)
        return carry

    lax.fori_loop(0, amp_ref.shape[0], one, 0)


def sorted_amplitudes(amplitudes, sort):
    return pl.pallas_call(
        permute_kernel,
        out_shape=jax.ShapeDtypeStruct(amplitudes.shape, amplitudes.dtype),
        compiler_params=pltpu.CompilerParams(vmem_limit_bytes=63 * 2**20),
        cost_estimate=pl.CostEstimate(flops=400_000_000, bytes_accessed=1_600_000, transcendentals=0),
        name="sort_amplitudes",
    )(amplitudes, jnp.asarray(sort), jnp.asarray(sort.T))


def hi_lo(value):
    high = value.astype(jnp.bfloat16)
    return high, (value - high.astype(jnp.float32)).astype(jnp.bfloat16)


def matrix(table_ref, odd, turned, axis):
    high, low = table_ref[4 * odd + turned], table_ref[4 * odd + 2 + turned]
    return jnp.concatenate([high, high, low], axis=axis)


def times_right(value, table_ref, odd, turned):
    high, low = hi_lo(value)
    stacked = jnp.concatenate([high, low, high], axis=1)
    return jnp.dot(stacked, matrix(table_ref, odd, turned, 0), preferred_element_type=jnp.float32)


def times_left(table_ref, odd, turned, value):
    high, low = hi_lo(value)
    stacked = jnp.concatenate([high, low, high], axis=0)
    return jnp.dot(matrix(table_ref, odd, turned, 1), stacked, preferred_element_type=jnp.float32)


def lane_rotated(left, right, shift, wrapped):
    left, right = pltpu.roll(left, shift, 1), pltpu.roll(right, shift, 1)
    return jnp.where(wrapped, right, left), jnp.where(wrapped, left, right)


def slot_steps(slot, live, descent, place_ref, amp_ref, probe_ref, table_ref, ext, total, grad_probe):
    side = probe_ref.shape[1]
    half = side // 2
    row, col = place_ref[slot, 0], place_ref[slot, 1]
    rows = pl.ds(row, side)
    first = col // LANE_TILE
    shift = col - first * LANE_TILE
    third = jnp.minimum(first + 2, ext.shape[1] - 1)
    lanes = lax.broadcasted_iota(jnp.int32, (side, LANE_TILE), 1)
    wrapped = lanes < shift

    def patch(part):
        return jnp.where(wrapped, ext[part, third, rows, :], ext[part, first, rows, :]), ext[part, first + 1, rows, :]

    def probe(part):
        return lane_rotated(probe_ref[part, :, :half], probe_ref[part, :, half:], shift, wrapped)

    patch_re, patch_im = patch(0), patch(1)
    probe_re, probe_im = probe(0), probe(1)
    exit_re = [p * q - r * s for p, q, r, s in zip(probe_re, patch_re, probe_im, patch_im)]
    exit_im = [p * q + r * s for p, q, r, s in zip(probe_re, patch_im, probe_im, patch_re)]
    even = jnp.concatenate([exit_re[0] + exit_re[1], exit_im[0] + exit_im[1]], axis=1)
    odd = jnp.concatenate([exit_re[0] - exit_re[1], exit_im[0] - exit_im[1]], axis=1)
    even = times_right(even, table_ref, 0, 0)
    odd = times_right(odd, table_ref, 1, 0)
    yield
    wave_re = jnp.concatenate([even[:, :half], odd[:, :half]], axis=1)
    wave_im = jnp.concatenate([even[:, half:], odd[:, half:]], axis=1)
    even = jnp.concatenate([wave_re[:half] + wave_re[half:], wave_im[:half] + wave_im[half:]], axis=0)
    odd = jnp.concatenate([wave_re[:half] - wave_re[half:], wave_im[:half] - wave_im[half:]], axis=0)
    even = times_left(table_ref, 0, 1, even)
    odd = times_left(table_ref, 1, 1, odd)
    yield

    def kept(spec, rows):
        spec_re, spec_im = spec[:half], spec[half:]
        amplitude = amp_ref[slot, rows, :].astype(jnp.float32)
        keeping = live - live * amplitude * lax.rsqrt(spec_re * spec_re + spec_im * spec_im + 1.0)
        return jnp.concatenate([spec_re * keeping, spec_im * keeping], axis=0)

    even = times_left(table_ref, 0, 0, kept(even, slice(0, half)))
    odd = times_left(table_ref, 1, 0, kept(odd, slice(half, side)))
    wave_re = jnp.concatenate([even[:half] + odd[:half], even[:half] - odd[:half]], axis=0)
    wave_im = jnp.concatenate([even[half:] + odd[half:], even[half:] - odd[half:]], axis=0)
    yield
    even = times_right(jnp.concatenate([wave_re[:, :half], wave_im[:, :half]], axis=1), table_ref, 0, 1)
    odd = times_right(jnp.concatenate([wave_re[:, half:], wave_im[:, half:]], axis=1), table_ref, 1, 1)
    yield
    resid_re = (even[:, :half] + odd[:, :half], even[:, :half] - odd[:, :half])
    resid_im = (even[:, half:] + odd[:, half:], even[:, half:] - odd[:, half:])
    back = jnp.where(shift == 0, 0, LANE_TILE - shift)
    from_left = lanes < LANE_TILE - shift
    for part in (0, 1):
        if part == 0:
            terms = [p * q + r * s for p, q, r, s in zip(patch_re, resid_re, patch_im, resid_im)]
        else:
            terms = [p * q - r * s for p, q, r, s in zip(patch_re, resid_im, patch_im, resid_re)]
        left, right = (pltpu.roll(term, back, 1) for term in terms)
        grad_probe[part, :, :half] += jnp.where(from_left, left, right)
        grad_probe[part, :, half:] += jnp.where(from_left, right, left)
    for part in (0, 1):
        if part == 0:
            terms = [p * q + r * s for p, q, r, s in zip(probe_re, resid_re, probe_im, resid_im)]
        else:
            terms = [p * q - r * s for p, q, r, s in zip(probe_re, resid_im, probe_im, resid_re)]
        terms = [descent * term for term in terms]
        total[part, first, rows, :] += jnp.where(wrapped, 0.0, terms[0])
        total[part, first + 1, rows, :] += terms[1]
        total[part, third, rows, :] += jnp.where(wrapped, terms[0], 0.0)


def iteration_kernel(first, *refs):
    if first:
        place_ref, info_ref, own_hbm, below_hbm, probe_hbm = refs[:5]
        refs = refs[5:]
    else:
        place_ref, info_ref, step_ref, own_hbm, above_hbm, low_hbm, below_hbm, probe_hbm = refs[:8]
        sum_hbms, refs = refs[8:10], refs[10:]
    amp_hbm, table_hbm, own_out, low_out, keep_out, send_out = refs[:6]
    refs = refs[6:]
    if not first:
        probe_out, refs = refs[0], refs[1:]
    ext, total, probe_ref, grad_probe, amp_ref, table_ref, sems, in_sems, out_sems = refs
    rows = own_hbm.shape[1]
    columns = ext.shape[1]
    half = probe_ref.shape[1] // 2
    own, low = pl.ds(0, rows), pl.ds(rows, rows)
    mine = pl.ds(pl.multiple_of(info_ref[2] * half, half), half)
    others = pl.ds(pl.multiple_of((1 - info_ref[2]) * half, half), half)

    def strip_pairs(hbm, vmem, start, part):
        where = pl.ds(start, hbm.shape[1])
        return [
            (hbm.at[part, :, pl.ds(LANE_TILE * column, LANE_TILE)], vmem.at[part, column, where, :])
            for column in range(columns)
        ]

    pairs = [(probe_hbm, probe_ref)]
    if not first:
        pairs += [(sum_hbms[0], grad_probe.at[:, mine, :]), (sum_hbms[1], grad_probe.at[:, others, :])]
    early = len(pairs)
    strips = [(own_hbm, ext, 0), (below_hbm, ext, rows)]
    if not first:
        strips += [(above_hbm, total, 0), (low_hbm, total, rows)]
    for hbm, vmem, start in strips:
        pairs += strip_pairs(hbm, vmem, start, 0) + strip_pairs(hbm, vmem, start, 1)
    pairs += [(table_hbm, table_ref), (amp_hbm, amp_ref)]
    copies = [pltpu.make_async_copy(src, dst, in_sems.at[i]) for i, (src, dst) in enumerate(pairs)]
    for copy in copies:
        copy.start()
    if first:
        total[:, :, low, :] = jnp.zeros((2, columns, rows, LANE_TILE), jnp.float32)
    for copy in copies[:early]:
        copy.wait()
    if not first:
        probe_ref[...] = probe_ref[...] - step_ref[0] * grad_probe[...]
        probe_copy = pltpu.make_async_copy(probe_ref, probe_out, sems.at[2])
        probe_copy.start()
    power = probe_ref[0] * probe_ref[0] + probe_ref[1] * probe_ref[1]
    descent = -1.0 / (jnp.max(power) + 1e-06)
    grad_probe[...] = jnp.zeros_like(grad_probe)
    for copy in copies[early:]:
        copy.wait()
    if first:
        total[:, :, own, :] = ext[:, :, own, :]
    else:
        now = ext[:, :, own, :] + total[:, :, own, :]
        ext[:, :, own, :] = now
        total[:, :, own, :] = now
        ext[:, :, low, :] += total[:, :, low, :]
        total[:, :, low, :] = jnp.zeros((2, columns, rows, LANE_TILE), jnp.float32)

    count = info_ref[0]

    def slots(index, carry):
        steps = []
        for slot in (2 * index, 2 * index + 1):
            live = (slot < count).astype(jnp.float32)
            slot = jnp.minimum(slot, amp_ref.shape[0] - 1)
            steps.append(
                slot_steps(slot, live, descent, place_ref, amp_ref, probe_ref, table_ref, ext, total, grad_probe)
            )
        for unused in zip_longest(*steps):
            pass
        return carry

    lax.fori_loop(0, (count + 1) // 2, slots, 0)

    @pl.when(info_ref[1] == 0)
    def _():
        total[:, :, low, :] = jnp.zeros((2, columns, rows, LANE_TILE), jnp.float32)

    outs = [
        pltpu.make_async_copy(grad_probe.at[:, others, :], send_out, sems.at[0]),
        pltpu.make_async_copy(grad_probe.at[:, mine, :], keep_out, sems.at[1]),
    ]
    pairs = []
    for strip_out, start in ((low_out, rows), (own_out, 0)):
        pairs += strip_pairs(strip_out, total, start, 0) + strip_pairs(strip_out, total, start, 1)
    outs += [pltpu.make_async_copy(src, dst, out_sems.at[i]) for i, (dst, src) in enumerate(pairs)]
    for copy in outs:
        copy.start()
    for copy in outs:
        copy.wait()
    if not first:
        probe_copy.wait()


def iteration(first, scalars, objects, probes, amplitudes, table):
    parts, rows, width = objects[0].shape
    smem = pl.BlockSpec(memory_space=pltpu.SMEM)
    anywhere = pl.BlockSpec(memory_space=pl.ANY)
    probe_shape = jax.ShapeDtypeStruct(probes[0].shape, jnp.float32)
    half_shape = jax.ShapeDtypeStruct((parts, probe_shape.shape[1] // 2, probe_shape.shape[2]), jnp.float32)
    arrays = (*objects, *probes, amplitudes, table)
    strip = jax.ShapeDtypeStruct((parts, rows, width), jnp.float32)
    out_shape = [strip, strip, half_shape, half_shape] + ([] if first else [probe_shape])
    columns = width // LANE_TILE
    extended = (parts, columns, 2 * rows, LANE_TILE)
    return pl.pallas_call(
        partial(iteration_kernel, first),
        out_shape=out_shape,
        in_specs=[smem] * len(scalars) + [anywhere] * len(arrays),
        out_specs=[anywhere] * len(out_shape),
        scratch_shapes=[
            pltpu.VMEM(extended, jnp.float32),
            pltpu.VMEM(extended, jnp.float32),
            pltpu.VMEM(probe_shape.shape, jnp.float32),
            pltpu.VMEM(probe_shape.shape, jnp.float32),
            pltpu.VMEM(amplitudes.shape, amplitudes.dtype),
            pltpu.VMEM(table.shape, table.dtype),
            pltpu.SemaphoreType.DMA((3,)),
            pltpu.SemaphoreType.DMA((5 + 4 * parts * columns,)),
            pltpu.SemaphoreType.DMA((2 * parts * columns,)),
        ],
        compiler_params=pltpu.CompilerParams(vmem_limit_bytes=62 * 2**20),
        cost_estimate=pl.CostEstimate(flops=8_000_000_000, bytes_accessed=8_000_000, transcendentals=400_000),
        name="iteration",
    )(*scalars, *arrays)


def passed_along(value, axis, by):
    size = lax.axis_size(axis)
    pairs = [(i, i + by) for i in range(size) if 0 <= i + by < size]
    return lax.ppermute(value, axis, pairs)


def swapped(value, axis, bit):
    size = lax.axis_size(axis)
    return lax.ppermute(value, axis, [(i, i ^ bit) for i in range(size)])


def upper_of(axis, bit):
    return (lax.axis_index(axis) & bit) != 0


def joined(mine, other, upper):
    return jnp.concatenate([jnp.where(upper, other, mine), jnp.where(upper, mine, other)], axis=1)


def by_pairs(axis):
    size = lax.axis_size(axis)
    return size & (size - 1) == 0 and size >= 4


def crossed(value, axis, bit, keepers):
    size = lax.axis_size(axis)
    return lax.ppermute(value, axis, [(i, i ^ bit) for i in range(size) if (i % 4 in (1, 2)) == keepers])


def scattered(keep, send, axis):
    if not by_pairs(axis):
        return lax.psum(joined(keep, send, upper_of(axis, 1)), axis)
    value = keep + swapped(send, axis, 1)
    value = value + crossed(value, axis, 2, False)
    bit = 4
    while bit < lax.axis_size(axis):
        value = value + crossed(value, axis, bit, True)
        bit *= 2
    return value


def gathered(value, axis):
    upper = upper_of(axis, 1)
    if not by_pairs(axis):
        half = value.shape[1] // 2
        first, second = value[:, :half], value[:, half:]
        return jnp.where(upper, second, first), jnp.where(upper, first, second)
    keeps = upper != upper_of(axis, 2)
    value = jnp.where(keeps, value, crossed(value, axis, 2, True))
    return value, swapped(value, axis, 1)


def on_device(object_field, probe, amplitudes, offsets, counts):
    strip_rows = object_field.shape[1]
    side = probe.shape[1]
    strip_count = lax.axis_size("pos")
    device_index = lax.axis_index("pos")
    table, sort = constants(side)
    table = jnp.asarray(table)
    below = passed_along(object_field, "pos", -1)
    own_count = lax.dynamic_index_in_dim(counts, device_index, keepdims=False)
    not_last = (device_index + 1 < strip_count).astype(jnp.int32)
    info = jnp.stack([own_count, not_last, device_index % 2])
    step = (8.0 / jnp.sum(counts).astype(jnp.float32))[None]
    place = jnp.stack([offsets[:, 0] - device_index * strip_rows, offsets[:, 1]], axis=1)
    amps = sorted_amplitudes(amplitudes, sort)
    own, low, keep, send = iteration(True, (place, info), (object_field, below), (probe,), amps, table)
    above = passed_along(low, "pos", 1)
    below = passed_along(own, "pos", -1)
    part = scattered(keep, send, "pos")
    part, above, below = lax.optimization_barrier((part, above, below))
    halves = gathered(part, "pos")
    own, low, keep, send, probe_now = iteration(
        False, (place, info, step), (own, above, low, below), (probe, *halves), amps, table
    )
    above = passed_along(low, "pos", 1)
    part = scattered(keep, send, "pos")
    part, above = lax.optimization_barrier((part, above))
    probe_sum = joined(*gathered(part, "pos"), upper_of("pos", 1))
    return (own + above, probe_now - step * probe_sum)


def solution(mesh):
    in_specs = (
        P("groups", "pos", None),
        P("groups", None, None),
        P(("groups", "pos"), None, None),
        P(("groups", "pos"), None),
        P("groups"),
    )
    out_specs = (P("groups", "pos", None), P("groups", None, None))
    return jax.shard_map(
        on_device, mesh=mesh, in_specs=in_specs, out_specs=out_specs, check_vma=False
    )
```

```python
from functools import partial
from itertools import zip_longest
import math

import jax
import jax.numpy as jnp
import numpy as np
from jax import lax
from jax.experimental import pallas as pl
from jax.experimental.pallas import tpu as pltpu
from jax.sharding import PartitionSpec as P

LANE_TILE = 128


def split_bf16(array):
    high = array.astype(jnp.bfloat16)
    low = (array - high.astype(np.float32)).astype(jnp.bfloat16)
    return high, low


def constants(side):
    half = side // 2
    index = np.arange(half)
    parts = []
    for odd in (0, 1):
        angle = 2.0 * np.pi / side * (index[:, None] * (2 * index[None, :] + odd) % side)
        cosine, sine = np.cos(angle), np.sin(angle)
        matrix = (np.block([[cosine, -sine], [sine, cosine]]) / math.sqrt(side)).astype(np.float32)
        parts.append(split_bf16(matrix))
    tables = [[part, part.T] for pair in parts for part in pair]
    order = np.concatenate([np.arange(0, side, 2), np.arange(1, side, 2)])
    sort = np.zeros((side, side), np.float32)
    sort[order, np.arange(side)] = 1.0
    return np.stack([m for pair in tables for m in pair]), sort.astype(jnp.bfloat16)


def permute_kernel(amp_ref, sort_ref, sort_t_ref, out_ref):
    def one(slot, carry):
        rows = jnp.dot(sort_t_ref[...], amp_ref[slot], preferred_element_type=jnp.float32)
        both = jnp.dot(rows.astype(jnp.bfloat16), sort_ref[...], preferred_element_type=jnp.float32)
        out_ref[slot] = both.astype(jnp.bfloat16)
        return carry

    lax.fori_loop(0, amp_ref.shape[0], one, 0)


def sorted_amplitudes(amplitudes, sort):
    return pl.pallas_call(
        permute_kernel,
        out_shape=jax.ShapeDtypeStruct(amplitudes.shape, amplitudes.dtype),
        compiler_params=pltpu.CompilerParams(vmem_limit_bytes=63 * 2**20),
        cost_estimate=pl.CostEstimate(flops=400_000_000, bytes_accessed=1_600_000, transcendentals=0),
        name="sort_amplitudes",
    )(amplitudes, jnp.asarray(sort), jnp.asarray(sort.T))


def hi_lo(value):
    high = value.astype(jnp.bfloat16)
    return high, (value - high.astype(jnp.float32)).astype(jnp.bfloat16)


def matrix(table_ref, odd, turned, axis):
    high, low = table_ref[4 * odd + turned], table_ref[4 * odd + 2 + turned]
    return jnp.concatenate([high, high, low], axis=axis)


def times_right(value, table_ref, odd, turned):
    high, low = hi_lo(value)
    stacked = jnp.concatenate([high, low, high], axis=1)
    return jnp.dot(stacked, matrix(table_ref, odd, turned, 0), preferred_element_type=jnp.float32)


def times_left(table_ref, odd, turned, value):
    high, low = hi_lo(value)
    stacked = jnp.concatenate([high, low, high], axis=0)
    return jnp.dot(matrix(table_ref, odd, turned, 1), stacked, preferred_element_type=jnp.float32)


def lane_rotated(left, right, shift, wrapped):
    left, right = pltpu.roll(left, shift, 1), pltpu.roll(right, shift, 1)
    return jnp.where(wrapped, right, left), jnp.where(wrapped, left, right)


def slot_steps(slot, live, descent, place_ref, amp_ref, probe_ref, table_ref, ext, total, grad_probe):
    side = probe_ref.shape[1]
    half = side // 2
    row, col = place_ref[slot, 0], place_ref[slot, 1]
    rows = pl.ds(row, side)
    first = col // LANE_TILE
    shift = col - first * LANE_TILE
    third = jnp.minimum(first + 2, ext.shape[1] - 1)
    lanes = lax.broadcasted_iota(jnp.int32, (side, LANE_TILE), 1)
    wrapped = lanes < shift

    def patch(part):
        return jnp.where(wrapped, ext[part, third, rows, :], ext[part, first, rows, :]), ext[part, first + 1, rows, :]

    def probe(part):
        return lane_rotated(probe_ref[part, :, :half], probe_ref[part, :, half:], shift, wrapped)

    patch_re, patch_im = patch(0), patch(1)
    probe_re, probe_im = probe(0), probe(1)
    exit_re = [p * q - r * s for p, q, r, s in zip(probe_re, patch_re, probe_im, patch_im)]
    exit_im = [p * q + r * s for p, q, r, s in zip(probe_re, patch_im, probe_im, patch_re)]
    even = jnp.concatenate([exit_re[0] + exit_re[1], exit_im[0] + exit_im[1]], axis=1)
    odd = jnp.concatenate([exit_re[0] - exit_re[1], exit_im[0] - exit_im[1]], axis=1)
    even = times_right(even, table_ref, 0, 0)
    odd = times_right(odd, table_ref, 1, 0)
    yield
    wave_re = jnp.concatenate([even[:, :half], odd[:, :half]], axis=1)
    wave_im = jnp.concatenate([even[:, half:], odd[:, half:]], axis=1)
    even = jnp.concatenate([wave_re[:half] + wave_re[half:], wave_im[:half] + wave_im[half:]], axis=0)
    odd = jnp.concatenate([wave_re[:half] - wave_re[half:], wave_im[:half] - wave_im[half:]], axis=0)
    even = times_left(table_ref, 0, 1, even)
    odd = times_left(table_ref, 1, 1, odd)
    yield

    def kept(spec, rows):
        spec_re, spec_im = spec[:half], spec[half:]
        amplitude = amp_ref[slot, rows, :].astype(jnp.float32)
        keeping = live - live * amplitude * lax.rsqrt(spec_re * spec_re + spec_im * spec_im + 1.0)
        return jnp.concatenate([spec_re * keeping, spec_im * keeping], axis=0)

    even = times_left(table_ref, 0, 0, kept(even, slice(0, half)))
    odd = times_left(table_ref, 1, 0, kept(odd, slice(half, side)))
    wave_re = jnp.concatenate([even[:half] + odd[:half], even[:half] - odd[:half]], axis=0)
    wave_im = jnp.concatenate([even[half:] + odd[half:], even[half:] - odd[half:]], axis=0)
    yield
    even = times_right(jnp.concatenate([wave_re[:, :half], wave_im[:, :half]], axis=1), table_ref, 0, 1)
    odd = times_right(jnp.concatenate([wave_re[:, half:], wave_im[:, half:]], axis=1), table_ref, 1, 1)
    yield
    resid_re = (even[:, :half] + odd[:, :half], even[:, :half] - odd[:, :half])
    resid_im = (even[:, half:] + odd[:, half:], even[:, half:] - odd[:, half:])
    back = jnp.where(shift == 0, 0, LANE_TILE - shift)
    from_left = lanes < LANE_TILE - shift
    for part in (0, 1):
        if part == 0:
            terms = [p * q + r * s for p, q, r, s in zip(patch_re, resid_re, patch_im, resid_im)]
        else:
            terms = [p * q - r * s for p, q, r, s in zip(patch_re, resid_im, patch_im, resid_re)]
        left, right = (pltpu.roll(term, back, 1) for term in terms)
        grad_probe[part, :, :half] += jnp.where(from_left, left, right)
        grad_probe[part, :, half:] += jnp.where(from_left, right, left)
    for part in (0, 1):
        if part == 0:
            terms = [p * q + r * s for p, q, r, s in zip(probe_re, resid_re, probe_im, resid_im)]
        else:
            terms = [p * q - r * s for p, q, r, s in zip(probe_re, resid_im, probe_im, resid_re)]
        terms = [descent * term for term in terms]
        total[part, first, rows, :] += jnp.where(wrapped, 0.0, terms[0])
        total[part, first + 1, rows, :] += terms[1]
        total[part, third, rows, :] += jnp.where(wrapped, terms[0], 0.0)


def iteration_kernel(first, *refs):
    if first:
        place_ref, info_ref, own_hbm, below_hbm, probe_hbm = refs[:5]
        refs = refs[5:]
    else:
        place_ref, info_ref, step_ref, own_hbm, above_hbm, low_hbm, below_hbm, probe_hbm = refs[:8]
        sum_hbm, refs = refs[8], refs[9:]
    amp_hbm, table_hbm, own_out, low_out, grad_out = refs[:5]
    refs = refs[5:]
    if not first:
        probe_out, refs = refs[0], refs[1:]
    ext, total, probe_ref, grad_probe, amp_ref, table_ref, sems, in_sems, out_sems = refs
    rows = own_hbm.shape[1]
    columns = ext.shape[1]
    half = probe_ref.shape[1] // 2
    own, low = pl.ds(0, rows), pl.ds(rows, rows)
    mine = pl.ds(pl.multiple_of(info_ref[2] * half, half), half)
    others = pl.ds(pl.multiple_of((1 - info_ref[2]) * half, half), half)

    def strip_pairs(hbm, vmem, start, part):
        where = pl.ds(start, hbm.shape[1])
        return [
            (hbm.at[part, :, pl.ds(LANE_TILE * column, LANE_TILE)], vmem.at[part, column, where, :])
            for column in range(columns)
        ]

    pairs = [(probe_hbm, probe_ref)]
    if not first:
        pairs += [(sum_hbm.at[0], grad_probe.at[:, mine, :]), (sum_hbm.at[1], grad_probe.at[:, others, :])]
    early = len(pairs)
    strips = [(own_hbm, ext, 0), (below_hbm, ext, rows)]
    if not first:
        strips += [(above_hbm, total, 0), (low_hbm, total, rows)]
    for hbm, vmem, start in strips:
        pairs += strip_pairs(hbm, vmem, start, 0) + strip_pairs(hbm, vmem, start, 1)
    pairs += [(table_hbm, table_ref), (amp_hbm, amp_ref)]
    copies = [pltpu.make_async_copy(src, dst, in_sems.at[i]) for i, (src, dst) in enumerate(pairs)]
    for copy in copies:
        copy.start()
    if first:
        total[:, :, low, :] = jnp.zeros((2, columns, rows, LANE_TILE), jnp.float32)
    for copy in copies[:early]:
        copy.wait()
    if not first:
        probe_ref[...] = probe_ref[...] - step_ref[0] * grad_probe[...]
        probe_copy = pltpu.make_async_copy(probe_ref, probe_out, sems.at[2])
        probe_copy.start()
    power = probe_ref[0] * probe_ref[0] + probe_ref[1] * probe_ref[1]
    descent = -1.0 / (jnp.max(power) + 1e-06)
    grad_probe[...] = jnp.zeros_like(grad_probe)
    for copy in copies[early:]:
        copy.wait()
    if first:
        total[:, :, own, :] = ext[:, :, own, :]
    else:
        now = ext[:, :, own, :] + total[:, :, own, :]
        ext[:, :, own, :] = now
        total[:, :, own, :] = now
        ext[:, :, low, :] += total[:, :, low, :]
        total[:, :, low, :] = jnp.zeros((2, columns, rows, LANE_TILE), jnp.float32)

    count = info_ref[0]

    def slots(index, carry):
        steps = []
        for slot in (2 * index, 2 * index + 1):
            live = (slot < count).astype(jnp.float32)
            slot = jnp.minimum(slot, amp_ref.shape[0] - 1)
            steps.append(
                slot_steps(slot, live, descent, place_ref, amp_ref, probe_ref, table_ref, ext, total, grad_probe)
            )
        for unused in zip_longest(*steps):
            pass
        return carry

    lax.fori_loop(0, (count + 1) // 2, slots, 0)

    @pl.when(info_ref[1] == 0)
    def _():
        total[:, :, low, :] = jnp.zeros((2, columns, rows, LANE_TILE), jnp.float32)

    outs = [
        pltpu.make_async_copy(grad_probe.at[:, others, :], grad_out.at[0], sems.at[0]),
        pltpu.make_async_copy(grad_probe.at[:, mine, :], grad_out.at[1], sems.at[1]),
    ]
    pairs = []
    for strip_out, start in ((low_out, rows), (own_out, 0)):
        pairs += strip_pairs(strip_out, total, start, 0) + strip_pairs(strip_out, total, start, 1)
    outs += [pltpu.make_async_copy(src, dst, out_sems.at[i]) for i, (dst, src) in enumerate(pairs)]
    for copy in outs:
        copy.start()
    for copy in outs:
        copy.wait()
    if not first:
        probe_copy.wait()


def iteration(first, scalars, objects, probes, amplitudes, table):
    parts, rows, width = objects[0].shape
    smem = pl.BlockSpec(memory_space=pltpu.SMEM)
    anywhere = pl.BlockSpec(memory_space=pl.ANY)
    probe_shape = jax.ShapeDtypeStruct(probes[0].shape, jnp.float32)
    halves = jax.ShapeDtypeStruct((2, parts, probe_shape.shape[1] // 2, probe_shape.shape[2]), jnp.float32)
    arrays = (*objects, *probes, amplitudes, table)
    strip = jax.ShapeDtypeStruct((parts, rows, width), jnp.float32)
    out_shape = [strip, strip, halves] + ([] if first else [probe_shape])
    columns = width // LANE_TILE
    extended = (parts, columns, 2 * rows, LANE_TILE)
    return pl.pallas_call(
        partial(iteration_kernel, first),
        out_shape=out_shape,
        in_specs=[smem] * len(scalars) + [anywhere] * len(arrays),
        out_specs=[anywhere] * len(out_shape),
        scratch_shapes=[
            pltpu.VMEM(extended, jnp.float32),
            pltpu.VMEM(extended, jnp.float32),
            pltpu.VMEM(probe_shape.shape, jnp.float32),
            pltpu.VMEM(probe_shape.shape, jnp.float32),
            pltpu.VMEM(amplitudes.shape, amplitudes.dtype),
            pltpu.VMEM(table.shape, table.dtype),
            pltpu.SemaphoreType.DMA((3,)),
            pltpu.SemaphoreType.DMA((5 + 4 * parts * columns,)),
            pltpu.SemaphoreType.DMA((2 * parts * columns,)),
        ],
        compiler_params=pltpu.CompilerParams(vmem_limit_bytes=62 * 2**20),
        cost_estimate=pl.CostEstimate(flops=8_000_000_000, bytes_accessed=8_000_000, transcendentals=400_000),
        name="iteration",
    )(*scalars, *arrays)


def passed_along(value, axis, by):
    size = lax.axis_size(axis)
    pairs = [(i, i + by) for i in range(size) if 0 <= i + by < size]
    return lax.ppermute(value, axis, pairs)


def by_keepers(axis):
    size = lax.axis_size(axis)
    return size & (size - 1) == 0 and size >= 8


def keepers_of(axis):
    return [i for i in range(lax.axis_size(axis)) if i % 4 in (1, 2)]


def crossed(value, axis, bits):
    return lax.ppermute(value, axis, [(i, i ^ bits) for i in keepers_of(axis)])


def scattered(halves, axis):
    if not by_keepers(axis):
        return halves
    halves = halves + lax.ppermute(halves, axis, [(i ^ 1, i) for i in keepers_of(axis)])
    value = halves[1] + crossed(halves[0], axis, 4)
    bit = 8
    while bit < lax.axis_size(axis):
        value = value + crossed(value, axis, bit)
        bit *= 2
    return value


def gathered(value, axis):
    index = lax.axis_index(axis)
    if not by_keepers(axis):
        upper = (index & 4) != 0
        whole = jnp.where(upper, value, value[::-1])
        whole = lax.psum(whole, axis)
        return jnp.where(upper, whole[::-1], whole)
    value = value + crossed(value, axis, 3)
    halves = jnp.stack([value, crossed(value, axis, 4)])
    arrived = lax.ppermute(halves, axis, [(i, i ^ 1) for i in keepers_of(axis)])
    keeps = ((index & 1) != 0) != ((index & 2) != 0)
    return jnp.where(keeps, halves, arrived)


def on_device(object_field, probe, amplitudes, offsets, counts):
    strip_rows = object_field.shape[1]
    side = probe.shape[1]
    strip_count = lax.axis_size("pos")
    device_index = lax.axis_index("pos")
    table, sort = constants(side)
    table = jnp.asarray(table)
    below = passed_along(object_field, "pos", -1)
    own_count = lax.dynamic_index_in_dim(counts, device_index, keepdims=False)
    not_last = (device_index + 1 < strip_count).astype(jnp.int32)
    upper = (device_index & 4) != 0
    info = jnp.stack([own_count, not_last, upper.astype(jnp.int32)])
    step = (8.0 / jnp.sum(counts).astype(jnp.float32))[None]
    place = jnp.stack([offsets[:, 0] - device_index * strip_rows, offsets[:, 1]], axis=1)
    amps = sorted_amplitudes(amplitudes, sort)
    own, low, grad = iteration(True, (place, info), (object_field, below), (probe,), amps, table)
    above = passed_along(low, "pos", 1)
    below = passed_along(own, "pos", -1)
    part = scattered(grad, "pos")
    part, above, below = lax.optimization_barrier((part, above, below))
    probe_sum = gathered(part, "pos")
    own, low, grad, probe_now = iteration(
        False, (place, info, step), (own, above, low, below), (probe, probe_sum), amps, table
    )
    above = passed_along(low, "pos", 1)
    part = scattered(grad, "pos")
    part, above = lax.optimization_barrier((part, above))
    mine, other = gathered(part, "pos")
    probe_sum = jnp.concatenate([jnp.where(upper, other, mine), jnp.where(upper, mine, other)], axis=1)
    return (own + above, probe_now - step * probe_sum)


def solution(mesh):
    in_specs = (
        P("groups", "pos", None),
        P("groups", None, None),
        P(("groups", "pos"), None, None),
        P(("groups", "pos"), None),
        P("groups"),
    )
    out_specs = (P("groups", "pos", None), P("groups", None, None))
    return jax.shard_map(
        on_device, mesh=mesh, in_specs=in_specs, out_specs=out_specs, check_vma=False
    )
```

```python
from functools import partial
from itertools import zip_longest
import math

import jax
import jax.numpy as jnp
import numpy as np
from jax import lax
from jax.experimental import pallas as pl
from jax.experimental.pallas import tpu as pltpu
from jax.sharding import PartitionSpec as P

LANE_TILE = 128
PIECES = 3


def split_bf16(array):
    high = array.astype(jnp.bfloat16)
    low = (array - high.astype(np.float32)).astype(jnp.bfloat16)
    return high, low


def constants(side):
    half = side // 2
    index = np.arange(half)
    parts = []
    for odd in (0, 1):
        angle = 2.0 * np.pi / side * (index[:, None] * (2 * index[None, :] + odd) % side)
        cosine, sine = np.cos(angle), np.sin(angle)
        matrix = (np.block([[cosine, -sine], [sine, cosine]]) / math.sqrt(side)).astype(np.float32)
        parts.append(split_bf16(matrix))
    tables = [[part, part.T] for pair in parts for part in pair]
    order = np.concatenate([np.arange(0, side, 2), np.arange(1, side, 2)])
    sort = np.zeros((side, side), np.float32)
    sort[order, np.arange(side)] = 1.0
    return np.stack([m for pair in tables for m in pair]), sort.astype(jnp.bfloat16)


def permute_kernel(amp_ref, sort_ref, sort_t_ref, out_ref):
    def one(slot, carry):
        rows = jnp.dot(sort_t_ref[...], amp_ref[slot], preferred_element_type=jnp.float32)
        both = jnp.dot(rows.astype(jnp.bfloat16), sort_ref[...], preferred_element_type=jnp.float32)
        out_ref[slot] = both.astype(jnp.bfloat16)
        return carry

    lax.fori_loop(0, amp_ref.shape[0], one, 0)


def sorted_amplitudes(amplitudes, sort):
    return pl.pallas_call(
        permute_kernel,
        out_shape=jax.ShapeDtypeStruct(amplitudes.shape, amplitudes.dtype),
        compiler_params=pltpu.CompilerParams(vmem_limit_bytes=63 * 2**20),
        cost_estimate=pl.CostEstimate(flops=400_000_000, bytes_accessed=1_600_000, transcendentals=0),
        name="sort_amplitudes",
    )(amplitudes, jnp.asarray(sort), jnp.asarray(sort.T))


def hi_lo(value):
    high = value.astype(jnp.bfloat16)
    return high, (value - high.astype(jnp.float32)).astype(jnp.bfloat16)


def matrix(table_ref, odd, turned, axis):
    high, low = table_ref[4 * odd + turned], table_ref[4 * odd + 2 + turned]
    return jnp.concatenate([high, high, low], axis=axis)


def times_right(value, table_ref, odd, turned):
    high, low = hi_lo(value)
    stacked = jnp.concatenate([high, low, high], axis=1)
    return jnp.dot(stacked, matrix(table_ref, odd, turned, 0), preferred_element_type=jnp.float32)


def times_left(table_ref, odd, turned, value):
    high, low = hi_lo(value)
    stacked = jnp.concatenate([high, low, high], axis=0)
    return jnp.dot(matrix(table_ref, odd, turned, 1), stacked, preferred_element_type=jnp.float32)


def lane_rotated(left, right, shift, wrapped):
    left, right = pltpu.roll(left, shift, 1), pltpu.roll(right, shift, 1)
    return jnp.where(wrapped, right, left), jnp.where(wrapped, left, right)


def slot_steps(slot, live, descent, place_ref, amp_ref, probe_ref, table_ref, ext, total, grad_probe):
    side = probe_ref.shape[1]
    half = side // 2
    row, col = place_ref[slot, 0], place_ref[slot, 1]
    rows = pl.ds(row, side)
    first = col // LANE_TILE
    shift = col - first * LANE_TILE
    third = jnp.minimum(first + 2, ext.shape[0] - 1)
    lanes = lax.broadcasted_iota(jnp.int32, (side, LANE_TILE), 1)
    wrapped = lanes < shift

    def patch(part):
        return jnp.where(wrapped, ext[third, part, rows, :], ext[first, part, rows, :]), ext[first + 1, part, rows, :]

    def probe(part):
        return lane_rotated(probe_ref[part, :, :half], probe_ref[part, :, half:], shift, wrapped)

    patch_re, patch_im = patch(0), patch(1)
    probe_re, probe_im = probe(0), probe(1)
    exit_re = [p * q - r * s for p, q, r, s in zip(probe_re, patch_re, probe_im, patch_im)]
    exit_im = [p * q + r * s for p, q, r, s in zip(probe_re, patch_im, probe_im, patch_re)]
    even = jnp.concatenate([exit_re[0] + exit_re[1], exit_im[0] + exit_im[1]], axis=1)
    odd = jnp.concatenate([exit_re[0] - exit_re[1], exit_im[0] - exit_im[1]], axis=1)
    even = times_right(even, table_ref, 0, 0)
    odd = times_right(odd, table_ref, 1, 0)
    yield
    wave_re = jnp.concatenate([even[:, :half], odd[:, :half]], axis=1)
    wave_im = jnp.concatenate([even[:, half:], odd[:, half:]], axis=1)
    even = jnp.concatenate([wave_re[:half] + wave_re[half:], wave_im[:half] + wave_im[half:]], axis=0)
    odd = jnp.concatenate([wave_re[:half] - wave_re[half:], wave_im[:half] - wave_im[half:]], axis=0)
    even = times_left(table_ref, 0, 1, even)
    odd = times_left(table_ref, 1, 1, odd)
    yield

    def kept(spec, rows):
        spec_re, spec_im = spec[:half], spec[half:]
        amplitude = amp_ref[slot, rows, :].astype(jnp.float32)
        keeping = live - live * amplitude * lax.rsqrt(spec_re * spec_re + spec_im * spec_im + 1.0)
        return jnp.concatenate([spec_re * keeping, spec_im * keeping], axis=0)

    even = times_left(table_ref, 0, 0, kept(even, slice(0, half)))
    odd = times_left(table_ref, 1, 0, kept(odd, slice(half, side)))
    wave_re = jnp.concatenate([even[:half] + odd[:half], even[:half] - odd[:half]], axis=0)
    wave_im = jnp.concatenate([even[half:] + odd[half:], even[half:] - odd[half:]], axis=0)
    yield
    even = times_right(jnp.concatenate([wave_re[:, :half], wave_im[:, :half]], axis=1), table_ref, 0, 1)
    odd = times_right(jnp.concatenate([wave_re[:, half:], wave_im[:, half:]], axis=1), table_ref, 1, 1)
    yield
    resid_re = (even[:, :half] + odd[:, :half], even[:, :half] - odd[:, :half])
    resid_im = (even[:, half:] + odd[:, half:], even[:, half:] - odd[:, half:])
    back = jnp.where(shift == 0, 0, LANE_TILE - shift)
    from_left = lanes < LANE_TILE - shift
    for part in (0, 1):
        if part == 0:
            terms = [p * q + r * s for p, q, r, s in zip(patch_re, resid_re, patch_im, resid_im)]
        else:
            terms = [p * q - r * s for p, q, r, s in zip(patch_re, resid_im, patch_im, resid_re)]
        left, right = (pltpu.roll(term, back, 1) for term in terms)
        grad_probe[part, :, :half] += jnp.where(from_left, left, right)
        grad_probe[part, :, half:] += jnp.where(from_left, right, left)
    for part in (0, 1):
        if part == 0:
            terms = [p * q + r * s for p, q, r, s in zip(probe_re, resid_re, probe_im, resid_im)]
        else:
            terms = [p * q - r * s for p, q, r, s in zip(probe_re, resid_im, probe_im, resid_re)]
        terms = [descent * term for term in terms]
        total[first, part, rows, :] += jnp.where(wrapped, 0.0, terms[0])
        total[first + 1, part, rows, :] += terms[1]
        total[third, part, rows, :] += jnp.where(wrapped, terms[0], 0.0)


def iteration_kernel(first, pieces, *refs):
    if first:
        place_ref, info_ref, own_hbm, below_hbm, probe_hbm = refs[:5]
        refs = refs[5:]
    else:
        place_ref, info_ref, step_ref = refs[:3]
        strips_hbm, probe_hbm, sum_hbms, refs = refs[3:7], refs[7], refs[8:10], refs[10:]
    amp_hbm, table_hbm, keep_out, send_out = refs[:4]
    low_outs, refs = refs[4 : 4 + pieces], refs[4 + pieces :]
    own_out, refs = refs[0], refs[1:]
    if not first:
        probe_out, refs = refs[0], refs[1:]
    ext, total, probe_ref, grad_probe, amp_ref, table_ref, sems, in_sems, out_sems = refs
    columns = ext.shape[0]
    rows = ext.shape[2] // 2
    half = probe_ref.shape[1] // 2
    own, low = pl.ds(0, rows), pl.ds(rows, rows)
    mine = pl.ds(pl.multiple_of(info_ref[2] * half, half), half)
    others = pl.ds(pl.multiple_of((1 - info_ref[2]) * half, half), half)

    def by_column(hbm, vmem, where):
        return [
            (hbm.at[part, :, pl.ds(LANE_TILE * column, LANE_TILE)], vmem.at[column, part, where, :])
            for part in (0, 1)
            for column in range(columns)
        ]

    def by_piece(hbms, vmem, where):
        size = columns // len(hbms)
        return [(hbm, vmem.at[pl.ds(size * piece, size), :, where, :]) for piece, hbm in enumerate(hbms)]

    pairs = [(probe_hbm, probe_ref)]
    if not first:
        pairs += [(sum_hbms[0], grad_probe.at[:, mine, :]), (sum_hbms[1], grad_probe.at[:, others, :])]
    early = len(pairs)
    if first:
        pairs += by_column(own_hbm, ext, own) + by_column(below_hbm, ext, low)
    else:
        for hbm, vmem, where in zip(strips_hbm, (ext, total, total, ext), (own, own, low, low)):
            pairs += by_piece([hbm], vmem, where)
    pairs += [(table_hbm, table_ref), (amp_hbm, amp_ref)]
    copies = [pltpu.make_async_copy(src, dst, in_sems.at[i]) for i, (src, dst) in enumerate(pairs)]
    for copy in copies:
        copy.start()
    if first:
        total[:, :, low, :] = jnp.zeros((columns, 2, rows, LANE_TILE), jnp.float32)
    for copy in copies[:early]:
        copy.wait()
    if not first:
        probe_ref[...] = probe_ref[...] - step_ref[0] * grad_probe[...]
        probe_copy = pltpu.make_async_copy(probe_ref, probe_out, sems.at[2])
        probe_copy.start()
    power = probe_ref[0] * probe_ref[0] + probe_ref[1] * probe_ref[1]
    descent = -1.0 / (jnp.max(power) + 1e-06)
    grad_probe[...] = jnp.zeros_like(grad_probe)
    for copy in copies[early:]:
        copy.wait()
    if first:
        total[:, :, own, :] = ext[:, :, own, :]
    else:
        now = ext[:, :, own, :] + total[:, :, own, :]
        ext[:, :, own, :] = now
        total[:, :, own, :] = now
        ext[:, :, low, :] += total[:, :, low, :]
        total[:, :, low, :] = jnp.zeros((columns, 2, rows, LANE_TILE), jnp.float32)

    count = info_ref[0]

    def slots(index, carry):
        steps = []
        for slot in (2 * index, 2 * index + 1):
            live = (slot < count).astype(jnp.float32)
            slot = jnp.minimum(slot, amp_ref.shape[0] - 1)
            steps.append(
                slot_steps(slot, live, descent, place_ref, amp_ref, probe_ref, table_ref, ext, total, grad_probe)
            )
        for unused in zip_longest(*steps):
            pass
        return carry

    lax.fori_loop(0, (count + 1) // 2, slots, 0)

    @pl.when(info_ref[1] == 0)
    def _():
        total[:, :, low, :] = jnp.zeros((columns, 2, rows, LANE_TILE), jnp.float32)

    outs = [
        pltpu.make_async_copy(grad_probe.at[:, others, :], send_out, sems.at[0]),
        pltpu.make_async_copy(grad_probe.at[:, mine, :], keep_out, sems.at[1]),
    ]
    pairs = by_piece(low_outs, total, low)
    pairs += by_piece([own_out], total, own) if first else by_column(own_out, total, own)
    outs += [pltpu.make_async_copy(src, dst, out_sems.at[i]) for i, (dst, src) in enumerate(pairs)]
    for copy in outs:
        copy.start()
    for copy in outs:
        copy.wait()
    if not first:
        probe_copy.wait()


def iteration(first, scalars, strips, probes, amplitudes, table, shape):
    parts, rows, width = shape
    columns = width // LANE_TILE
    pieces = 1 if first or columns % PIECES else PIECES
    smem = pl.BlockSpec(memory_space=pltpu.SMEM)
    anywhere = pl.BlockSpec(memory_space=pl.ANY)
    probe_shape = jax.ShapeDtypeStruct(probes[0].shape, jnp.float32)
    half_shape = jax.ShapeDtypeStruct((parts, probe_shape.shape[1] // 2, probe_shape.shape[2]), jnp.float32)
    strip = jax.ShapeDtypeStruct((columns, parts, rows, LANE_TILE), jnp.float32)
    piece = jax.ShapeDtypeStruct((columns // pieces, *strip.shape[1:]), jnp.float32)
    arrays = (*strips, *probes, amplitudes, table)
    out_shape = [half_shape, half_shape] + [piece] * pieces
    out_shape += [strip] if first else [jax.ShapeDtypeStruct(shape, jnp.float32), probe_shape]
    extended = (columns, parts, 2 * rows, LANE_TILE)
    outs = pl.pallas_call(
        partial(iteration_kernel, first, pieces),
        out_shape=out_shape,
        in_specs=[smem] * len(scalars) + [anywhere] * len(arrays),
        out_specs=[anywhere] * len(out_shape),
        scratch_shapes=[
            pltpu.VMEM(extended, jnp.float32),
            pltpu.VMEM(extended, jnp.float32),
            pltpu.VMEM(probe_shape.shape, jnp.float32),
            pltpu.VMEM(probe_shape.shape, jnp.float32),
            pltpu.VMEM(amplitudes.shape, amplitudes.dtype),
            pltpu.VMEM(table.shape, table.dtype),
            pltpu.SemaphoreType.DMA((3,)),
            pltpu.SemaphoreType.DMA((5 + 2 * parts * columns,)),
            pltpu.SemaphoreType.DMA((parts * columns + pieces,)),
        ],
        compiler_params=pltpu.CompilerParams(vmem_limit_bytes=62 * 2**20),
        cost_estimate=pl.CostEstimate(flops=8_000_000_000, bytes_accessed=8_000_000, transcendentals=400_000),
        name="iteration",
    )(*scalars, *arrays)
    return outs[:2], outs[2 : 2 + pieces], outs[2 + pieces :]


def passed_along(value, axis, by):
    size = lax.axis_size(axis)
    pairs = [(i, i + by) for i in range(size) if 0 <= i + by < size]
    return lax.ppermute(value, axis, pairs)


def swapped(value, axis, bit):
    size = lax.axis_size(axis)
    return lax.ppermute(value, axis, [(i, i ^ bit) for i in range(size)])


def upper_of(axis, bit):
    return (lax.axis_index(axis) & bit) != 0


def bits_of(axis):
    size = lax.axis_size(axis)
    if size & (size - 1) or size < 8:
        return []
    bits = [1 << k for k in range(size.bit_length() - 1)]
    return [bits[0], *bits[2:], bits[1]]


def joined(mine, other, upper):
    return jnp.concatenate([jnp.where(upper, other, mine), jnp.where(upper, mine, other)], axis=1)


def summed_beside(keep, send, axis, pieces, late):
    bits = bits_of(axis)
    pieces = [[list(arrays), by] for arrays, by in pieces]
    upper = upper_of(axis, 1)

    def moving(piece):
        return [passed_along(array, axis, by) for array, by in zip(*piece)]

    if not bits:
        value = lax.psum(joined(keep, send, upper), axis)
        half = value.shape[1] // 2
        first, second = value[:, :half], value[:, half:]
        return jnp.where(upper, second, first), jnp.where(upper, first, second), [moving(piece) for piece in pieces]
    moved = [moving(piece) for piece in pieces[:1]]
    arrived = -late

    def behind(value):
        if len(moved) < len(pieces):
            value, pieces[len(moved)][0] = lax.optimization_barrier((value, pieces[len(moved)][0]))
            moved.append(moving(pieces[len(moved)]))
        return value

    def ahead(value):
        nonlocal arrived
        if 0 <= arrived < len(moved):
            value, moved[arrived] = lax.optimization_barrier((value, moved[arrived]))
        arrived += 1
        return value

    value = keep + swapped(send, axis, bits[0])
    inner = upper_of(axis, bits[1])
    half = value.shape[1] // 2
    first, second = value[:, :half], value[:, half:]
    value = jnp.where(inner, second, first) + swapped(jnp.where(inner, first, second), axis, bits[1])
    for bit in bits[2:]:
        value = behind(value)
        value = ahead(value + swapped(value, axis, bit))
    value = ahead(joined(value, swapped(value, axis, bits[1]), inner))
    return value, swapped(value, axis, bits[0]), moved


def on_device(object_field, probe, amplitudes, offsets, counts):
    strip_rows = object_field.shape[1]
    side = probe.shape[1]
    strip_count = lax.axis_size("pos")
    device_index = lax.axis_index("pos")
    table, sort = constants(side)
    table = jnp.asarray(table)
    below = passed_along(object_field, "pos", -1)
    own_count = lax.dynamic_index_in_dim(counts, device_index, keepdims=False)
    not_last = (device_index + 1 < strip_count).astype(jnp.int32)
    info = jnp.stack([own_count, not_last, device_index % 2])
    step = (8.0 / jnp.sum(counts).astype(jnp.float32))[None]
    place = jnp.stack([offsets[:, 0] - device_index * strip_rows, offsets[:, 1]], axis=1)
    amps = sorted_amplitudes(amplitudes, sort)
    shape = object_field.shape
    (keep, send), (low,), (own,) = iteration(True, (place, info), (object_field, below), (probe,), amps, table, shape)
    mine, other, [(above, below)] = summed_beside(keep, send, "pos", [((low, own), (1, -1))], 1)
    strips = (own, above, low, below)
    (keep, send), lows, (own, probe_now) = iteration(
        False, (place, info, step), strips, (probe, mine, other), amps, table, shape
    )
    mine, other, moved = summed_beside(keep, send, "pos", [((low,), (1,)) for low in lows], 0)
    above = [above[column] for (above,) in moved for column in range(above.shape[0])]
    probe_sum = joined(mine, other, upper_of("pos", 1))
    return (own + jnp.concatenate(above, axis=2), probe_now - step * probe_sum)


def solution(mesh):
    in_specs = (
        P("groups", "pos", None),
        P("groups", None, None),
        P(("groups", "pos"), None, None),
        P(("groups", "pos"), None),
        P("groups"),
    )
    out_specs = (P("groups", "pos", None), P("groups", None, None))
    return jax.shard_map(
        on_device, mesh=mesh, in_specs=in_specs, out_specs=out_specs, check_vma=False
    )
```

```python
from functools import partial
from itertools import zip_longest
import math

import jax
import jax.numpy as jnp
import numpy as np
from jax import lax
from jax.experimental import pallas as pl
from jax.experimental.pallas import tpu as pltpu
from jax.sharding import PartitionSpec as P

LANE_TILE = 128
PIECES = 3
TOGETHER = 3


def split_bf16(array):
    high = array.astype(jnp.bfloat16)
    low = (array - high.astype(np.float32)).astype(jnp.bfloat16)
    return high, low


def constants(side):
    half = side // 2
    index = np.arange(half)
    parts = []
    for odd in (0, 1):
        angle = 2.0 * np.pi / side * (index[:, None] * (2 * index[None, :] + odd) % side)
        cosine, sine = np.cos(angle), np.sin(angle)
        matrix = (np.block([[cosine, -sine], [sine, cosine]]) / math.sqrt(side)).astype(np.float32)
        parts.append(split_bf16(matrix))
    tables = [[part, part.T] for pair in parts for part in pair]
    order = np.concatenate([np.arange(0, side, 2), np.arange(1, side, 2)])
    sort = np.zeros((side, side), np.float32)
    sort[order, np.arange(side)] = 1.0
    return np.stack([m for pair in tables for m in pair]), sort.astype(jnp.bfloat16)


def permute_kernel(amp_ref, sort_ref, sort_t_ref, out_ref):
    def one(slot, carry):
        rows = jnp.dot(sort_t_ref[...], amp_ref[slot], preferred_element_type=jnp.float32)
        both = jnp.dot(rows.astype(jnp.bfloat16), sort_ref[...], preferred_element_type=jnp.float32)
        out_ref[slot] = both.astype(jnp.bfloat16)
        return carry

    lax.fori_loop(0, amp_ref.shape[0], one, 0)


def sorted_amplitudes(amplitudes, sort):
    return pl.pallas_call(
        permute_kernel,
        out_shape=jax.ShapeDtypeStruct(amplitudes.shape, amplitudes.dtype),
        compiler_params=pltpu.CompilerParams(vmem_limit_bytes=63 * 2**20),
        cost_estimate=pl.CostEstimate(flops=400_000_000, bytes_accessed=1_600_000, transcendentals=0),
        name="sort_amplitudes",
    )(amplitudes, jnp.asarray(sort), jnp.asarray(sort.T))


def hi_lo(value):
    high = value.astype(jnp.bfloat16)
    return high, (value - high.astype(jnp.float32)).astype(jnp.bfloat16)


def matrix(table_ref, odd, turned, axis):
    high, low = table_ref[4 * odd + turned], table_ref[4 * odd + 2 + turned]
    return jnp.concatenate([high, high, low], axis=axis)


def times_right(value, table_ref, odd, turned):
    high, low = hi_lo(value)
    stacked = jnp.concatenate([high, low, high], axis=1)
    return jnp.dot(stacked, matrix(table_ref, odd, turned, 0), preferred_element_type=jnp.float32)


def times_left(table_ref, odd, turned, value):
    high, low = hi_lo(value)
    stacked = jnp.concatenate([high, low, high], axis=0)
    return jnp.dot(matrix(table_ref, odd, turned, 1), stacked, preferred_element_type=jnp.float32)


def lane_rotated(left, right, shift, wrapped):
    left, right = pltpu.roll(left, shift, 1), pltpu.roll(right, shift, 1)
    return jnp.where(wrapped, right, left), jnp.where(wrapped, left, right)


def slot_steps(slot, live, descent, place_ref, amp_ref, probe_ref, table_ref, ext, total, grad_probe):
    side = probe_ref.shape[1]
    half = side // 2
    row, col = place_ref[slot, 0], place_ref[slot, 1]
    rows = pl.ds(row, side)
    first = col // LANE_TILE
    shift = col - first * LANE_TILE
    third = jnp.minimum(first + 2, ext.shape[0] - 1)
    lanes = lax.broadcasted_iota(jnp.int32, (side, LANE_TILE), 1)
    wrapped = lanes < shift

    def patch(part):
        return jnp.where(wrapped, ext[third, part, rows, :], ext[first, part, rows, :]), ext[first + 1, part, rows, :]

    def probe(part):
        return lane_rotated(probe_ref[part, :, :half], probe_ref[part, :, half:], shift, wrapped)

    patch_re, patch_im = patch(0), patch(1)
    probe_re, probe_im = probe(0), probe(1)
    exit_re = [p * q - r * s for p, q, r, s in zip(probe_re, patch_re, probe_im, patch_im)]
    exit_im = [p * q + r * s for p, q, r, s in zip(probe_re, patch_im, probe_im, patch_re)]
    even = jnp.concatenate([exit_re[0] + exit_re[1], exit_im[0] + exit_im[1]], axis=1)
    odd = jnp.concatenate([exit_re[0] - exit_re[1], exit_im[0] - exit_im[1]], axis=1)
    even = times_right(even, table_ref, 0, 0)
    odd = times_right(odd, table_ref, 1, 0)
    yield
    wave_re = jnp.concatenate([even[:, :half], odd[:, :half]], axis=1)
    wave_im = jnp.concatenate([even[:, half:], odd[:, half:]], axis=1)
    even = jnp.concatenate([wave_re[:half] + wave_re[half:], wave_im[:half] + wave_im[half:]], axis=0)
    odd = jnp.concatenate([wave_re[:half] - wave_re[half:], wave_im[:half] - wave_im[half:]], axis=0)
    even = times_left(table_ref, 0, 1, even)
    odd = times_left(table_ref, 1, 1, odd)
    yield

    def kept(spec, rows):
        spec_re, spec_im = spec[:half], spec[half:]
        amplitude = amp_ref[slot, rows, :].astype(jnp.float32)
        keeping = live - live * amplitude * lax.rsqrt(spec_re * spec_re + spec_im * spec_im + 1.0)
        return jnp.concatenate([spec_re * keeping, spec_im * keeping], axis=0)

    even = times_left(table_ref, 0, 0, kept(even, slice(0, half)))
    odd = times_left(table_ref, 1, 0, kept(odd, slice(half, side)))
    wave_re = jnp.concatenate([even[:half] + odd[:half], even[:half] - odd[:half]], axis=0)
    wave_im = jnp.concatenate([even[half:] + odd[half:], even[half:] - odd[half:]], axis=0)
    yield
    even = times_right(jnp.concatenate([wave_re[:, :half], wave_im[:, :half]], axis=1), table_ref, 0, 1)
    odd = times_right(jnp.concatenate([wave_re[:, half:], wave_im[:, half:]], axis=1), table_ref, 1, 1)
    yield
    resid_re = (even[:, :half] + odd[:, :half], even[:, :half] - odd[:, :half])
    resid_im = (even[:, half:] + odd[:, half:], even[:, half:] - odd[:, half:])
    back = jnp.where(shift == 0, 0, LANE_TILE - shift)
    from_left = lanes < LANE_TILE - shift
    for part in (0, 1):
        if part == 0:
            terms = [p * q + r * s for p, q, r, s in zip(patch_re, resid_re, patch_im, resid_im)]
        else:
            terms = [p * q - r * s for p, q, r, s in zip(patch_re, resid_im, patch_im, resid_re)]
        left, right = (pltpu.roll(term, back, 1) for term in terms)
        grad_probe[part, :, :half] += jnp.where(from_left, left, right)
        grad_probe[part, :, half:] += jnp.where(from_left, right, left)
    for part in (0, 1):
        if part == 0:
            terms = [p * q + r * s for p, q, r, s in zip(probe_re, resid_re, probe_im, resid_im)]
        else:
            terms = [p * q - r * s for p, q, r, s in zip(probe_re, resid_im, probe_im, resid_re)]
        terms = [descent * term for term in terms]
        total[first, part, rows, :] += jnp.where(wrapped, 0.0, terms[0])
        total[first + 1, part, rows, :] += terms[1]
        total[third, part, rows, :] += jnp.where(wrapped, terms[0], 0.0)


def iteration_kernel(first, pieces, *refs):
    if first:
        place_ref, info_ref, own_hbm, below_hbm, probe_hbm = refs[:5]
        refs = refs[5:]
    else:
        place_ref, info_ref, step_ref, own_hbm, below_hbm, probe_hbm = refs[:6]
        sum_hbms, refs = refs[6:8], refs[8:]
    amp_hbm, table_hbm, keep_out, send_out = refs[:4]
    low_outs, refs = refs[4 : 4 + pieces], refs[4 + pieces :]
    own_out, refs = refs[0], refs[1:]
    if not first:
        probe_out, refs = refs[0], refs[1:]
    ext, total, probe_ref, grad_probe, amp_ref, table_ref, sems, in_sems, out_sems = refs
    columns = ext.shape[0]
    rows = ext.shape[2] // 2
    half = probe_ref.shape[1] // 2
    own, low = pl.ds(0, rows), pl.ds(rows, rows)
    mine = pl.ds(pl.multiple_of(info_ref[2] * half, half), half)
    others = pl.ds(pl.multiple_of((1 - info_ref[2]) * half, half), half)

    def by_column(hbm, vmem, where):
        return [
            (hbm.at[part, :, pl.ds(LANE_TILE * column, LANE_TILE)], vmem.at[column, part, where, :])
            for part in (0, 1)
            for column in range(columns)
        ]

    def by_piece(hbms, vmem, where):
        size = columns // len(hbms)
        return [(hbm, vmem.at[pl.ds(size * piece, size), :, where, :]) for piece, hbm in enumerate(hbms)]

    pairs = [(probe_hbm, probe_ref)]
    if not first:
        pairs += [(sum_hbms[0], grad_probe.at[:, mine, :]), (sum_hbms[1], grad_probe.at[:, others, :])]
    early = len(pairs)
    if first:
        pairs += by_column(own_hbm, ext, own) + by_column(below_hbm, ext, low)
    else:
        pairs += by_piece([own_hbm], ext, own) + by_piece([below_hbm], ext, low)
    pairs += [(table_hbm, table_ref), (amp_hbm, amp_ref)]
    copies = [pltpu.make_async_copy(src, dst, in_sems.at[i]) for i, (src, dst) in enumerate(pairs)]
    for copy in copies:
        copy.start()
    total[:, :, low, :] = jnp.zeros((columns, 2, rows, LANE_TILE), jnp.float32)
    for copy in copies[:early]:
        copy.wait()
    if not first:
        probe_ref[...] = probe_ref[...] - step_ref[0] * grad_probe[...]
        probe_copy = pltpu.make_async_copy(probe_ref, probe_out, sems.at[2])
        probe_copy.start()
    power = probe_ref[0] * probe_ref[0] + probe_ref[1] * probe_ref[1]
    descent = -1.0 / (jnp.max(power) + 1e-06)
    grad_probe[...] = jnp.zeros_like(grad_probe)
    for copy in copies[early:]:
        copy.wait()
    total[:, :, own, :] = ext[:, :, own, :]

    count = info_ref[0]

    def slots(index, carry):
        steps = []
        for slot in (TOGETHER * index + k for k in range(TOGETHER)):
            live = (slot < count).astype(jnp.float32)
            slot = jnp.minimum(slot, amp_ref.shape[0] - 1)
            steps.append(
                slot_steps(slot, live, descent, place_ref, amp_ref, probe_ref, table_ref, ext, total, grad_probe)
            )
        for unused in zip_longest(*steps):
            pass
        return carry

    lax.fori_loop(0, (count + TOGETHER - 1) // TOGETHER, slots, 0)

    @pl.when(info_ref[1] == 0)
    def _():
        total[:, :, low, :] = jnp.zeros((columns, 2, rows, LANE_TILE), jnp.float32)

    outs = [
        pltpu.make_async_copy(grad_probe.at[:, others, :], send_out, sems.at[0]),
        pltpu.make_async_copy(grad_probe.at[:, mine, :], keep_out, sems.at[1]),
    ]
    pairs = by_piece(low_outs, total, low)
    pairs += by_piece([own_out], total, own) if first else by_column(own_out, total, own)
    outs += [pltpu.make_async_copy(src, dst, out_sems.at[i]) for i, (dst, src) in enumerate(pairs)]
    for copy in outs:
        copy.start()
    for copy in outs:
        copy.wait()
    if not first:
        probe_copy.wait()


def iteration(first, scalars, strips, probes, amplitudes, table, shape):
    parts, rows, width = shape
    columns = width // LANE_TILE
    pieces = 1 if first or columns % PIECES else PIECES
    smem = pl.BlockSpec(memory_space=pltpu.SMEM)
    anywhere = pl.BlockSpec(memory_space=pl.ANY)
    probe_shape = jax.ShapeDtypeStruct(probes[0].shape, jnp.float32)
    half_shape = jax.ShapeDtypeStruct((parts, probe_shape.shape[1] // 2, probe_shape.shape[2]), jnp.float32)
    strip = jax.ShapeDtypeStruct((columns, parts, rows, LANE_TILE), jnp.float32)
    piece = jax.ShapeDtypeStruct((columns // pieces, *strip.shape[1:]), jnp.float32)
    arrays = (*strips, *probes, amplitudes, table)
    out_shape = [half_shape, half_shape] + [piece] * pieces
    out_shape += [strip] if first else [jax.ShapeDtypeStruct(shape, jnp.float32), probe_shape]
    extended = (columns, parts, 2 * rows, LANE_TILE)
    outs = pl.pallas_call(
        partial(iteration_kernel, first, pieces),
        out_shape=out_shape,
        in_specs=[smem] * len(scalars) + [anywhere] * len(arrays),
        out_specs=[anywhere] * len(out_shape),
        scratch_shapes=[
            pltpu.VMEM(extended, jnp.float32),
            pltpu.VMEM(extended, jnp.float32),
            pltpu.VMEM(probe_shape.shape, jnp.float32),
            pltpu.VMEM(probe_shape.shape, jnp.float32),
            pltpu.VMEM(amplitudes.shape, amplitudes.dtype),
            pltpu.VMEM(table.shape, table.dtype),
            pltpu.SemaphoreType.DMA((3,)),
            pltpu.SemaphoreType.DMA((5 + 2 * parts * columns,)),
            pltpu.SemaphoreType.DMA((parts * columns + pieces,)),
        ],
        compiler_params=pltpu.CompilerParams(vmem_limit_bytes=62 * 2**20),
        cost_estimate=pl.CostEstimate(flops=8_000_000_000, bytes_accessed=8_000_000, transcendentals=400_000),
        name="iteration",
    )(*scalars, *arrays)
    return outs[:2], outs[2 : 2 + pieces], outs[2 + pieces :]


def passed_along(value, axis, by):
    size = lax.axis_size(axis)
    pairs = [(i, i + by) for i in range(size) if 0 <= i + by < size]
    return lax.ppermute(value, axis, pairs)


def swapped(value, axis, bit):
    size = lax.axis_size(axis)
    return lax.ppermute(value, axis, [(i, i ^ bit) for i in range(size)])


def upper_of(axis, bit):
    return (lax.axis_index(axis) & bit) != 0


def bits_of(axis):
    size = lax.axis_size(axis)
    if size & (size - 1) or size < 8:
        return []
    bits = [1 << k for k in range(size.bit_length() - 1)]
    return [bits[0], *bits[2:], bits[1]]


def joined(mine, other, upper):
    return jnp.concatenate([jnp.where(upper, other, mine), jnp.where(upper, mine, other)], axis=1)


def summed_beside(keep, send, axis, pieces, late, used=None):
    bits = bits_of(axis)
    pieces = [[list(arrays), by] for arrays, by in pieces]
    upper = upper_of(axis, 1)

    def moving(piece):
        return [passed_along(array, axis, by) for array, by in zip(*piece)]

    if not bits:
        value = lax.psum(joined(keep, send, upper), axis)
        half = value.shape[1] // 2
        first, second = value[:, :half], value[:, half:]
        return jnp.where(upper, second, first), jnp.where(upper, first, second), [
            used(*moving(piece)) if used else moving(piece) for piece in pieces
        ]
    moved = [moving(piece) for piece in pieces[:1]]
    arrived = -late

    def behind(value):
        if len(moved) < len(pieces):
            value, pieces[len(moved)][0] = lax.optimization_barrier((value, pieces[len(moved)][0]))
            moved.append(moving(pieces[len(moved)]))
        return value

    def ahead(value):
        nonlocal arrived
        if 0 <= arrived < len(moved):
            value, moved[arrived] = lax.optimization_barrier((value, moved[arrived]))
        arrived += 1
        return value

    value = keep + swapped(send, axis, bits[0])
    inner = upper_of(axis, bits[1])
    half = value.shape[1] // 2
    first, second = value[:, :half], value[:, half:]
    value = jnp.where(inner, second, first) + swapped(jnp.where(inner, first, second), axis, bits[1])
    for bit in bits[2:]:
        value = behind(value)
        value = ahead(value + swapped(value, axis, bit))
    if used:
        moved = [used(*moved[0])]
        arrived = 0
    value = ahead(joined(value, swapped(value, axis, bits[1]), inner))
    return value, swapped(value, axis, bits[0]), moved


def on_device(object_field, probe, amplitudes, offsets, counts):
    strip_rows = object_field.shape[1]
    side = probe.shape[1]
    strip_count = lax.axis_size("pos")
    device_index = lax.axis_index("pos")
    table, sort = constants(side)
    table = jnp.asarray(table)
    below = passed_along(object_field, "pos", -1)
    own_count = lax.dynamic_index_in_dim(counts, device_index, keepdims=False)
    not_last = (device_index + 1 < strip_count).astype(jnp.int32)
    info = jnp.stack([own_count, not_last, device_index % 2])
    step = (8.0 / jnp.sum(counts).astype(jnp.float32))[None]
    place = jnp.stack([offsets[:, 0] - device_index * strip_rows, offsets[:, 1]], axis=1)
    amps = sorted_amplitudes(amplitudes, sort)
    shape = object_field.shape
    (keep, send), (low,), (own,) = iteration(True, (place, info), (object_field, below), (probe,), amps, table, shape)
    mine, other, [strips] = summed_beside(
        keep, send, "pos", [((low, own), (1, -1))], 1, lambda above, below: (own + above, below + low)
    )
    (keep, send), lows, (own, probe_now) = iteration(
        False, (place, info, step), strips, (probe, mine, other), amps, table, shape
    )
    mine, other, moved = summed_beside(keep, send, "pos", [((low,), (1,)) for low in lows], 0)
    above = [above[column] for (above,) in moved for column in range(above.shape[0])]
    probe_sum = joined(mine, other, upper_of("pos", 1))
    return (own + jnp.concatenate(above, axis=2), probe_now - step * probe_sum)


def solution(mesh):
    in_specs = (
        P("groups", "pos", None),
        P("groups", None, None),
        P(("groups", "pos"), None, None),
        P(("groups", "pos"), None),
        P("groups"),
    )
    out_specs = (P("groups", "pos", None), P("groups", None, None))
    return jax.shard_map(
        on_device, mesh=mesh, in_specs=in_specs, out_specs=out_specs, check_vma=False
    )
```

```python
from functools import partial
from itertools import zip_longest
import math

import jax
import jax.numpy as jnp
import numpy as np
from jax import lax
from jax.experimental import pallas as pl
from jax.experimental.pallas import tpu as pltpu
from jax.sharding import PartitionSpec as P

LANE_TILE = 128
PIECES = 3
TOGETHER = 3


def split_bf16(array):
    high = array.astype(jnp.bfloat16)
    low = (array - high.astype(np.float32)).astype(jnp.bfloat16)
    return high, low


def constants(side):
    half = side // 2
    index = np.arange(half)
    parts = []
    for odd in (0, 1):
        angle = 2.0 * np.pi / side * (index[:, None] * (2 * index[None, :] + odd) % side)
        cosine, sine = np.cos(angle), np.sin(angle)
        matrix = (np.block([[cosine, -sine], [sine, cosine]]) / math.sqrt(side)).astype(np.float32)
        parts.append(split_bf16(matrix))
    tables = [[part, part.T] for pair in parts for part in pair]
    order = np.concatenate([np.arange(0, side, 2), np.arange(1, side, 2)])
    sort = np.zeros((side, side), np.float32)
    sort[order, np.arange(side)] = 1.0
    return np.stack([m for pair in tables for m in pair]), sort.astype(jnp.bfloat16)


def permute_kernel(amp_ref, sort_ref, sort_t_ref, out_ref):
    def one(slot, carry):
        rows = jnp.dot(sort_t_ref[...], amp_ref[slot], preferred_element_type=jnp.float32)
        both = jnp.dot(rows.astype(jnp.bfloat16), sort_ref[...], preferred_element_type=jnp.float32)
        out_ref[slot] = both.astype(jnp.bfloat16)
        return carry

    lax.fori_loop(0, amp_ref.shape[0], one, 0)


def sorted_amplitudes(amplitudes, sort):
    return pl.pallas_call(
        permute_kernel,
        out_shape=jax.ShapeDtypeStruct(amplitudes.shape, amplitudes.dtype),
        compiler_params=pltpu.CompilerParams(vmem_limit_bytes=63 * 2**20),
        cost_estimate=pl.CostEstimate(flops=400_000_000, bytes_accessed=1_600_000, transcendentals=0),
        name="sort_amplitudes",
    )(amplitudes, jnp.asarray(sort), jnp.asarray(sort.T))


def hi_lo(value):
    high = value.astype(jnp.bfloat16)
    return high, (value - high.astype(jnp.float32)).astype(jnp.bfloat16)


def matrix(table_ref, odd, turned, axis):
    high, low = table_ref[4 * odd + turned], table_ref[4 * odd + 2 + turned]
    return jnp.concatenate([high, high, low], axis=axis)


def times_right(value, table_ref, odd, turned):
    high, low = hi_lo(value)
    stacked = jnp.concatenate([high, low, high], axis=1)
    return jnp.dot(stacked, matrix(table_ref, odd, turned, 0), preferred_element_type=jnp.float32)


def times_left(table_ref, odd, turned, value):
    high, low = hi_lo(value)
    stacked = jnp.concatenate([high, low, high], axis=0)
    return jnp.dot(matrix(table_ref, odd, turned, 1), stacked, preferred_element_type=jnp.float32)


def lane_rotated(left, right, shift, wrapped):
    left, right = pltpu.roll(left, shift, 1), pltpu.roll(right, shift, 1)
    return jnp.where(wrapped, right, left), jnp.where(wrapped, left, right)


def slot_steps(slot, live, descent, place_ref, amp_ref, probe_ref, table_ref, ext, total, grad_probe):
    side = probe_ref.shape[1]
    half = side // 2
    row, col = place_ref[slot, 0], place_ref[slot, 1]
    rows = pl.ds(row, side)
    first = col // LANE_TILE
    shift = col - first * LANE_TILE
    third = jnp.minimum(first + 2, ext.shape[0] - 1)
    lanes = lax.broadcasted_iota(jnp.int32, (side, LANE_TILE), 1)
    wrapped = lanes < shift

    def patch(part):
        return jnp.where(wrapped, ext[third, part, rows, :], ext[first, part, rows, :]), ext[first + 1, part, rows, :]

    def probe(part):
        return lane_rotated(probe_ref[part, :, :half], probe_ref[part, :, half:], shift, wrapped)

    patch_re, patch_im = patch(0), patch(1)
    probe_re, probe_im = probe(0), probe(1)
    exit_re = [p * q - r * s for p, q, r, s in zip(probe_re, patch_re, probe_im, patch_im)]
    exit_im = [p * q + r * s for p, q, r, s in zip(probe_re, patch_im, probe_im, patch_re)]
    even = jnp.concatenate([exit_re[0] + exit_re[1], exit_im[0] + exit_im[1]], axis=1)
    odd = jnp.concatenate([exit_re[0] - exit_re[1], exit_im[0] - exit_im[1]], axis=1)
    even = times_right(even, table_ref, 0, 0)
    odd = times_right(odd, table_ref, 1, 0)
    yield
    wave_re = jnp.concatenate([even[:, :half], odd[:, :half]], axis=1)
    wave_im = jnp.concatenate([even[:, half:], odd[:, half:]], axis=1)
    even = jnp.concatenate([wave_re[:half] + wave_re[half:], wave_im[:half] + wave_im[half:]], axis=0)
    odd = jnp.concatenate([wave_re[:half] - wave_re[half:], wave_im[:half] - wave_im[half:]], axis=0)
    even = times_left(table_ref, 0, 1, even)
    odd = times_left(table_ref, 1, 1, odd)
    yield

    def kept(spec, rows):
        spec_re, spec_im = spec[:half], spec[half:]
        amplitude = amp_ref[slot, rows, :].astype(jnp.float32)
        keeping = live - live * amplitude * lax.rsqrt(spec_re * spec_re + spec_im * spec_im + 1.0)
        return jnp.concatenate([spec_re * keeping, spec_im * keeping], axis=0)

    even = times_left(table_ref, 0, 0, kept(even, slice(0, half)))
    odd = times_left(table_ref, 1, 0, kept(odd, slice(half, side)))
    wave_re = jnp.concatenate([even[:half] + odd[:half], even[:half] - odd[:half]], axis=0)
    wave_im = jnp.concatenate([even[half:] + odd[half:], even[half:] - odd[half:]], axis=0)
    yield
    even = times_right(jnp.concatenate([wave_re[:, :half], wave_im[:, :half]], axis=1), table_ref, 0, 1)
    odd = times_right(jnp.concatenate([wave_re[:, half:], wave_im[:, half:]], axis=1), table_ref, 1, 1)
    yield
    resid_re = (even[:, :half] + odd[:, :half], even[:, :half] - odd[:, :half])
    resid_im = (even[:, half:] + odd[:, half:], even[:, half:] - odd[:, half:])
    back = jnp.where(shift == 0, 0, LANE_TILE - shift)
    from_left = lanes < LANE_TILE - shift
    for part in (0, 1):
        if part == 0:
            terms = [p * q + r * s for p, q, r, s in zip(patch_re, resid_re, patch_im, resid_im)]
        else:
            terms = [p * q - r * s for p, q, r, s in zip(patch_re, resid_im, patch_im, resid_re)]
        left, right = (pltpu.roll(term, back, 1) for term in terms)
        grad_probe[part, :, :half] += jnp.where(from_left, left, right)
        grad_probe[part, :, half:] += jnp.where(from_left, right, left)
    for part in (0, 1):
        if part == 0:
            terms = [p * q + r * s for p, q, r, s in zip(probe_re, resid_re, probe_im, resid_im)]
        else:
            terms = [p * q - r * s for p, q, r, s in zip(probe_re, resid_im, probe_im, resid_re)]
        terms = [descent * term for term in terms]
        total[first, part, rows, :] += jnp.where(wrapped, 0.0, terms[0])
        total[first + 1, part, rows, :] += terms[1]
        total[third, part, rows, :] += jnp.where(wrapped, terms[0], 0.0)


def iteration_kernel(first, pieces, *refs):
    if first:
        place_ref, info_ref, own_hbm, below_hbm, probe_hbm = refs[:5]
        refs = refs[5:]
    else:
        place_ref, info_ref, step_ref, own_hbm, below_hbm, probe_hbm = refs[:6]
        sum_hbms, refs = refs[6:8], refs[8:]
    amp_hbm, table_hbm, keep_out, send_out = refs[:4]
    low_outs, refs = refs[4 : 4 + pieces], refs[4 + pieces :]
    own_out, refs = refs[0], refs[1:]
    if not first:
        probe_out, refs = refs[0], refs[1:]
    ext, total, probe_ref, grad_probe, amp_ref, table_ref, sems, in_sems, out_sems = refs
    columns = ext.shape[0]
    rows = ext.shape[2] // 2
    half = probe_ref.shape[1] // 2
    own, low = pl.ds(0, rows), pl.ds(rows, rows)
    mine = pl.ds(pl.multiple_of(info_ref[2] * half, half), half)
    others = pl.ds(pl.multiple_of((1 - info_ref[2]) * half, half), half)

    def by_column(hbm, vmem, where):
        return [
            (hbm.at[part, :, pl.ds(LANE_TILE * column, LANE_TILE)], vmem.at[column, part, where, :])
            for part in (0, 1)
            for column in range(columns)
        ]

    def by_piece(hbms, vmem, where):
        size = columns // len(hbms)
        return [(hbm, vmem.at[pl.ds(size * piece, size), :, where, :]) for piece, hbm in enumerate(hbms)]

    pairs = [(probe_hbm, probe_ref)]
    if not first:
        pairs += [(sum_hbms[0], grad_probe.at[:, mine, :]), (sum_hbms[1], grad_probe.at[:, others, :])]
    early = len(pairs)
    if first:
        pairs += by_column(own_hbm, ext, own) + by_column(below_hbm, ext, low)
    else:
        pairs += by_piece([own_hbm], ext, own) + by_piece([below_hbm], ext, low)
    pairs += [(table_hbm, table_ref), (amp_hbm, amp_ref)]
    copies = [pltpu.make_async_copy(src, dst, in_sems.at[i]) for i, (src, dst) in enumerate(pairs)]
    for copy in copies:
        copy.start()
    total[:, :, low, :] = jnp.zeros((columns, 2, rows, LANE_TILE), jnp.float32)
    for copy in copies[:early]:
        copy.wait()
    if not first:
        probe_ref[...] = probe_ref[...] - step_ref[0] * grad_probe[...]
        probe_copy = pltpu.make_async_copy(probe_ref, probe_out, sems.at[2])
        probe_copy.start()
    power = probe_ref[0] * probe_ref[0] + probe_ref[1] * probe_ref[1]
    descent = -1.0 / (jnp.max(power) + 1e-06)
    grad_probe[...] = jnp.zeros_like(grad_probe)
    for copy in copies[early:]:
        copy.wait()
    total[:, :, own, :] = ext[:, :, own, :]

    count = info_ref[0]

    def slots(index, carry):
        steps = []
        for slot in (TOGETHER * index + k for k in range(TOGETHER)):
            live = (slot < count).astype(jnp.float32)
            slot = jnp.minimum(slot, amp_ref.shape[0] - 1)
            steps.append(
                slot_steps(slot, live, descent, place_ref, amp_ref, probe_ref, table_ref, ext, total, grad_probe)
            )
        for unused in zip_longest(*steps):
            pass
        return carry

    lax.fori_loop(0, (count + TOGETHER - 1) // TOGETHER, slots, 0)

    @pl.when(info_ref[1] == 0)
    def _():
        total[:, :, low, :] = jnp.zeros((columns, 2, rows, LANE_TILE), jnp.float32)

    outs = [
        pltpu.make_async_copy(grad_probe.at[:, others, :], send_out, sems.at[0]),
        pltpu.make_async_copy(grad_probe.at[:, mine, :], keep_out, sems.at[1]),
    ]
    pairs = by_piece(low_outs, total, low)
    pairs += by_piece([own_out], total, own) if first else by_column(own_out, total, own)
    outs += [pltpu.make_async_copy(src, dst, out_sems.at[i]) for i, (dst, src) in enumerate(pairs)]
    for copy in outs:
        copy.start()
    for copy in outs:
        copy.wait()
    if not first:
        probe_copy.wait()


def iteration(first, scalars, strips, probes, amplitudes, table, shape):
    parts, rows, width = shape
    columns = width // LANE_TILE
    pieces = 1 if first or columns % PIECES else PIECES
    smem = pl.BlockSpec(memory_space=pltpu.SMEM)
    anywhere = pl.BlockSpec(memory_space=pl.ANY)
    probe_shape = jax.ShapeDtypeStruct(probes[0].shape, jnp.float32)
    half_shape = jax.ShapeDtypeStruct((parts, probe_shape.shape[1] // 2, probe_shape.shape[2]), jnp.float32)
    strip = jax.ShapeDtypeStruct((columns, parts, rows, LANE_TILE), jnp.float32)
    piece = jax.ShapeDtypeStruct((columns // pieces, *strip.shape[1:]), jnp.float32)
    arrays = (*strips, *probes, amplitudes, table)
    out_shape = [half_shape, half_shape] + [piece] * pieces
    out_shape += [strip] if first else [jax.ShapeDtypeStruct(shape, jnp.float32), probe_shape]
    extended = (columns, parts, 2 * rows, LANE_TILE)
    outs = pl.pallas_call(
        partial(iteration_kernel, first, pieces),
        out_shape=out_shape,
        in_specs=[smem] * len(scalars) + [anywhere] * len(arrays),
        out_specs=[anywhere] * len(out_shape),
        scratch_shapes=[
            pltpu.VMEM(extended, jnp.float32),
            pltpu.VMEM(extended, jnp.float32),
            pltpu.VMEM(probe_shape.shape, jnp.float32),
            pltpu.VMEM(probe_shape.shape, jnp.float32),
            pltpu.VMEM(amplitudes.shape, amplitudes.dtype),
            pltpu.VMEM(table.shape, table.dtype),
            pltpu.SemaphoreType.DMA((3,)),
            pltpu.SemaphoreType.DMA((5 + 2 * parts * columns,)),
            pltpu.SemaphoreType.DMA((parts * columns + pieces,)),
        ],
        compiler_params=pltpu.CompilerParams(vmem_limit_bytes=62 * 2**20),
        cost_estimate=pl.CostEstimate(flops=8_000_000_000, bytes_accessed=8_000_000, transcendentals=400_000),
        name="iteration",
    )(*scalars, *arrays)
    return outs[:2], outs[2 : 2 + pieces], outs[2 + pieces :]


def passed_along(value, axis, by):
    size = lax.axis_size(axis)
    pairs = [(i, i + by) for i in range(size) if 0 <= i + by < size]
    return lax.ppermute(value, axis, pairs)


def swapped(value, axis, bit):
    size = lax.axis_size(axis)
    return lax.ppermute(value, axis, [(i, i ^ bit) for i in range(size)])


def upper_of(axis, bit):
    return (lax.axis_index(axis) & bit) != 0


def bits_of(axis):
    size = lax.axis_size(axis)
    if size & (size - 1) or size < 8:
        return []
    bits = [1 << k for k in range(size.bit_length() - 1)]
    return [bits[0], *bits[2:], bits[1]]


def joined(mine, other, upper):
    return jnp.concatenate([jnp.where(upper, other, mine), jnp.where(upper, mine, other)], axis=1)


def summed_beside(keep, send, axis, pieces, late, used=None):
    bits = bits_of(axis)
    pieces = [[list(arrays), by] for arrays, by in pieces]
    upper = upper_of(axis, 1)

    def moving(piece):
        return [passed_along(array, axis, by) for array, by in zip(*piece)]

    if not bits:
        value = lax.psum(joined(keep, send, upper), axis)
        half = value.shape[1] // 2
        first, second = value[:, :half], value[:, half:]
        return jnp.where(upper, second, first), jnp.where(upper, first, second), [
            used(*moving(piece)) if used else moving(piece) for piece in pieces
        ]
    moved = [moving(piece) for piece in pieces[:1]]
    arrived = -late

    def behind(value):
        if len(moved) < len(pieces):
            value, pieces[len(moved)][0] = lax.optimization_barrier((value, pieces[len(moved)][0]))
            moved.append(moving(pieces[len(moved)]))
        return value

    def ahead(value):
        nonlocal arrived
        if 0 <= arrived < len(moved):
            value, moved[arrived] = lax.optimization_barrier((value, moved[arrived]))
        arrived += 1
        return value

    value = keep + swapped(send, axis, bits[0])
    inner = upper_of(axis, bits[1])
    half = value.shape[1] // 2
    first, second = value[:, :half], value[:, half:]
    value = jnp.where(inner, second, first) + swapped(jnp.where(inner, first, second), axis, bits[1])
    for step, bit in enumerate(bits[2:]):
        if step >= late:
            value = behind(value)
        value = ahead(value + swapped(value, axis, bit))
    while len(moved) < len(pieces):
        value = behind(value)
    if used:
        moved = [used(*moved[0])]
        arrived = 0
    value = ahead(joined(value, swapped(value, axis, bits[1]), inner))
    return value, swapped(value, axis, bits[0]), moved


def on_device(object_field, probe, amplitudes, offsets, counts):
    strip_rows = object_field.shape[1]
    side = probe.shape[1]
    strip_count = lax.axis_size("pos")
    device_index = lax.axis_index("pos")
    table, sort = constants(side)
    table = jnp.asarray(table)
    below = passed_along(object_field, "pos", -1)
    own_count = lax.dynamic_index_in_dim(counts, device_index, keepdims=False)
    not_last = (device_index + 1 < strip_count).astype(jnp.int32)
    info = jnp.stack([own_count, not_last, device_index % 2])
    step = (8.0 / jnp.sum(counts).astype(jnp.float32))[None]
    place = jnp.stack([offsets[:, 0] - device_index * strip_rows, offsets[:, 1]], axis=1)
    amps = sorted_amplitudes(amplitudes, sort)
    shape = object_field.shape
    (keep, send), (low,), (own,) = iteration(True, (place, info), (object_field, below), (probe,), amps, table, shape)
    mine, other, [strips] = summed_beside(
        keep, send, "pos", [((low, own), (1, -1))], 1, lambda above, below: (own + above, below + low)
    )
    (keep, send), lows, (own, probe_now) = iteration(
        False, (place, info, step), strips, (probe, mine, other), amps, table, shape
    )
    mine, other, moved = summed_beside(keep, send, "pos", [((low,), (1,)) for low in lows], 1)
    above = [above[column] for (above,) in moved for column in range(above.shape[0])]
    probe_sum = joined(mine, other, upper_of("pos", 1))
    return (own + jnp.concatenate(above, axis=2), probe_now - step * probe_sum)


def solution(mesh):
    in_specs = (
        P("groups", "pos", None),
        P("groups", None, None),
        P(("groups", "pos"), None, None),
        P(("groups", "pos"), None),
        P("groups"),
    )
    out_specs = (P("groups", "pos", None), P("groups", None, None))
    return jax.shard_map(
        on_device, mesh=mesh, in_specs=in_specs, out_specs=out_specs, check_vma=False
    )
```

```python
from functools import partial
from itertools import zip_longest
import math

import jax
import jax.numpy as jnp
import numpy as np
from jax import lax
from jax.experimental import pallas as pl
from jax.experimental.pallas import tpu as pltpu
from jax.sharding import PartitionSpec as P

LANE_TILE = 128
PIECES = 3
TOGETHER = 3


def split_bf16(array):
    high = array.astype(jnp.bfloat16)
    low = (array - high.astype(np.float32)).astype(jnp.bfloat16)
    return high, low


def constants(side):
    half = side // 2
    index = np.arange(half)
    parts = []
    for odd in (0, 1):
        angle = 2.0 * np.pi / side * (index[:, None] * (2 * index[None, :] + odd) % side)
        cosine, sine = np.cos(angle), np.sin(angle)
        matrix = (np.block([[cosine, -sine], [sine, cosine]]) / math.sqrt(side)).astype(np.float32)
        parts.append(split_bf16(matrix))
    tables = [[part, part.T] for pair in parts for part in pair]
    order = np.concatenate([np.arange(0, side, 2), np.arange(1, side, 2)])
    sort = np.zeros((side, side), np.float32)
    sort[order, np.arange(side)] = 1.0
    return np.stack([m for pair in tables for m in pair]), sort.astype(jnp.bfloat16)


def permute_kernel(amp_ref, sort_ref, sort_t_ref, out_ref):
    def one(slot, carry):
        rows = jnp.dot(sort_t_ref[...], amp_ref[slot], preferred_element_type=jnp.float32)
        both = jnp.dot(rows.astype(jnp.bfloat16), sort_ref[...], preferred_element_type=jnp.float32)
        out_ref[slot] = both.astype(jnp.bfloat16)
        return carry

    lax.fori_loop(0, amp_ref.shape[0], one, 0)


def sorted_amplitudes(amplitudes, sort):
    return pl.pallas_call(
        permute_kernel,
        out_shape=jax.ShapeDtypeStruct(amplitudes.shape, amplitudes.dtype),
        compiler_params=pltpu.CompilerParams(vmem_limit_bytes=63 * 2**20),
        cost_estimate=pl.CostEstimate(flops=400_000_000, bytes_accessed=1_600_000, transcendentals=0),
        name="sort_amplitudes",
    )(amplitudes, jnp.asarray(sort), jnp.asarray(sort.T))


def hi_lo(value):
    high = value.astype(jnp.bfloat16)
    return high, (value - high.astype(jnp.float32)).astype(jnp.bfloat16)


def matrix(table_ref, odd, turned, axis):
    high, low = table_ref[4 * odd + turned], table_ref[4 * odd + 2 + turned]
    return jnp.concatenate([high, high, low], axis=axis)


def times_right(value, table_ref, odd, turned):
    high, low = hi_lo(value)
    stacked = jnp.concatenate([high, low, high], axis=1)
    return jnp.dot(stacked, matrix(table_ref, odd, turned, 0), preferred_element_type=jnp.float32)


def times_left(table_ref, odd, turned, value):
    high, low = hi_lo(value)
    stacked = jnp.concatenate([high, low, high], axis=0)
    return jnp.dot(matrix(table_ref, odd, turned, 1), stacked, preferred_element_type=jnp.float32)


def lane_rotated(left, right, shift, wrapped):
    left, right = pltpu.roll(left, shift, 1), pltpu.roll(right, shift, 1)
    return jnp.where(wrapped, right, left), jnp.where(wrapped, left, right)


def slot_steps(slot, live, descent, place_ref, amp_ref, probe_ref, table_ref, ext, total, grad_probe):
    side = probe_ref.shape[1]
    half = side // 2
    row, col = place_ref[slot, 0], place_ref[slot, 1]
    rows = pl.ds(row, side)
    first = col // LANE_TILE
    shift = col - first * LANE_TILE
    third = jnp.minimum(first + 2, ext.shape[0] - 1)
    lanes = lax.broadcasted_iota(jnp.int32, (side, LANE_TILE), 1)
    wrapped = lanes < shift

    def patch(part):
        return jnp.where(wrapped, ext[third, part, rows, :], ext[first, part, rows, :]), ext[first + 1, part, rows, :]

    def probe(part):
        return lane_rotated(probe_ref[part, :, :half], probe_ref[part, :, half:], shift, wrapped)

    patch_re, patch_im = patch(0), patch(1)
    probe_re, probe_im = probe(0), probe(1)
    exit_re = [p * q - r * s for p, q, r, s in zip(probe_re, patch_re, probe_im, patch_im)]
    exit_im = [p * q + r * s for p, q, r, s in zip(probe_re, patch_im, probe_im, patch_re)]
    even = jnp.concatenate([exit_re[0] + exit_re[1], exit_im[0] + exit_im[1]], axis=1)
    odd = jnp.concatenate([exit_re[0] - exit_re[1], exit_im[0] - exit_im[1]], axis=1)
    even = times_right(even, table_ref, 0, 0)
    odd = times_right(odd, table_ref, 1, 0)
    yield
    wave_re = jnp.concatenate([even[:, :half], odd[:, :half]], axis=1)
    wave_im = jnp.concatenate([even[:, half:], odd[:, half:]], axis=1)
    even = jnp.concatenate([wave_re[:half] + wave_re[half:], wave_im[:half] + wave_im[half:]], axis=0)
    odd = jnp.concatenate([wave_re[:half] - wave_re[half:], wave_im[:half] - wave_im[half:]], axis=0)
    even = times_left(table_ref, 0, 1, even)
    odd = times_left(table_ref, 1, 1, odd)
    yield

    def kept(spec, rows):
        spec_re, spec_im = spec[:half], spec[half:]
        amplitude = amp_ref[slot, rows, :].astype(jnp.float32)
        keeping = live - live * amplitude * lax.rsqrt(spec_re * spec_re + spec_im * spec_im + 1.0)
        return jnp.concatenate([spec_re * keeping, spec_im * keeping], axis=0)

    even = times_left(table_ref, 0, 0, kept(even, slice(0, half)))
    odd = times_left(table_ref, 1, 0, kept(odd, slice(half, side)))
    wave_re = jnp.concatenate([even[:half] + odd[:half], even[:half] - odd[:half]], axis=0)
    wave_im = jnp.concatenate([even[half:] + odd[half:], even[half:] - odd[half:]], axis=0)
    yield
    even = times_right(jnp.concatenate([wave_re[:, :half], wave_im[:, :half]], axis=1), table_ref, 0, 1)
    odd = times_right(jnp.concatenate([wave_re[:, half:], wave_im[:, half:]], axis=1), table_ref, 1, 1)
    yield
    resid_re = (even[:, :half] + odd[:, :half], even[:, :half] - odd[:, :half])
    resid_im = (even[:, half:] + odd[:, half:], even[:, half:] - odd[:, half:])
    back = jnp.where(shift == 0, 0, LANE_TILE - shift)
    from_left = lanes < LANE_TILE - shift
    for part in (0, 1):
        if part == 0:
            terms = [p * q + r * s for p, q, r, s in zip(patch_re, resid_re, patch_im, resid_im)]
        else:
            terms = [p * q - r * s for p, q, r, s in zip(patch_re, resid_im, patch_im, resid_re)]
        left, right = (pltpu.roll(term, back, 1) for term in terms)
        grad_probe[part, :, :half] += jnp.where(from_left, left, right)
        grad_probe[part, :, half:] += jnp.where(from_left, right, left)
    for part in (0, 1):
        if part == 0:
            terms = [p * q + r * s for p, q, r, s in zip(probe_re, resid_re, probe_im, resid_im)]
        else:
            terms = [p * q - r * s for p, q, r, s in zip(probe_re, resid_im, probe_im, resid_re)]
        terms = [descent * term for term in terms]
        total[first, part, rows, :] += jnp.where(wrapped, 0.0, terms[0])
        total[first + 1, part, rows, :] += terms[1]
        total[third, part, rows, :] += jnp.where(wrapped, terms[0], 0.0)


def iteration_kernel(first, pieces, *refs):
    place_ref, info_ref, step_ref, own_hbm, below_hbm, probe_hbm = refs[:6]
    refs = refs[6:]
    if not first:
        sum_hbms, refs = refs[:2], refs[2:]
    amp_hbm, table_hbm, keep_out, send_out = refs[:4]
    low_outs, refs = refs[4 : 4 + pieces], refs[4 + pieces :]
    own_out, refs = refs[0], refs[1:]
    if not first:
        probe_out, refs = refs[0], refs[1:]
    ext, total, probe_ref, grad_probe, amp_ref, table_ref, sems, in_sems, out_sems = refs
    columns = ext.shape[0]
    rows = ext.shape[2] // 2
    half = probe_ref.shape[1] // 2
    own, low = pl.ds(0, rows), pl.ds(rows, rows)
    mine = pl.ds(pl.multiple_of(info_ref[2] * half, half), half)
    others = pl.ds(pl.multiple_of((1 - info_ref[2]) * half, half), half)

    def by_column(hbm, vmem, where):
        return [
            (hbm.at[part, :, pl.ds(LANE_TILE * column, LANE_TILE)], vmem.at[column, part, where, :])
            for part in (0, 1)
            for column in range(columns)
        ]

    def by_piece(hbms, vmem, where):
        size = columns // len(hbms)
        return [(hbm, vmem.at[pl.ds(size * piece, size), :, where, :]) for piece, hbm in enumerate(hbms)]

    pairs = [(probe_hbm, probe_ref)]
    if not first:
        pairs += [(sum_hbms[0], grad_probe.at[:, mine, :]), (sum_hbms[1], grad_probe.at[:, others, :])]
    early = len(pairs)
    if first:
        pairs += by_column(own_hbm, ext, own) + by_column(below_hbm, ext, low)
    else:
        pairs += by_piece([own_hbm], ext, own) + by_piece([below_hbm], ext, low)
    pairs += [(table_hbm, table_ref), (amp_hbm, amp_ref)]
    copies = [pltpu.make_async_copy(src, dst, in_sems.at[i]) for i, (src, dst) in enumerate(pairs)]
    for copy in copies:
        copy.start()
    total[:, :, low, :] = jnp.zeros((columns, 2, rows, LANE_TILE), jnp.float32)
    for copy in copies[:early]:
        copy.wait()
    if not first:
        probe_ref[...] = probe_ref[...] - step_ref[0] * grad_probe[...]
        probe_copy = pltpu.make_async_copy(probe_ref, probe_out, sems.at[2])
        probe_copy.start()
    power = probe_ref[0] * probe_ref[0] + probe_ref[1] * probe_ref[1]
    descent = -1.0 / (jnp.max(power) + 1e-06)
    grad_probe[...] = jnp.zeros_like(grad_probe)
    for copy in copies[early:]:
        copy.wait()
    total[:, :, own, :] = ext[:, :, own, :]

    count = info_ref[0]

    def slots(index, carry):
        steps = []
        for slot in (TOGETHER * index + k for k in range(TOGETHER)):
            live = (slot < count).astype(jnp.float32)
            slot = jnp.minimum(slot, amp_ref.shape[0] - 1)
            steps.append(
                slot_steps(slot, live, descent, place_ref, amp_ref, probe_ref, table_ref, ext, total, grad_probe)
            )
        for unused in zip_longest(*steps):
            pass
        return carry

    lax.fori_loop(0, (count + TOGETHER - 1) // TOGETHER, slots, 0)

    @pl.when(info_ref[1] == 0)
    def _():
        total[:, :, low, :] = jnp.zeros((columns, 2, rows, LANE_TILE), jnp.float32)

    outs = [
        pltpu.make_async_copy(grad_probe.at[:, others, :], send_out, sems.at[0]),
        pltpu.make_async_copy(grad_probe.at[:, mine, :], keep_out, sems.at[1]),
    ]
    pairs = by_piece(low_outs, total, low)
    pairs += by_piece([own_out], total, own) if first else by_column(own_out, total, own)
    outs += [pltpu.make_async_copy(src, dst, out_sems.at[i]) for i, (dst, src) in enumerate(pairs)]
    for copy in outs:
        copy.start()
    for copy in outs:
        copy.wait()
    if not first:
        probe_copy.wait()


def iteration(first, scalars, strips, probes, amplitudes, table, shape):
    parts, rows, width = shape
    columns = width // LANE_TILE
    pieces = 1 if first or columns % PIECES else PIECES
    smem = pl.BlockSpec(memory_space=pltpu.SMEM)
    anywhere = pl.BlockSpec(memory_space=pl.ANY)
    probe_shape = jax.ShapeDtypeStruct(probes[0].shape, jnp.float32)
    half_shape = jax.ShapeDtypeStruct((parts, probe_shape.shape[1] // 2, probe_shape.shape[2]), jnp.float32)
    strip = jax.ShapeDtypeStruct((columns, parts, rows, LANE_TILE), jnp.float32)
    piece = jax.ShapeDtypeStruct((columns // pieces, *strip.shape[1:]), jnp.float32)
    arrays = (*strips, *probes, amplitudes, table)
    out_shape = [half_shape, half_shape] + [piece] * pieces
    out_shape += [strip] if first else [jax.ShapeDtypeStruct(shape, jnp.float32), probe_shape]
    extended = (columns, parts, 2 * rows, LANE_TILE)
    outs = pl.pallas_call(
        partial(iteration_kernel, first, pieces),
        out_shape=out_shape,
        in_specs=[smem] * len(scalars) + [anywhere] * len(arrays),
        out_specs=[anywhere] * len(out_shape),
        scratch_shapes=[
            pltpu.VMEM(extended, jnp.float32),
            pltpu.VMEM(extended, jnp.float32),
            pltpu.VMEM(probe_shape.shape, jnp.float32),
            pltpu.VMEM(probe_shape.shape, jnp.float32),
            pltpu.VMEM(amplitudes.shape, amplitudes.dtype),
            pltpu.VMEM(table.shape, table.dtype),
            pltpu.SemaphoreType.DMA((3,)),
            pltpu.SemaphoreType.DMA((5 + 2 * parts * columns,)),
            pltpu.SemaphoreType.DMA((parts * columns + pieces,)),
        ],
        compiler_params=pltpu.CompilerParams(vmem_limit_bytes=62 * 2**20),
        cost_estimate=pl.CostEstimate(flops=8_000_000_000, bytes_accessed=8_000_000, transcendentals=400_000),
        name="iteration",
    )(*scalars, *arrays)
    return outs[:2], outs[2 : 2 + pieces], outs[2 + pieces :]


def passed_along(value, axis, by):
    size = lax.axis_size(axis)
    pairs = [(i, i + by) for i in range(size) if 0 <= i + by < size]
    return lax.ppermute(value, axis, pairs)


def swapped(value, axis, bit):
    size = lax.axis_size(axis)
    return lax.ppermute(value, axis, [(i, i ^ bit) for i in range(size)])


def upper_of(axis, bit):
    return (lax.axis_index(axis) & bit) != 0


def bits_of(axis):
    size = lax.axis_size(axis)
    if size & (size - 1) or size < 8:
        return []
    bits = [1 << k for k in range(size.bit_length() - 1)]
    return [bits[0], *bits[2:], bits[1]]


def joined(mine, other, upper):
    return jnp.concatenate([jnp.where(upper, other, mine), jnp.where(upper, mine, other)], axis=1)


def summed_beside(keep, send, axis, pieces, late, used=None):
    bits = bits_of(axis)
    pieces = [[list(arrays), by] for arrays, by in pieces]
    upper = upper_of(axis, 1)

    def moving(piece):
        return [passed_along(array, axis, by) for array, by in zip(*piece)]

    if not bits:
        value = lax.psum(joined(keep, send, upper), axis)
        half = value.shape[1] // 2
        first, second = value[:, :half], value[:, half:]
        return jnp.where(upper, second, first), jnp.where(upper, first, second), [
            used(*moving(piece)) if used else moving(piece) for piece in pieces
        ]
    moved = [moving(piece) for piece in pieces[:1]]
    arrived = -late

    def behind(value):
        if len(moved) < len(pieces):
            value, pieces[len(moved)][0] = lax.optimization_barrier((value, pieces[len(moved)][0]))
            moved.append(moving(pieces[len(moved)]))
        return value

    def ahead(value):
        nonlocal arrived
        if 0 <= arrived < len(moved):
            value, moved[arrived] = lax.optimization_barrier((value, moved[arrived]))
        arrived += 1
        return value

    value = keep + swapped(send, axis, bits[0])
    inner = upper_of(axis, bits[1])
    half = value.shape[1] // 2
    first, second = value[:, :half], value[:, half:]
    value = jnp.where(inner, second, first) + swapped(jnp.where(inner, first, second), axis, bits[1])
    for bit in bits[2:]:
        value = behind(value)
        value = ahead(value + swapped(value, axis, bit))
    if used:
        moved = [used(*moved[0])]
        arrived = 0
    value = ahead(joined(value, swapped(value, axis, bits[1]), inner))
    return value, swapped(value, axis, bits[0]), moved


def on_device(object_field, probe, amplitudes, offsets, counts):
    strip_rows = object_field.shape[1]
    side = probe.shape[1]
    strip_count = lax.axis_size("pos")
    device_index = lax.axis_index("pos")
    table, sort = constants(side)
    table = jnp.asarray(table)
    below = passed_along(object_field, "pos", -1)
    own_count = lax.dynamic_index_in_dim(counts, device_index, keepdims=False)
    not_last = (device_index + 1 < strip_count).astype(jnp.int32)
    info = jnp.stack([own_count, not_last, device_index % 2])
    step = (8.0 / jnp.sum(counts).astype(jnp.float32))[None]
    place = jnp.stack([offsets[:, 0] - device_index * strip_rows, offsets[:, 1]], axis=1)
    amps = sorted_amplitudes(amplitudes, sort)
    shape = object_field.shape
    (keep, send), (low,), (own,) = iteration(True, (place, info, step), (object_field, below), (probe,), amps, table, shape)
    mine, other, [strips] = summed_beside(
        keep, send, "pos", [((low, own), (1, -1))], 1, lambda above, below: (own + above, below + low)
    )
    (keep, send), lows, (own, probe_now) = iteration(
        False, (place, info, step), strips, (probe, mine, other), amps, table, shape
    )
    mine, other, moved = summed_beside(keep, send, "pos", [((low,), (1,)) for low in lows], 0)
    above = [above[column] for (above,) in moved for column in range(above.shape[0])]
    probe_sum = joined(mine, other, upper_of("pos", 1))
    return (own + jnp.concatenate(above, axis=2), probe_now - step * probe_sum)


def solution(mesh):
    in_specs = (
        P("groups", "pos", None),
        P("groups", None, None),
        P(("groups", "pos"), None, None),
        P(("groups", "pos"), None),
        P("groups"),
    )
    out_specs = (P("groups", "pos", None), P("groups", None, None))
    return jax.shard_map(
        on_device, mesh=mesh, in_specs=in_specs, out_specs=out_specs, check_vma=False
    )
```

```python
from functools import partial
from itertools import zip_longest
import math

import jax
import jax.numpy as jnp
import numpy as np
from jax import lax
from jax.experimental import pallas as pl
from jax.experimental.pallas import tpu as pltpu
from jax.sharding import PartitionSpec as P

LANE_TILE = 128
PIECES = 3
TOGETHER = 3


def split_bf16(array):
    high = array.astype(jnp.bfloat16)
    low = (array - high.astype(np.float32)).astype(jnp.bfloat16)
    return high, low


def constants(side):
    half = side // 2
    index = np.arange(half)
    parts = []
    for odd in (0, 1):
        angle = 2.0 * np.pi / side * (index[:, None] * (2 * index[None, :] + odd) % side)
        cosine, sine = np.cos(angle), np.sin(angle)
        matrix = (np.block([[cosine, -sine], [sine, cosine]]) / math.sqrt(side)).astype(np.float32)
        parts.append(split_bf16(matrix))
    tables = [[part, part.T] for pair in parts for part in pair]
    order = np.concatenate([np.arange(0, side, 2), np.arange(1, side, 2)])
    sort = np.zeros((side, side), np.float32)
    sort[order, np.arange(side)] = 1.0
    return np.stack([m for pair in tables for m in pair]), sort.astype(jnp.bfloat16)


def permute_kernel(amp_ref, sort_ref, sort_t_ref, out_ref):
    def one(slot, carry):
        rows = jnp.dot(sort_t_ref[...], amp_ref[slot], preferred_element_type=jnp.float32)
        both = jnp.dot(rows.astype(jnp.bfloat16), sort_ref[...], preferred_element_type=jnp.float32)
        out_ref[slot] = both.astype(jnp.bfloat16)
        return carry

    lax.fori_loop(0, amp_ref.shape[0], one, 0)


def sorted_amplitudes(amplitudes, sort):
    return pl.pallas_call(
        permute_kernel,
        out_shape=jax.ShapeDtypeStruct(amplitudes.shape, amplitudes.dtype),
        compiler_params=pltpu.CompilerParams(vmem_limit_bytes=63 * 2**20),
        cost_estimate=pl.CostEstimate(flops=400_000_000, bytes_accessed=1_600_000, transcendentals=0),
        name="sort_amplitudes",
    )(amplitudes, jnp.asarray(sort), jnp.asarray(sort.T))


def hi_lo(value):
    high = value.astype(jnp.bfloat16)
    return high, (value - high.astype(jnp.float32)).astype(jnp.bfloat16)


def matrix(table_ref, odd, turned, axis):
    high, low = table_ref[4 * odd + turned], table_ref[4 * odd + 2 + turned]
    return jnp.concatenate([high, high, low], axis=axis)


def times_right(value, table_ref, odd, turned):
    high, low = hi_lo(value)
    stacked = jnp.concatenate([high, low, high], axis=1)
    return jnp.dot(stacked, matrix(table_ref, odd, turned, 0), preferred_element_type=jnp.float32)


def times_left(table_ref, odd, turned, value):
    high, low = hi_lo(value)
    stacked = jnp.concatenate([high, low, high], axis=0)
    return jnp.dot(matrix(table_ref, odd, turned, 1), stacked, preferred_element_type=jnp.float32)


def lane_rotated(left, right, shift, wrapped):
    left, right = pltpu.roll(left, shift, 1), pltpu.roll(right, shift, 1)
    return jnp.where(wrapped, right, left), jnp.where(wrapped, left, right)


def slot_steps(slot, live, descent, place_ref, amp_ref, probe_ref, table_ref, ext, total, grad_probe):
    side = probe_ref.shape[1]
    half = side // 2
    row, col = place_ref[slot, 0], place_ref[slot, 1]
    rows = pl.ds(row, side)
    first = col // LANE_TILE
    shift = col - first * LANE_TILE
    third = jnp.minimum(first + 2, ext.shape[0] - 1)
    lanes = lax.broadcasted_iota(jnp.int32, (side, LANE_TILE), 1)
    wrapped = lanes < shift

    def patch(part):
        return jnp.where(wrapped, ext[third, part, rows, :], ext[first, part, rows, :]), ext[first + 1, part, rows, :]

    def probe(part):
        return lane_rotated(probe_ref[part, :, :half], probe_ref[part, :, half:], shift, wrapped)

    patch_re, patch_im = patch(0), patch(1)
    probe_re, probe_im = probe(0), probe(1)
    exit_re = [p * q - r * s for p, q, r, s in zip(probe_re, patch_re, probe_im, patch_im)]
    exit_im = [p * q + r * s for p, q, r, s in zip(probe_re, patch_im, probe_im, patch_re)]
    even = jnp.concatenate([exit_re[0] + exit_re[1], exit_im[0] + exit_im[1]], axis=1)
    odd = jnp.concatenate([exit_re[0] - exit_re[1], exit_im[0] - exit_im[1]], axis=1)
    even = times_right(even, table_ref, 0, 0)
    odd = times_right(odd, table_ref, 1, 0)
    yield
    wave_re = jnp.concatenate([even[:, :half], odd[:, :half]], axis=1)
    wave_im = jnp.concatenate([even[:, half:], odd[:, half:]], axis=1)
    even = jnp.concatenate([wave_re[:half] + wave_re[half:], wave_im[:half] + wave_im[half:]], axis=0)
    odd = jnp.concatenate([wave_re[:half] - wave_re[half:], wave_im[:half] - wave_im[half:]], axis=0)
    even = times_left(table_ref, 0, 1, even)
    odd = times_left(table_ref, 1, 1, odd)
    yield

    def kept(spec, rows):
        spec_re, spec_im = spec[:half], spec[half:]
        amplitude = amp_ref[slot, rows, :].astype(jnp.float32)
        keeping = live - live * amplitude * lax.rsqrt(spec_re * spec_re + spec_im * spec_im + 1.0)
        return jnp.concatenate([spec_re * keeping, spec_im * keeping], axis=0)

    even = times_left(table_ref, 0, 0, kept(even, slice(0, half)))
    odd = times_left(table_ref, 1, 0, kept(odd, slice(half, side)))
    wave_re = jnp.concatenate([even[:half] + odd[:half], even[:half] - odd[:half]], axis=0)
    wave_im = jnp.concatenate([even[half:] + odd[half:], even[half:] - odd[half:]], axis=0)
    yield
    even = times_right(jnp.concatenate([wave_re[:, :half], wave_im[:, :half]], axis=1), table_ref, 0, 1)
    odd = times_right(jnp.concatenate([wave_re[:, half:], wave_im[:, half:]], axis=1), table_ref, 1, 1)
    yield
    resid_re = (even[:, :half] + odd[:, :half], even[:, :half] - odd[:, :half])
    resid_im = (even[:, half:] + odd[:, half:], even[:, half:] - odd[:, half:])
    back = jnp.where(shift == 0, 0, LANE_TILE - shift)
    from_left = lanes < LANE_TILE - shift
    for part in (0, 1):
        if part == 0:
            terms = [p * q + r * s for p, q, r, s in zip(patch_re, resid_re, patch_im, resid_im)]
        else:
            terms = [p * q - r * s for p, q, r, s in zip(patch_re, resid_im, patch_im, resid_re)]
        left, right = (pltpu.roll(term, back, 1) for term in terms)
        grad_probe[part, :, :half] += jnp.where(from_left, left, right)
        grad_probe[part, :, half:] += jnp.where(from_left, right, left)
    for part in (0, 1):
        if part == 0:
            terms = [p * q + r * s for p, q, r, s in zip(probe_re, resid_re, probe_im, resid_im)]
        else:
            terms = [p * q - r * s for p, q, r, s in zip(probe_re, resid_im, probe_im, resid_re)]
        terms = [descent * term for term in terms]
        total[first, part, rows, :] += jnp.where(wrapped, 0.0, terms[0])
        total[first + 1, part, rows, :] += terms[1]
        total[third, part, rows, :] += jnp.where(wrapped, terms[0], 0.0)


def iteration_kernel(first, pieces, *refs):
    place_ref, info_ref, step_ref, own_hbm, below_hbm, probe_hbm = refs[:6]
    refs = refs[6:]
    if not first:
        sum_hbms, refs = refs[:2], refs[2:]
    amp_hbm, table_hbm, keep_out, send_out = refs[:4]
    low_outs, refs = refs[4 : 4 + pieces], refs[4 + pieces :]
    own_out, refs = refs[0], refs[1:]
    if not first:
        probe_out, refs = refs[0], refs[1:]
    ext, total, probe_ref, grad_probe, amp_ref, table_ref, sems, in_sems, out_sems = refs
    columns = ext.shape[0]
    rows = ext.shape[2] // 2
    half = probe_ref.shape[1] // 2
    own, low = pl.ds(0, rows), pl.ds(rows, rows)
    mine = pl.ds(pl.multiple_of(info_ref[2] * half, half), half)
    others = pl.ds(pl.multiple_of((1 - info_ref[2]) * half, half), half)

    def by_column(hbm, vmem, where):
        return [
            (hbm.at[part, :, pl.ds(LANE_TILE * column, LANE_TILE)], vmem.at[column, part, where, :])
            for part in (0, 1)
            for column in range(columns)
        ]

    def by_piece(hbms, vmem, where):
        size = columns // len(hbms)
        return [(hbm, vmem.at[pl.ds(size * piece, size), :, where, :]) for piece, hbm in enumerate(hbms)]

    pairs = [(probe_hbm, probe_ref)]
    if not first:
        pairs += [(sum_hbms[0], grad_probe.at[:, mine, :]), (sum_hbms[1], grad_probe.at[:, others, :])]
    early = len(pairs)
    if first:
        pairs += by_column(own_hbm, ext, own) + by_column(below_hbm, ext, low)
    else:
        pairs += by_piece([own_hbm], ext, own) + by_piece([below_hbm], ext, low)
    pairs += [(table_hbm, table_ref), (amp_hbm, amp_ref)]
    copies = [pltpu.make_async_copy(src, dst, in_sems.at[i]) for i, (src, dst) in enumerate(pairs)]
    for copy in copies:
        copy.start()
    total[:, :, low, :] = jnp.zeros((columns, 2, rows, LANE_TILE), jnp.float32)
    for copy in copies[:early]:
        copy.wait()
    if not first:
        probe_ref[...] = probe_ref[...] - step_ref[0] * grad_probe[...]
        probe_copy = pltpu.make_async_copy(probe_ref, probe_out, sems.at[2])
        probe_copy.start()
    power = probe_ref[0] * probe_ref[0] + probe_ref[1] * probe_ref[1]
    descent = -1.0 / (jnp.max(power) + 1e-06)
    grad_probe[...] = jnp.zeros_like(grad_probe)
    for copy in copies[early:]:
        copy.wait()
    total[:, :, own, :] = ext[:, :, own, :]

    count = info_ref[0]

    def slots(index, carry):
        steps = []
        for slot in (TOGETHER * index + k for k in range(TOGETHER)):
            live = (slot < count).astype(jnp.float32)
            slot = jnp.minimum(slot, amp_ref.shape[0] - 1)
            steps.append(
                slot_steps(slot, live, descent, place_ref, amp_ref, probe_ref, table_ref, ext, total, grad_probe)
            )
        for unused in zip_longest(*steps):
            pass
        return carry

    lax.fori_loop(0, (count + TOGETHER - 1) // TOGETHER, slots, 0)

    @pl.when(info_ref[1] == 0)
    def _():
        total[:, :, low, :] = jnp.zeros((columns, 2, rows, LANE_TILE), jnp.float32)

    outs = [
        pltpu.make_async_copy(grad_probe.at[:, others, :], send_out, sems.at[0]),
        pltpu.make_async_copy(grad_probe.at[:, mine, :], keep_out, sems.at[1]),
    ]
    pairs = by_piece(low_outs, total, low)
    pairs += by_piece([own_out], total, own) if first else by_column(own_out, total, own)
    outs += [pltpu.make_async_copy(src, dst, out_sems.at[i]) for i, (dst, src) in enumerate(pairs)]
    for copy in outs:
        copy.start()
    for copy in outs:
        copy.wait()
    if not first:
        probe_copy.wait()


def iteration(first, scalars, strips, probes, amplitudes, table, shape):
    parts, rows, width = shape
    columns = width // LANE_TILE
    pieces = 1 if first or columns % PIECES else PIECES
    smem = pl.BlockSpec(memory_space=pltpu.SMEM)
    anywhere = pl.BlockSpec(memory_space=pl.ANY)
    probe_shape = jax.ShapeDtypeStruct(probes[0].shape, jnp.float32)
    half_shape = jax.ShapeDtypeStruct((parts, probe_shape.shape[1] // 2, probe_shape.shape[2]), jnp.float32)
    strip = jax.ShapeDtypeStruct((columns, parts, rows, LANE_TILE), jnp.float32)
    piece = jax.ShapeDtypeStruct((columns // pieces, *strip.shape[1:]), jnp.float32)
    arrays = (*strips, *probes, amplitudes, table)
    out_shape = [half_shape, half_shape] + [piece] * pieces
    out_shape += [strip] if first else [jax.ShapeDtypeStruct(shape, jnp.float32), probe_shape]
    extended = (columns, parts, 2 * rows, LANE_TILE)
    outs = pl.pallas_call(
        partial(iteration_kernel, first, pieces),
        out_shape=out_shape,
        in_specs=[smem] * len(scalars) + [anywhere] * len(arrays),
        out_specs=[anywhere] * len(out_shape),
        scratch_shapes=[
            pltpu.VMEM(extended, jnp.float32),
            pltpu.VMEM(extended, jnp.float32),
            pltpu.VMEM(probe_shape.shape, jnp.float32),
            pltpu.VMEM(probe_shape.shape, jnp.float32),
            pltpu.VMEM(amplitudes.shape, amplitudes.dtype),
            pltpu.VMEM(table.shape, table.dtype),
            pltpu.SemaphoreType.DMA((3,)),
            pltpu.SemaphoreType.DMA((5 + 2 * parts * columns,)),
            pltpu.SemaphoreType.DMA((parts * columns + pieces,)),
        ],
        compiler_params=pltpu.CompilerParams(vmem_limit_bytes=62 * 2**20),
        cost_estimate=pl.CostEstimate(flops=8_000_000_000, bytes_accessed=8_000_000, transcendentals=400_000),
        name="iteration",
    )(*scalars, *arrays)
    return outs[:2], outs[2 : 2 + pieces], outs[2 + pieces :]


def passed_along(value, axis, by):
    size = lax.axis_size(axis)
    pairs = [(i, i + by) for i in range(size) if 0 <= i + by < size]
    return lax.ppermute(value, axis, pairs)


def swapped(value, axis, bit):
    size = lax.axis_size(axis)
    return lax.ppermute(value, axis, [(i, i ^ bit) for i in range(size)])


def upper_of(axis, bit):
    return (lax.axis_index(axis) & bit) != 0


def bits_of(axis):
    size = lax.axis_size(axis)
    if size & (size - 1) or size < 8:
        return []
    bits = [1 << k for k in range(size.bit_length() - 1)]
    return [bits[0], *bits[2:], bits[1]]


def joined(mine, other, upper):
    return jnp.concatenate([jnp.where(upper, other, mine), jnp.where(upper, mine, other)], axis=1)


def summed_beside(keep, send, axis, pieces, late, used=None):
    bits = bits_of(axis)
    pieces = [[list(arrays), by] for arrays, by in pieces]
    upper = upper_of(axis, 1)

    def moving(piece):
        return [passed_along(array, axis, by) for array, by in zip(*piece)]

    if not bits:
        value = lax.psum(joined(keep, send, upper), axis)
        half = value.shape[1] // 2
        first, second = value[:, :half], value[:, half:]
        return jnp.where(upper, second, first), jnp.where(upper, first, second), [
            used(*moving(piece)) if used else moving(piece) for piece in pieces
        ]
    moved = [moving(piece) for piece in pieces[:1]]
    value = keep + swapped(send, axis, bits[0])
    inner = upper_of(axis, bits[1])
    half = value.shape[1] // 2
    first, second = value[:, :half], value[:, half:]
    value = jnp.where(inner, second, first) + swapped(jnp.where(inner, first, second), axis, bits[1])
    for bit in bits[2:]:
        if bit == bits[-1]:
            value, rest = lax.optimization_barrier((value, [piece[0] for piece in pieces[1:]]))
            moved += [moving((arrays, by)) for arrays, (unused, by) in zip(rest, pieces[1:])]
        value = value + swapped(value, axis, bit)
        if bit == bits[-1 if late else 2]:
            value, moved[0] = lax.optimization_barrier((value, moved[0]))
    if used:
        moved = [used(*moved[0])]
    value = joined(value, swapped(value, axis, bits[1]), inner)
    value, moved = lax.optimization_barrier((value, moved))
    return value, swapped(value, axis, bits[0]), moved


def on_device(object_field, probe, amplitudes, offsets, counts):
    strip_rows = object_field.shape[1]
    side = probe.shape[1]
    strip_count = lax.axis_size("pos")
    device_index = lax.axis_index("pos")
    table, sort = constants(side)
    table = jnp.asarray(table)
    below = passed_along(object_field, "pos", -1)
    own_count = lax.dynamic_index_in_dim(counts, device_index, keepdims=False)
    not_last = (device_index + 1 < strip_count).astype(jnp.int32)
    info = jnp.stack([own_count, not_last, device_index % 2])
    step = (8.0 / jnp.sum(counts).astype(jnp.float32))[None]
    place = jnp.stack([offsets[:, 0] - device_index * strip_rows, offsets[:, 1]], axis=1)
    amps = sorted_amplitudes(amplitudes, sort)
    shape = object_field.shape
    (keep, send), (low,), (own,) = iteration(True, (place, info, step), (object_field, below), (probe,), amps, table, shape)
    mine, other, [strips] = summed_beside(
        keep, send, "pos", [((low, own), (1, -1))], 1, lambda above, below: (own + above, below + low)
    )
    (keep, send), lows, (own, probe_now) = iteration(
        False, (place, info, step), strips, (probe, mine, other), amps, table, shape
    )
    mine, other, moved = summed_beside(keep, send, "pos", [((low,), (1,)) for low in lows], 0)
    above = [above[column] for (above,) in moved for column in range(above.shape[0])]
    probe_sum = joined(mine, other, upper_of("pos", 1))
    return (own + jnp.concatenate(above, axis=2), probe_now - step * probe_sum)


def solution(mesh):
    in_specs = (
        P("groups", "pos", None),
        P("groups", None, None),
        P(("groups", "pos"), None, None),
        P(("groups", "pos"), None),
        P("groups"),
    )
    out_specs = (P("groups", "pos", None), P("groups", None, None))
    return jax.shard_map(
        on_device, mesh=mesh, in_specs=in_specs, out_specs=out_specs, check_vma=False
    )
```

```python
from functools import partial
from itertools import zip_longest
import math

import jax
import jax.numpy as jnp
import numpy as np
from jax import lax
from jax.experimental import pallas as pl
from jax.experimental.pallas import tpu as pltpu
from jax.sharding import PartitionSpec as P

LANE_TILE = 128
PIECES = 2
TOGETHER = 3


def split_bf16(array):
    high = array.astype(jnp.bfloat16)
    low = (array - high.astype(np.float32)).astype(jnp.bfloat16)
    return high, low


def constants(side):
    half = side // 2
    index = np.arange(half)
    parts = []
    for odd in (0, 1):
        angle = 2.0 * np.pi / side * (index[:, None] * (2 * index[None, :] + odd) % side)
        cosine, sine = np.cos(angle), np.sin(angle)
        matrix = (np.block([[cosine, -sine], [sine, cosine]]) / math.sqrt(side)).astype(np.float32)
        parts.append(split_bf16(matrix))
    tables = [[part, part.T] for pair in parts for part in pair]
    order = np.concatenate([np.arange(0, side, 2), np.arange(1, side, 2)])
    sort = np.zeros((side, side), np.float32)
    sort[order, np.arange(side)] = 1.0
    return np.stack([m for pair in tables for m in pair]), sort.astype(jnp.bfloat16)


def permute_kernel(amp_ref, sort_ref, sort_t_ref, out_ref):
    def one(slot, carry):
        rows = jnp.dot(sort_t_ref[...], amp_ref[slot], preferred_element_type=jnp.float32)
        both = jnp.dot(rows.astype(jnp.bfloat16), sort_ref[...], preferred_element_type=jnp.float32)
        out_ref[slot] = both.astype(jnp.bfloat16)
        return carry

    lax.fori_loop(0, amp_ref.shape[0], one, 0)


def sorted_amplitudes(amplitudes, sort):
    return pl.pallas_call(
        permute_kernel,
        out_shape=jax.ShapeDtypeStruct(amplitudes.shape, amplitudes.dtype),
        compiler_params=pltpu.CompilerParams(vmem_limit_bytes=63 * 2**20),
        cost_estimate=pl.CostEstimate(flops=400_000_000, bytes_accessed=1_600_000, transcendentals=0),
        name="sort_amplitudes",
    )(amplitudes, jnp.asarray(sort), jnp.asarray(sort.T))


def hi_lo(value):
    high = value.astype(jnp.bfloat16)
    return high, (value - high.astype(jnp.float32)).astype(jnp.bfloat16)


def matrix(table_ref, odd, turned, axis):
    high, low = table_ref[4 * odd + turned], table_ref[4 * odd + 2 + turned]
    return jnp.concatenate([high, high, low], axis=axis)


def times_right(value, table_ref, odd, turned):
    high, low = hi_lo(value)
    stacked = jnp.concatenate([high, low, high], axis=1)
    return jnp.dot(stacked, matrix(table_ref, odd, turned, 0), preferred_element_type=jnp.float32)


def times_left(table_ref, odd, turned, value):
    high, low = hi_lo(value)
    stacked = jnp.concatenate([high, low, high], axis=0)
    return jnp.dot(matrix(table_ref, odd, turned, 1), stacked, preferred_element_type=jnp.float32)


def lane_rotated(left, right, shift, wrapped):
    left, right = pltpu.roll(left, shift, 1), pltpu.roll(right, shift, 1)
    return jnp.where(wrapped, right, left), jnp.where(wrapped, left, right)


def slot_steps(slot, live, descent, place_ref, amp_ref, probe_ref, table_ref, ext, total, grad_probe):
    side = probe_ref.shape[1]
    half = side // 2
    row, col = place_ref[slot, 0], place_ref[slot, 1]
    rows = pl.ds(row, side)
    first = col // LANE_TILE
    shift = col - first * LANE_TILE
    third = jnp.minimum(first + 2, ext.shape[0] - 1)
    lanes = lax.broadcasted_iota(jnp.int32, (side, LANE_TILE), 1)
    wrapped = lanes < shift

    def patch(part):
        return jnp.where(wrapped, ext[third, part, rows, :], ext[first, part, rows, :]), ext[first + 1, part, rows, :]

    def probe(part):
        return lane_rotated(probe_ref[part, :, :half], probe_ref[part, :, half:], shift, wrapped)

    patch_re, patch_im = patch(0), patch(1)
    probe_re, probe_im = probe(0), probe(1)
    exit_re = [p * q - r * s for p, q, r, s in zip(probe_re, patch_re, probe_im, patch_im)]
    exit_im = [p * q + r * s for p, q, r, s in zip(probe_re, patch_im, probe_im, patch_re)]
    even = jnp.concatenate([exit_re[0] + exit_re[1], exit_im[0] + exit_im[1]], axis=1)
    odd = jnp.concatenate([exit_re[0] - exit_re[1], exit_im[0] - exit_im[1]], axis=1)
    even = times_right(even, table_ref, 0, 0)
    odd = times_right(odd, table_ref, 1, 0)
    yield
    wave_re = jnp.concatenate([even[:, :half], odd[:, :half]], axis=1)
    wave_im = jnp.concatenate([even[:, half:], odd[:, half:]], axis=1)
    even = jnp.concatenate([wave_re[:half] + wave_re[half:], wave_im[:half] + wave_im[half:]], axis=0)
    odd = jnp.concatenate([wave_re[:half] - wave_re[half:], wave_im[:half] - wave_im[half:]], axis=0)
    even = times_left(table_ref, 0, 1, even)
    odd = times_left(table_ref, 1, 1, odd)
    yield

    def kept(spec, rows):
        spec_re, spec_im = spec[:half], spec[half:]
        amplitude = amp_ref[slot, rows, :].astype(jnp.float32)
        keeping = live - live * amplitude * lax.rsqrt(spec_re * spec_re + spec_im * spec_im + 1.0)
        return jnp.concatenate([spec_re * keeping, spec_im * keeping], axis=0)

    even = times_left(table_ref, 0, 0, kept(even, slice(0, half)))
    odd = times_left(table_ref, 1, 0, kept(odd, slice(half, side)))
    wave_re = jnp.concatenate([even[:half] + odd[:half], even[:half] - odd[:half]], axis=0)
    wave_im = jnp.concatenate([even[half:] + odd[half:], even[half:] - odd[half:]], axis=0)
    yield
    even = times_right(jnp.concatenate([wave_re[:, :half], wave_im[:, :half]], axis=1), table_ref, 0, 1)
    odd = times_right(jnp.concatenate([wave_re[:, half:], wave_im[:, half:]], axis=1), table_ref, 1, 1)
    yield
    resid_re = (even[:, :half] + odd[:, :half], even[:, :half] - odd[:, :half])
    resid_im = (even[:, half:] + odd[:, half:], even[:, half:] - odd[:, half:])
    back = jnp.where(shift == 0, 0, LANE_TILE - shift)
    from_left = lanes < LANE_TILE - shift
    for part in (0, 1):
        if part == 0:
            terms = [p * q + r * s for p, q, r, s in zip(patch_re, resid_re, patch_im, resid_im)]
        else:
            terms = [p * q - r * s for p, q, r, s in zip(patch_re, resid_im, patch_im, resid_re)]
        left, right = (pltpu.roll(term, back, 1) for term in terms)
        grad_probe[part, :, :half] += jnp.where(from_left, left, right)
        grad_probe[part, :, half:] += jnp.where(from_left, right, left)
    for part in (0, 1):
        if part == 0:
            terms = [p * q + r * s for p, q, r, s in zip(probe_re, resid_re, probe_im, resid_im)]
        else:
            terms = [p * q - r * s for p, q, r, s in zip(probe_re, resid_im, probe_im, resid_re)]
        terms = [descent * term for term in terms]
        total[first, part, rows, :] += jnp.where(wrapped, 0.0, terms[0])
        total[first + 1, part, rows, :] += terms[1]
        total[third, part, rows, :] += jnp.where(wrapped, terms[0], 0.0)


def iteration_kernel(first, pieces, *refs):
    place_ref, info_ref, step_ref, own_hbm, below_hbm, probe_hbm = refs[:6]
    refs = refs[6:]
    if not first:
        sum_hbms, refs = refs[:2], refs[2:]
    amp_hbm, table_hbm, keep_out, send_out = refs[:4]
    low_outs, refs = refs[4 : 4 + pieces], refs[4 + pieces :]
    own_out, refs = refs[0], refs[1:]
    if not first:
        probe_out, refs = refs[0], refs[1:]
    ext, total, probe_ref, grad_probe, amp_ref, table_ref, sems, in_sems, out_sems = refs
    columns = ext.shape[0]
    rows = ext.shape[2] // 2
    half = probe_ref.shape[1] // 2
    own, low = pl.ds(0, rows), pl.ds(rows, rows)
    mine = pl.ds(pl.multiple_of(info_ref[2] * half, half), half)
    others = pl.ds(pl.multiple_of((1 - info_ref[2]) * half, half), half)

    def by_column(hbm, vmem, where):
        return [
            (hbm.at[part, :, pl.ds(LANE_TILE * column, LANE_TILE)], vmem.at[column, part, where, :])
            for part in (0, 1)
            for column in range(columns)
        ]

    def by_piece(hbms, vmem, where):
        size = columns // len(hbms)
        return [(hbm, vmem.at[pl.ds(size * piece, size), :, where, :]) for piece, hbm in enumerate(hbms)]

    pairs = [(probe_hbm, probe_ref)]
    if not first:
        pairs += [(sum_hbms[0], grad_probe.at[:, mine, :]), (sum_hbms[1], grad_probe.at[:, others, :])]
    early = len(pairs)
    if first:
        pairs += by_column(own_hbm, ext, own) + by_column(below_hbm, ext, low)
    else:
        pairs += by_piece([own_hbm], ext, own) + by_piece([below_hbm], ext, low)
    pairs += [(table_hbm, table_ref), (amp_hbm, amp_ref)]
    copies = [pltpu.make_async_copy(src, dst, in_sems.at[i]) for i, (src, dst) in enumerate(pairs)]
    for copy in copies:
        copy.start()
    total[:, :, low, :] = jnp.zeros((columns, 2, rows, LANE_TILE), jnp.float32)
    for copy in copies[:early]:
        copy.wait()
    if not first:
        probe_ref[...] = probe_ref[...] - step_ref[0] * grad_probe[...]
        probe_copy = pltpu.make_async_copy(probe_ref, probe_out, sems.at[2])
        probe_copy.start()
    power = probe_ref[0] * probe_ref[0] + probe_ref[1] * probe_ref[1]
    descent = -1.0 / (jnp.max(power) + 1e-06)
    grad_probe[...] = jnp.zeros_like(grad_probe)
    for copy in copies[early:]:
        copy.wait()
    total[:, :, own, :] = ext[:, :, own, :]

    count = info_ref[0]

    def slots(index, carry):
        steps = []
        for slot in (TOGETHER * index + k for k in range(TOGETHER)):
            live = (slot < count).astype(jnp.float32)
            slot = jnp.minimum(slot, amp_ref.shape[0] - 1)
            steps.append(
                slot_steps(slot, live, descent, place_ref, amp_ref, probe_ref, table_ref, ext, total, grad_probe)
            )
        for unused in zip_longest(*steps):
            pass
        return carry

    lax.fori_loop(0, (count + TOGETHER - 1) // TOGETHER, slots, 0)

    @pl.when(info_ref[1] == 0)
    def _():
        total[:, :, low, :] = jnp.zeros((columns, 2, rows, LANE_TILE), jnp.float32)

    outs = [
        pltpu.make_async_copy(grad_probe.at[:, others, :], send_out, sems.at[0]),
        pltpu.make_async_copy(grad_probe.at[:, mine, :], keep_out, sems.at[1]),
    ]
    pairs = by_piece(low_outs, total, low)
    pairs += by_piece([own_out], total, own) if first else by_column(own_out, total, own)
    outs += [pltpu.make_async_copy(src, dst, out_sems.at[i]) for i, (dst, src) in enumerate(pairs)]
    for copy in outs:
        copy.start()
    for copy in outs:
        copy.wait()
    if not first:
        probe_copy.wait()


def iteration(first, scalars, strips, probes, amplitudes, table, shape):
    parts, rows, width = shape
    columns = width // LANE_TILE
    pieces = 1 if first or columns % PIECES else PIECES
    smem = pl.BlockSpec(memory_space=pltpu.SMEM)
    anywhere = pl.BlockSpec(memory_space=pl.ANY)
    probe_shape = jax.ShapeDtypeStruct(probes[0].shape, jnp.float32)
    half_shape = jax.ShapeDtypeStruct((parts, probe_shape.shape[1] // 2, probe_shape.shape[2]), jnp.float32)
    strip = jax.ShapeDtypeStruct((columns, parts, rows, LANE_TILE), jnp.float32)
    piece = jax.ShapeDtypeStruct((columns // pieces, *strip.shape[1:]), jnp.float32)
    arrays = (*strips, *probes, amplitudes, table)
    out_shape = [half_shape, half_shape] + [piece] * pieces
    out_shape += [strip] if first else [jax.ShapeDtypeStruct(shape, jnp.float32), probe_shape]
    extended = (columns, parts, 2 * rows, LANE_TILE)
    outs = pl.pallas_call(
        partial(iteration_kernel, first, pieces),
        out_shape=out_shape,
        in_specs=[smem] * len(scalars) + [anywhere] * len(arrays),
        out_specs=[anywhere] * len(out_shape),
        scratch_shapes=[
            pltpu.VMEM(extended, jnp.float32),
            pltpu.VMEM(extended, jnp.float32),
            pltpu.VMEM(probe_shape.shape, jnp.float32),
            pltpu.VMEM(probe_shape.shape, jnp.float32),
            pltpu.VMEM(amplitudes.shape, amplitudes.dtype),
            pltpu.VMEM(table.shape, table.dtype),
            pltpu.SemaphoreType.DMA((3,)),
            pltpu.SemaphoreType.DMA((5 + 2 * parts * columns,)),
            pltpu.SemaphoreType.DMA((parts * columns + pieces,)),
        ],
        compiler_params=pltpu.CompilerParams(vmem_limit_bytes=62 * 2**20),
        cost_estimate=pl.CostEstimate(flops=8_000_000_000, bytes_accessed=8_000_000, transcendentals=400_000),
        name="iteration",
    )(*scalars, *arrays)
    return outs[:2], outs[2 : 2 + pieces], outs[2 + pieces :]


def passed_along(value, axis, by):
    size = lax.axis_size(axis)
    pairs = [(i, i + by) for i in range(size) if 0 <= i + by < size]
    return lax.ppermute(value, axis, pairs)


def swapped(value, axis, bit):
    size = lax.axis_size(axis)
    return lax.ppermute(value, axis, [(i, i ^ bit) for i in range(size)])


def upper_of(axis, bit):
    return (lax.axis_index(axis) & bit) != 0


def bits_of(axis):
    size = lax.axis_size(axis)
    if size & (size - 1) or size < 8:
        return []
    bits = [1 << k for k in range(size.bit_length() - 1)]
    return [bits[0], *bits[2:], bits[1]]


def joined(mine, other, upper):
    return jnp.concatenate([jnp.where(upper, other, mine), jnp.where(upper, mine, other)], axis=1)


def summed_beside(keep, send, axis, pieces, late, used=None):
    bits = bits_of(axis)
    pieces = [[list(arrays), by] for arrays, by in pieces]
    upper = upper_of(axis, 1)

    def moving(piece):
        return [passed_along(array, axis, by) for array, by in zip(*piece)]

    if not bits:
        value = lax.psum(joined(keep, send, upper), axis)
        half = value.shape[1] // 2
        first, second = value[:, :half], value[:, half:]
        return jnp.where(upper, second, first), jnp.where(upper, first, second), [
            used(*moving(piece)) if used else moving(piece) for piece in pieces
        ]
    moved = [moving(piece) for piece in pieces[:1]]
    value = keep + swapped(send, axis, bits[0])
    inner = upper_of(axis, bits[1])
    half = value.shape[1] // 2
    first, second = value[:, :half], value[:, half:]
    value = jnp.where(inner, second, first) + swapped(jnp.where(inner, first, second), axis, bits[1])
    for bit in bits[2:]:
        if bit == bits[-1]:
            value, rest = lax.optimization_barrier((value, [piece[0] for piece in pieces[1:]]))
            moved += [moving((arrays, by)) for arrays, (unused, by) in zip(rest, pieces[1:])]
        value = value + swapped(value, axis, bit)
        if bit == bits[-1 if late else 2]:
            value, moved[0] = lax.optimization_barrier((value, moved[0]))
    if used:
        moved = [used(*moved[0])]
    value = joined(value, swapped(value, axis, bits[1]), inner)
    value, moved = lax.optimization_barrier((value, moved))
    return value, swapped(value, axis, bits[0]), moved


def on_device(object_field, probe, amplitudes, offsets, counts):
    strip_rows = object_field.shape[1]
    side = probe.shape[1]
    strip_count = lax.axis_size("pos")
    device_index = lax.axis_index("pos")
    table, sort = constants(side)
    table = jnp.asarray(table)
    below = passed_along(object_field, "pos", -1)
    own_count = lax.dynamic_index_in_dim(counts, device_index, keepdims=False)
    not_last = (device_index + 1 < strip_count).astype(jnp.int32)
    info = jnp.stack([own_count, not_last, device_index % 2])
    step = (8.0 / jnp.sum(counts).astype(jnp.float32))[None]
    place = jnp.stack([offsets[:, 0] - device_index * strip_rows, offsets[:, 1]], axis=1)
    amps = sorted_amplitudes(amplitudes, sort)
    shape = object_field.shape
    (keep, send), (low,), (own,) = iteration(True, (place, info, step), (object_field, below), (probe,), amps, table, shape)
    mine, other, [strips] = summed_beside(
        keep, send, "pos", [((low, own), (1, -1))], 1, lambda above, below: (own + above, below + low)
    )
    (keep, send), lows, (own, probe_now) = iteration(
        False, (place, info, step), strips, (probe, mine, other), amps, table, shape
    )
    mine, other, moved = summed_beside(keep, send, "pos", [((low,), (1,)) for low in lows], 0)
    above = [above[column] for (above,) in moved for column in range(above.shape[0])]
    probe_sum = joined(mine, other, upper_of("pos", 1))
    return (own + jnp.concatenate(above, axis=2), probe_now - step * probe_sum)


def solution(mesh):
    in_specs = (
        P("groups", "pos", None),
        P("groups", None, None),
        P(("groups", "pos"), None, None),
        P(("groups", "pos"), None),
        P("groups"),
    )
    out_specs = (P("groups", "pos", None), P("groups", None, None))
    return jax.shard_map(
        on_device, mesh=mesh, in_specs=in_specs, out_specs=out_specs, check_vma=False
    )
```
